256 devices in a mesh: tm: 8 (over y, core), group: 32 (over x, z).
Axes of the slice: x: 4, y: 4, z: 8, core: 2. Of those that a mesh axis runs over, the one named last changes fastest.
Arguments:
- field: float32 [2, 4096, 384], P(None, 'tm'), may hold values from -12 to 12
- occupations: float32 [512, 384], P('group'), may hold values from 0.2 to 1
- dephase: float32 [512], P('group'), may hold values from 4.8828125e-05 to 0.04
- detune_class: int32 [512], P('group'), may hold values from 0 to 31
- dot_count: int32 [512], P('group'), may hold values from 1 to 16
Outputs:
- amplified: float32 [2, 4096, 384], P(None, 'tm')
- polarization: float32 [2, 4096, 384], P(None, 'tm')
- occupancy: float32 [512, 384], P('group')
The draws below stay inside these ranges and needn't reach their ends.
All inputs are finite; a program needn't handle non-finite values.
Results may differ from the reference program's by a relative error of at most 0.0003.
Values sent between devices are 32-bit elements; how exact they have to be, the bound alone decides.
No kernel may reach another device: no remote copies, remote signals or barrier semaphores. Data moves between devices by JAX's collectives and lax.ppermute only.
A program may use at most 64 MiB of HBM per device.

```python
import math
import jax
import jax.numpy as jnp
from jax import lax

X = 384
NCLASS = 32
ZSTEPS = 2
GROUPS = 512
TIME = 4096


def draw_field(key, part):
    key = jax.random.fold_in(key, 11)
    first = jax.random.fold_in(key, 0)
    ramp = 0.6 + 1.2 * jnp.arange(TIME, dtype=jnp.float32) / TIME
    values = jnp.clip(jax.random.normal(first, (2, TIME, X), jnp.float32), -5.0, 5.0)
    return values * ramp[None, :, None]


def draw_dephase(key, part):
    key = jax.random.fold_in(key, 23)
    first, second, third = jax.random.split(key, 3)
    slow_share = 0.45
    middle_share = 0.25
    picked = jax.random.uniform(first, (GROUPS,), jnp.float32)
    level = jax.random.uniform(second, (GROUPS,), jnp.float32)
    spread = jax.random.uniform(third, (GROUPS,), jnp.float32)
    slow_rate = jnp.exp(math.log(0.2 / TIME) + spread * math.log(10.0))
    middle_low = math.log(2.0 / TIME)
    middle_rate = jnp.exp(middle_low + spread * (math.log(0.02) - middle_low))
    fast_rate = 0.02 + 0.02 * level
    return jnp.where(picked < slow_share, slow_rate, jnp.where(picked < slow_share + middle_share, middle_rate, fast_rate))


def touch_ends(result, key, smallest, largest):
    dims = result.shape
    index_at = [jax.random.randint(jax.random.fold_in(key, axis), (), 0, dims[axis]) for axis in range(len(dims))]
    result = result.at[tuple(index_at)].set(smallest)
    longest = dims.index(max(dims))
    index_at[longest] = (index_at[longest] + 1) % dims[longest]
    return result.at[tuple(index_at)].set(largest)


def shard_levels(own_key, shape, shards, low, high):
    def one(dim, blocks):
        heights = jax.random.uniform(jax.random.fold_in(jax.random.fold_in(own_key, 6), dim), (blocks,), jnp.float32, low / len(shards), high / len(shards))
        return jnp.repeat(jnp.exp(heights), shape[dim] // blocks).reshape((-1,) + (1,) * (len(shape) - dim - 1))

    gain = one(*shards[0])
    for cut in shards[1:]:
        gain = gain * one(*cut)
    return gain


def setup_inputs(seed: int = 0) -> dict:
    key_of = jax.random.split(jax.random.key(seed), 6)
    return {
        "field": draw_field(jax.random.fold_in(key_of[5], 71), 0),
        "occupations": jnp.clip(0.2 + 0.8 * jax.random.uniform(key_of[1], (GROUPS, X), jnp.float32) ** shard_levels(key_of[1], (GROUPS, X), ((0, 32),), -0.2, 0.2), 0.2, 1.0),
        "dephase": draw_dephase(jax.random.fold_in(key_of[5], 71), 0),
        "detune_class": touch_ends(jax.random.randint(key_of[3], (GROUPS,), 0, NCLASS), jax.random.fold_in(key_of[3], 1), 0, NCLASS - 1).astype(jnp.int32),
        "dot_count": touch_ends(jax.random.randint(key_of[4], (GROUPS,), 1, 17), jax.random.fold_in(key_of[4], 1), 1, 16).astype(jnp.int32),
    }


POL_GAIN = 0.25
SATURATE = 1.5
DIFF_PHASE = 6.0
ANGLE_UNIT = 0.01

def diffract_ref(stacked):
    complex_field = stacked[0] + 1j * stacked[1]
    spectrum = jnp.fft.fft(complex_field, axis=-1)
    column = jnp.arange(X)
    signed_freq = jnp.where(column < X // 2, column, column - X)
    phase_shift = DIFF_PHASE * (signed_freq * signed_freq).astype(stacked.dtype) / float((X // 2) ** 2)
    turned = jnp.fft.ifft(spectrum * jnp.exp(-1j * phase_shift), axis=-1)
    return jnp.stack([jnp.real(turned), jnp.imag(turned)]).astype(stacked.dtype)

def reference(field, occupations, dephase, detune_class, dot_count):
    decay_mag = jnp.exp(-dephase)
    wave_index = (2 * detune_class - (NCLASS - 1)).astype(dephase.dtype)
    theta_step = wave_index * ANGLE_UNIT
    step_real = (decay_mag * jnp.cos(theta_step))[:, None]
    step_imag = (-decay_mag * jnp.sin(theta_step))[:, None]
    drive_gain = jnp.sqrt((1.0 - step_real) ** 2 + step_imag ** 2)
    count_weight = POL_GAIN / GROUPS * dot_count.astype(dephase.dtype)
    occupancy = occupations
    current = field
    polar = field
    for z_step in range(ZSTEPS):
        coupling = count_weight[:, None] * occupancy

        def advance(carry, sample):
            resp_real, resp_imag, intersection = carry
            drive_real, drive_imag = sample
            next_real = step_real * resp_real - step_imag * resp_imag + drive_gain * drive_real[None, :]
            next_imag = step_real * resp_imag + step_imag * resp_real + drive_gain * drive_imag[None, :]
            intersection = intersection + drive_real[None, :] * next_real + drive_imag[None, :] * next_imag
            return ((next_real, next_imag, intersection), (lax.optimization_barrier(jnp.sum(coupling * next_real, 0)), lax.optimization_barrier(jnp.sum(coupling * next_imag, 0))))
        zeros_state = jnp.zeros((GROUPS, X), dephase.dtype)
        (_, _, intersection), (polar_real, polar_imag) = lax.scan(advance, (zeros_state, zeros_state, zeros_state), (current[0], current[1]))
        polar = jnp.stack([polar_real, polar_imag])
        occupancy = occupancy * jnp.exp(-SATURATE * intersection / TIME)
        current = diffract_ref(current + polar)
    return (current, polar, occupancy)
```

```python
import functools

import jax
import jax.numpy as jnp
import numpy as np
from jax import lax
from jax.experimental import pallas as pl
from jax.experimental.pallas import tpu as pltpu
from jax.sharding import PartitionSpec as P

NCLASS = 32
POL_GAIN = 0.25
SATURATE = 1.5
DIFF_PHASE = 6.0
ANGLE_UNIT = 0.01

NX, NZ, NY = 4, 8, 4
LATERAL = 384
TOTAL_TIME = 4096
TOTAL_GROUPS = 512
SPAN = 512
OWN = 12
PAD = 16
PHASES = 8
ROWS = 64
LANES = 128

F32 = jnp.float32
BF16 = jnp.bfloat16
HIGHEST = lax.Precision.HIGHEST
VMEM = pl.BlockSpec(memory_space=pltpu.VMEM)


def split2_np(value):
    import ml_dtypes

    high = value.astype(np.float32).astype(ml_dtypes.bfloat16)
    low = (value - high.astype(np.float64)).astype(np.float32).astype(ml_dtypes.bfloat16)
    return high, low


@functools.cache
def lateral_constants():
    column = np.arange(LATERAL)
    signed = np.where(column < LATERAL // 2, column, column - LATERAL).astype(np.float64)
    phase = DIFF_PHASE * signed**2 / float((LATERAL // 2) ** 2)
    twist = np.exp(-1j * phase)

    def real_form(multiplier):
        kernel = np.fft.ifft(multiplier)
        full = kernel[(column[None, :] - column[:, None]) % LATERAL]
        return np.block([[full.real, full.imag], [-full.imag, full.real]])

    owner = np.arange(NX * NZ)[:, None, None]
    part = np.arange(2)[None, :, None]
    inner = np.arange(OWN)[None, None, :]
    order = (part * LATERAL + owner * OWN + inner).reshape(-1)
    once = real_form(twist)
    twice = real_form(twist * twist)
    place = np.zeros((2 * LATERAL, 2 * LATERAL))
    place[np.arange(2 * LATERAL), order] = 1.0
    return {
        "once_nat": split2_np(once),
        "once_perm": split2_np(once[order]),
        "twice_nat": split2_np(twice),
        "twice_perm": split2_np(twice[order]),
        "place": split2_np(place)[0],
    }


def halves(value):
    high = value.astype(BF16)
    low = (value - high.astype(F32)).astype(BF16)
    return high, low


def thirds(value):
    high = value.astype(BF16)
    rest = value - high.astype(F32)
    mid = rest.astype(BF16)
    low = (rest - mid.astype(F32)).astype(BF16)
    return high, mid, low


def mm(left, right):
    return jnp.dot(left, right, preferred_element_type=F32)


def mm3(left, right):
    (lh, ll), (rh, rl) = left, right
    return mm(lh, rh) + (mm(lh, rl) + mm(ll, rh))


def exact_pick(value, pick):
    high, mid, low = thirds(value)
    return (mm(high, pick) + mm(mid, pick)) + mm(low, pick)


def nt(left, right):
    return lax.dot_general(
        left, right, (((1,), (1,)), ((), ())), precision=HIGHEST, preferred_element_type=F32
    )


def nn(left, right):
    return jnp.dot(left, right, precision=HIGHEST, preferred_element_type=F32)


def own_pick():
    first = lax.axis_index("group") * OWN
    row = lax.broadcasted_iota(jnp.int32, (LATERAL, LANES), 0)
    lane = lax.broadcasted_iota(jnp.int32, (LATERAL, LANES), 1) % PAD
    return jnp.where((row == first + lane) & (lane < OWN), 1.0, 0.0).astype(BF16)


def lane_phase(rows):
    return lax.broadcasted_iota(jnp.int32, (rows, LANES), 1) // PAD


def times(ar, ai, br, bi):
    return ar * br - ai * bi, ar * bi + ai * br


AV, A64 = 0, 16
MISC = 32
SMALL = 40


def powers(first, step, rate, wave):
    exponent = (lax.broadcasted_iota(jnp.int32, (8, 1), 0) * step + first).astype(F32)
    magnitude = jnp.exp(-exponent * rate)
    angle = (exponent * wave) * ANGLE_UNIT
    return magnitude * jnp.cos(angle), -magnitude * jnp.sin(angle)


def edge_state(er, ei, rev_ref, small_ref):
    phase = lane_phase(ROWS)
    row_r = jnp.zeros((ROWS, LANES), F32)
    row_i = jnp.zeros((ROWS, LANES), F32)
    for q in range(PHASES):
        row_r = jnp.where(phase == q, er[q * ROWS : (q + 1) * ROWS], row_r)
        row_i = jnp.where(phase == q, ei[q * ROWS : (q + 1) * ROWS], row_i)
    left = jnp.concatenate([row_r, row_i], 1).T
    with_r = nn(left, rev_ref[:ROWS])
    with_i = nn(left, rev_ref[ROWS:])
    z_r = with_r[:LANES] - with_i[LANES:]
    z_i = with_r[LANES:] + with_i[:LANES]
    step_r = small_ref[A64 + 1 : A64 + 2]
    step_i = small_ref[A64 + 9 : A64 + 10]
    s_r, s_i = z_r[:PAD], z_i[:PAD]
    for q in range(1, PHASES):
        s_r, s_i = times(step_r, step_i, s_r, s_i)
        s_r = s_r + z_r[q * PAD : (q + 1) * PAD]
        s_i = s_i + z_i[q * PAD : (q + 1) * PAD]
    return jnp.concatenate([s_r, s_i], 0)


def own_field_kernel(field_ref, big_ref):
    pick = own_pick()
    big_ref[0] = exact_pick(field_ref[0], pick)
    big_ref[1] = exact_pick(field_ref[1], pick)


def own_tables_kernel(field_ref, ph_ref, pl_ref, nh_ref, nl_ref, high_ref, low_ref, pre_ref):
    pick = own_pick()
    field = (halves(field_ref[0]), halves(field_ref[1]))
    for c in range(2):
        lanes = slice(c * LANES, (c + 1) * LANES)
        cols = slice(c * LATERAL, (c + 1) * LATERAL)
        high_ref[:, lanes] = mm(ph_ref[:, cols], pick).astype(BF16)
        low_ref[:, lanes] = mm(pl_ref[:, cols], pick).astype(BF16)
        nat_h = mm(nh_ref[:, cols], pick).astype(BF16)
        nat_l = mm(nl_ref[:, cols], pick).astype(BF16)
        pre_ref[:, lanes] = mm3(field[0], (nat_h[:LATERAL], nat_l[:LATERAL])) + mm3(
            field[1], (nat_h[LATERAL:], nat_l[LATERAL:])
        )


def begin_kernel(params_ref, big_ref, fwd1_ref, rev1_ref, fwd8_ref, small_ref, edge_ref):
    rate = params_ref[12:13]
    wave = 2.0 * params_ref[13:14] - (NCLASS - 1)
    count = params_ref[14:15]
    av_r, av_i = powers(0, 1, rate, wave)
    back_r, back_i = powers(7, -1, rate, wave)
    a8_r, a8_i = powers(0, 8, rate, wave)
    a64_r, a64_i = powers(0, 64, rate, wave)
    far_r, far_i = powers(0, SPAN, rate, wave)
    for u in range(8):
        top = slice(8 * u, 8 * u + 8)
        bottom = slice(ROWS + 8 * u, ROWS + 8 * u + 8)
        fwd1_ref[top], fwd1_ref[bottom] = times(a8_r[u : u + 1], a8_i[u : u + 1], av_r, av_i)
        rev1_ref[top], rev1_ref[bottom] = times(
            a8_r[7 - u : 8 - u], a8_i[7 - u : 8 - u], back_r, back_i
        )
        fwd8_ref[top], fwd8_ref[bottom] = times(a64_r[u : u + 1], a64_i[u : u + 1], a8_r, a8_i)
    small_ref[AV : AV + 8] = av_r
    small_ref[AV + 8 : AV + 16] = av_i
    small_ref[A64 : A64 + 8] = a64_r
    small_ref[A64 + 8 : A64 + 16] = a64_i
    drive = jnp.sqrt((1.0 - av_r[1:2]) ** 2 + av_i[1:2] ** 2)
    small_ref[MISC : MISC + 1] = far_r[1:2]
    small_ref[MISC + 1 : MISC + 2] = far_i[1:2]
    small_ref[MISC + 2 : MISC + 3] = far_r[2:3]
    small_ref[MISC + 3 : MISC + 4] = far_i[2:3]
    small_ref[MISC + 4 : MISC + 5] = POL_GAIN / TOTAL_GROUPS * count * drive
    small_ref[MISC + 5 : MISC + 6] = drive / TOTAL_TIME
    small_ref[MISC + 6 : MISC + 8] = jnp.zeros((2, TOTAL_GROUPS), F32)
    edge_ref[...] = edge_state(big_ref[0], big_ref[1], rev1_ref, small_ref)


def overlap_kernel(big_ref, fwd1_ref, fwd8_ref, small_ref, lag_ref, inside_ref, entry_ref, corr_ref):
    row = lax.broadcasted_iota(jnp.int32, (SPAN, LANES), 0)
    phase = lane_phase(SPAN)
    for c in range(2):
        value = big_ref[c]
        out = value
        for q in range(1, PHASES):
            out = jnp.where(phase == q, pltpu.roll(value, q, 0), out)
        lag_ref[c, :ROWS] = jnp.zeros((ROWS, LANES), F32)
        lag_ref[c, ROWS:] = jnp.where(row >= phase, out, 0.0)

    for b in range(8):
        zero = jnp.zeros((8, 8, LANES), F32)

        def body(t, acc):
            acc_r, acc_i = acc
            at = pl.multiple_of(8 * t, 8)
            start = pl.multiple_of(8 * t + (ROWS - 8 * (8 * b + 7)), 8)
            e_r = big_ref[0, pl.ds(at, 8)][None]
            e_i = big_ref[1, pl.ds(at, 8)][None]
            l_r = lag_ref[0, pl.ds(start, ROWS)].reshape(8, 8, LANES)
            l_i = lag_ref[1, pl.ds(start, ROWS)].reshape(8, 8, LANES)
            return (acc_r + (e_r * l_r + e_i * l_i), acc_i + (e_r * l_i - e_i * l_r))

        acc_r, acc_i = lax.fori_loop(8 * b, ROWS, body, (zero, zero), unroll=8)
        sum_r = jnp.sum(acc_r, axis=1)
        sum_i = jnp.sum(acc_i, axis=1)
        for k in range(8):
            p = 8 * b + 7 - k
            corr_ref[p : p + 1, :LANES] = sum_r[k : k + 1]
            corr_ref[p : p + 1, LANES:] = sum_i[k : k + 1]

    left = corr_ref[...].T
    with_r = nn(left, fwd8_ref[:ROWS])
    with_i = nn(left, fwd8_ref[ROWS:])
    z_r = with_r[:LANES] - with_i[LANES:]
    z_i = with_i[:LANES] + with_r[LANES:]
    total = jnp.zeros((PAD, TOTAL_GROUPS), F32)
    for q in range(PHASES):
        part = slice(q * PAD, (q + 1) * PAD)
        total += small_ref[AV + q : AV + q + 1] * z_r[part]
        total -= small_ref[AV + 8 + q : AV + 9 + q] * z_i[part]
    inside_ref[...] = total

    phase = lane_phase(ROWS)
    row_r = jnp.zeros((ROWS, LANES), F32)
    row_i = jnp.zeros((ROWS, LANES), F32)
    for q in range(PHASES):
        row_r = jnp.where(phase == q, big_ref[0, q * ROWS : (q + 1) * ROWS], row_r)
        row_i = jnp.where(phase == q, big_ref[1, q * ROWS : (q + 1) * ROWS], row_i)
    left = jnp.concatenate([row_r, row_i], 1).T
    with_r = nn(left, fwd1_ref[:ROWS])
    with_i = nn(left, fwd1_ref[ROWS:])
    z_r = with_r[:LANES] + with_i[LANES:]
    z_i = with_i[:LANES] - with_r[LANES:]
    f_r = jnp.zeros((PAD, TOTAL_GROUPS), F32)
    f_i = jnp.zeros((PAD, TOTAL_GROUPS), F32)
    for q in range(PHASES):
        part = slice(q * PAD, (q + 1) * PAD)
        add_r, add_i = times(
            small_ref[A64 + q : A64 + q + 1], small_ref[A64 + 8 + q : A64 + 9 + q], z_r[part], z_i[part]
        )
        f_r += add_r
        f_i += add_i
    one_r = small_ref[AV + 1 : AV + 2]
    one_i = small_ref[AV + 9 : AV + 10]
    f_r, f_i = times(one_r, one_i, f_r, f_i)
    entry_ref[:PAD] = f_r
    entry_ref[PAD:] = f_i


def row_weights(weights_r, weights_i, table_ref):
    by_r = nt(table_ref[...], weights_r)
    by_i = nt(table_ref[...], weights_i)
    return by_r[:ROWS] - by_i[ROWS:], by_r[ROWS:] + by_i[:ROWS]


def inside_response(coupling, lag_ref, fwd8_ref, small_ref, kern_ref, polar_ref):
    one_r, one_i = [], []
    for q in range(PHASES):
        one_r.append(small_ref[AV + q : AV + q + 1] * coupling)
        one_i.append(small_ref[AV + 8 + q : AV + 9 + q] * coupling)
    k_r, k_i = row_weights(jnp.concatenate(one_r, 0), jnp.concatenate(one_i, 0), fwd8_ref)
    kern_ref[0] = k_r
    kern_ref[1] = k_i
    for b in range(8):
        zero = jnp.zeros((ROWS, LANES), F32)

        def body(u, acc):
            acc_r, acc_i = acc
            at = pl.multiple_of(8 * u, 8)
            eight_r = kern_ref[0, pl.ds(at, 8)]
            eight_i = kern_ref[1, pl.ds(at, 8)]
            for v in range(8):
                start = pl.multiple_of(ROWS + ROWS * b - ROWS * u - 8 * v, 8)
                k_r, k_i = eight_r[v : v + 1], eight_i[v : v + 1]
                l_r = lag_ref[0, pl.ds(start, ROWS)]
                l_i = lag_ref[1, pl.ds(start, ROWS)]
                acc_r = acc_r + (k_r * l_r - k_i * l_i)
                acc_i = acc_i + (k_r * l_i + k_i * l_r)
            return acc_r, acc_i

        acc_r, acc_i = lax.fori_loop(0, b + 1, body, (zero, zero))
        polar_ref[0, ROWS * b : ROWS * (b + 1)] = acc_r
        polar_ref[1, ROWS * b : ROWS * (b + 1)] = acc_i


def coupling_of(params_ref, small_ref):
    occupied = jnp.concatenate([params_ref[:OWN], jnp.zeros((PAD - OWN, TOTAL_GROUPS), F32)], 0)
    return small_ref[MISC + 4 : MISC + 5] * occupied


def enter_and_finish(
    coupling, edge_ref, other_ref, r1, r2, r3, polar_ref, inside_ref, entry_ref, fwd1_ref, small_ref, send_ref
):
    place = lax.axis_index("tm")
    far_r = small_ref[MISC + 2 : MISC + 3]
    far_i = small_ref[MISC + 3 : MISC + 4]
    half_r = small_ref[MISC : MISC + 1]
    half_i = small_ref[MISC + 1 : MISC + 2]
    y = place // 2
    keep1 = jnp.where(y >= 1, 1.0, 0.0)
    keep2 = jnp.where(y >= 2, 1.0, 0.0)
    keep3 = jnp.where(y >= 3, 1.0, 0.0)
    s_r, s_i = times(far_r, far_i, r3[:PAD] * keep3, r3[PAD : 2 * PAD] * keep3)
    s_r, s_i = times(far_r, far_i, s_r + r2[:PAD] * keep2, s_i + r2[PAD : 2 * PAD] * keep2)
    s_r = s_r + r1[:PAD] * keep1
    s_i = s_i + r1[PAD : 2 * PAD] * keep1
    later_r, later_i = times(half_r, half_i, s_r, s_i)
    odd = (place % 2) == 1
    s_r = jnp.where(odd, later_r + other_ref[:PAD], s_r)
    s_i = jnp.where(odd, later_i + other_ref[PAD : 2 * PAD], s_i)
    cross = s_r * entry_ref[:PAD] - s_i * entry_ref[PAD:]
    met = (inside_ref[...] + cross) * small_ref[MISC + 5 : MISC + 6]
    d_r, d_i = times(small_ref[AV + 1 : AV + 2], small_ref[AV + 9 : AV + 10], coupling * s_r, coupling * s_i)
    one_r, one_i = [], []
    for q in range(PHASES):
        w_r, w_i = times(small_ref[A64 + q : A64 + q + 1], small_ref[A64 + 8 + q : A64 + 9 + q], d_r, d_i)
        one_r.append(w_r)
        one_i.append(w_i)
    c_r, c_i = row_weights(jnp.concatenate(one_r, 0), jnp.concatenate(one_i, 0), fwd1_ref)
    phase = lane_phase(ROWS)
    for q in range(PHASES):
        rows = slice(q * ROWS, (q + 1) * ROWS)
        polar_ref[0, rows] += jnp.where(phase == q, c_r, 0.0)
        polar_ref[1, rows] += jnp.where(phase == q, c_i, 0.0)
    row = lax.broadcasted_iota(jnp.int32, (2 * OWN, LANES), 0)
    lane = lax.broadcasted_iota(jnp.int32, (2 * OWN, LANES), 1) % PAD
    pick_r = jnp.where(row == lane, jnp.where(row < OWN, 1.0, 0.0), 0.0)
    pick_i = jnp.where(row == lane + OWN, jnp.where(lane < OWN, 1.0, 0.0), 0.0)
    send_ref[: 2 * OWN] = nt(pick_r, polar_ref[0]) + nt(pick_i, polar_ref[1])
    return met


def first_inside_kernel(params_ref, lag_ref, fwd8_ref, small_ref, polar_ref, kern_ref):
    inside_response(coupling_of(params_ref, small_ref), lag_ref, fwd8_ref, small_ref, kern_ref, polar_ref)


def first_finish_kernel(
    params_ref, edge_ref, other_ref, r1, r2, r3, part_ref, inside_ref, entry_ref, fwd1_ref, small_ref,
    send_ref, met_ref, polar_ref,
):
    polar_ref[...] = part_ref[...]
    met_ref[...] = enter_and_finish(
        coupling_of(params_ref, small_ref), edge_ref, other_ref, r1, r2, r3, polar_ref, inside_ref, entry_ref,
        fwd1_ref, small_ref, send_ref,
    )


def last_finish_kernel(
    params_ref, edge_ref, other_ref, r1, r2, r3, lag_ref, inside_ref, entry_ref, fwd1_ref, fwd8_ref, small_ref,
    send_ref, kern_ref, polar_ref,
):
    mine = slice(2 * PAD, 3 * PAD)
    met = (edge_ref[mine] + other_ref[mine]) + (r1[mine] + r2[mine] + r3[mine])
    coupling = coupling_of(params_ref, small_ref) * jnp.exp(-SATURATE * met)
    inside_response(coupling, lag_ref, fwd8_ref, small_ref, kern_ref, polar_ref)
    met = enter_and_finish(
        coupling, edge_ref, other_ref, r1, r2, r3, polar_ref, inside_ref, entry_ref, fwd1_ref, small_ref, send_ref
    )
    send_ref[2 * OWN :] = met + edge_ref[mine]


def assemble(blocks, whole_ref, met_ref):
    me = lax.axis_index("group")
    x, z = me // NZ, me % NZ
    offsets = (0, -1, 1, -2, 2, -3, 3)
    for block, offset in zip(blocks[:7], offsets):
        plane = lax.rem(z + offset + NZ, NZ)
        for r in range(NX):
            owner = lax.rem(x - r + NX, NX) * NZ + plane
            at = pl.multiple_of(owner * 24, 8)
            whole_ref[pl.ds(at, 24)] = block[24 * r : 24 * r + 24]
            if met_ref is not None:
                at = pl.multiple_of(owner * PAD, 8)
                met_ref[pl.ds(at, PAD)] = block[96:, LANES * r : LANES * r + LANES]
    plane = lax.rem(z + 4, NZ)
    for r in range(NX):
        owner = lax.rem(x - r + NX, NX) * NZ + plane
        at = pl.multiple_of(owner * 24, 8)
        block = blocks[7] if r < 2 else blocks[8]
        low = 24 * r if r < 2 else 24 * (r - 2)
        whole_ref[pl.ds(at, 24)] = block[low : low + 24]
        if met_ref is not None:
            at = pl.multiple_of(owner * PAD, 8)
            met_ref[pl.ds(at, PAD)] = blocks[8][48:, LANES * r : LANES * r + LANES]


def next_field_kernel(*refs):
    blocks = refs[:9]
    high_ref, low_ref, pre_ref, rev1_ref, small_ref, met_ref = refs[9:15]
    big_ref, turned_ref, edge_ref, whole_ref = refs[15:]
    assemble(blocks, whole_ref, None)
    turned = whole_ref[...].T
    turned_ref[...] = turned
    field = pre_ref[...] + mm3(halves(turned), (high_ref[...], low_ref[...]))
    big_ref[0] = field[:, :LANES]
    big_ref[1] = field[:, LANES:]
    edge_ref[: 2 * PAD] = edge_state(field[:, :LANES], field[:, LANES:], rev1_ref, small_ref)
    edge_ref[2 * PAD :] = met_ref[...]


def carried_kernel(field_ref, turned_ref, nh_ref, nl_ref, ph_ref, pl_ref, out_ref):
    real, imag, turned = halves(field_ref[0]), halves(field_ref[1]), halves(turned_ref[...])
    for c in range(2):
        cols = slice(c * LATERAL, (c + 1) * LATERAL)
        out_ref[c] = (
            mm3(real, (nh_ref[:LATERAL, cols], nl_ref[:LATERAL, cols]))
            + mm3(imag, (nh_ref[LATERAL:, cols], nl_ref[LATERAL:, cols]))
        ) + mm3(turned, (ph_ref[:, cols], pl_ref[:, cols]))


def last_field_kernel(*refs):
    blocks = refs[:9]
    carried_ref, ph_ref, pl_ref, place_ref = refs[9:13]
    out_ref, polar_ref, met_ref, whole_ref, gathered_ref = refs[13:]
    assemble(blocks, whole_ref, gathered_ref)
    high, mid, low = thirds(whole_ref[...].T)
    for c in range(2):
        cols = slice(c * LATERAL, (c + 1) * LATERAL)
        out_ref[c] = carried_ref[c] + mm3((high, mid), (ph_ref[:, cols], pl_ref[:, cols]))
        place = place_ref[:, cols]
        polar_ref[c] = (mm(high, place) + mm(mid, place)) + mm(low, place)
    z = lax.axis_index("group") % NZ
    row = lax.broadcasted_iota(jnp.int32, (PAD, LANES), 0)
    lane = lax.broadcasted_iota(jnp.int32, (PAD, LANES), 1)
    mine = jnp.where(lane == row + PAD * z, 1.0, 0.0)
    turned = nt(mine, gathered_ref[...])
    row = lax.broadcasted_iota(jnp.int32, (TOTAL_GROUPS, LATERAL), 0)
    col = lax.broadcasted_iota(jnp.int32, (TOTAL_GROUPS, LATERAL), 1)
    inner = row % PAD
    place = jnp.where((inner < OWN) & (col == (row // PAD) * OWN + inner), 1.0, 0.0)
    met_ref[...] = nn(turned, place)


def call(kernel, outs, scratch=(), cost=2e9):
    return pl.pallas_call(
        kernel,
        out_shape=[jax.ShapeDtypeStruct(shape, dtype) for shape, dtype in outs],
        scratch_shapes=[pltpu.VMEM(shape, dtype) for shape, dtype in scratch],
        compiler_params=pltpu.CompilerParams(vmem_limit_bytes=48 * 1024 * 1024),
        cost_estimate=pl.CostEstimate(flops=int(cost), bytes_accessed=1 << 20, transcendentals=0),
    )


def to_group(value, dx, dz):
    pairs = [
        (x * NZ + z, ((x + dx) % NX) * NZ + (z + dz) % NZ) for x in range(NX) for z in range(NZ)
    ]
    return lax.ppermute(value, "group", pairs)


def to_time(value, dy, wrap):
    pairs = [
        (2 * y + c, 2 * ((y + dy) % NY) + c)
        for y in range(NY)
        for c in range(2)
        if wrap or y + dy < NY
    ]
    return lax.ppermute(value, "tm", pairs)


def other_core(value):
    return lax.ppermute(value, "tm", [(i, i ^ 1) for i in range(2 * NY)])


def ring(block):
    cut = 48
    forward, backward, blocks = block, block, [block]
    for _ in range(3):
        forward = to_group(forward, 0, 1)
        backward = to_group(backward, 0, -1)
        blocks += [forward, backward]
    return blocks + [to_group(forward[:cut], 0, 1), to_group(backward[cut:], 0, -1)]


def chip_edges(edge, other, small):
    odd = (lax.axis_index("tm") % 2) == 1
    early = jnp.where(odd, other, edge)
    late = jnp.where(odd, edge, other)
    far_r, far_i = small[MISC : MISC + 1], small[MISC + 1 : MISC + 2]
    s_r, s_i = times(far_r, far_i, early[:PAD], early[PAD : 2 * PAD])
    rest = early[2 * PAD :]
    return jnp.concatenate([s_r, s_i, rest], 0) + late


def on_device(field, occupations, dephase, detune_class, dot_count):
    const = lateral_constants()
    groups = dephase.shape[0]
    table = ((2 * ROWS, TOTAL_GROUPS), F32)
    big_shape = ((2, SPAN, LANES), F32)
    lag_shape = ((2, SPAN + ROWS, LANES), F32)
    kern_shape = ((2, ROWS, LANES), F32)
    corr_shape = ((ROWS, 2 * LANES), F32)
    entry_shape = ((2 * PAD, TOTAL_GROUPS), F32)
    inside_shape = ((PAD, TOTAL_GROUPS), F32)
    field_shape = ((2, SPAN, LATERAL), F32)

    pieces = occupations.reshape(groups, NX * NZ, OWN).transpose(1, 2, 0)
    rates = jnp.stack(
        [dephase, detune_class.astype(F32), dot_count.astype(F32), jnp.zeros_like(dephase)], 0
    )
    pieces = jnp.concatenate([pieces, jnp.broadcast_to(rates, (NX * NZ, 4, groups))], 1)
    params = lax.all_to_all(pieces, "group", 0, 0)
    params = params.transpose(1, 0, 2).reshape(PAD, TOTAL_GROUPS)

    (big,) = call(own_field_kernel, [big_shape])(field)
    fwd1, rev1, fwd8, small, edge = call(
        begin_kernel, [table, table, table, ((SMALL, TOTAL_GROUPS), F32), entry_shape]
    )(params, big)

    other = other_core(edge)
    both = chip_edges(edge, other, small)
    r1, r2, r3 = (to_time(both, k, False) for k in (1, 2, 3))
    lag, inside, entry = call(overlap_kernel, [lag_shape, inside_shape, entry_shape], [corr_shape], 6e9)(
        big, fwd1, fwd8, small
    )
    (part,) = call(first_inside_kernel, [big_shape], [kern_shape], 4e9)(params, lag, fwd8, small)
    send, met = call(first_finish_kernel, [((2 * OWN, SPAN), F32), inside_shape], [big_shape])(
        params, edge, other, r1, r2, r3, part, inside, entry, fwd1, small
    )

    once_nat, once_perm = const["once_nat"], const["once_perm"]
    twice_nat, twice_perm = const["twice_nat"], const["twice_perm"]
    own_high, own_low, pre = call(
        own_tables_kernel,
        [((2 * LATERAL, 2 * LANES), BF16), ((2 * LATERAL, 2 * LANES), BF16), ((SPAN, 2 * LANES), F32)],
    )(field, once_perm[0], once_perm[1], once_nat[0], once_nat[1])

    block = jnp.concatenate([send] + [to_group(send, k, 0) for k in (1, 2, 3)], 0)
    big, turned, edge = call(
        next_field_kernel,
        [big_shape, ((SPAN, 2 * LATERAL), F32), ((3 * PAD, TOTAL_GROUPS), F32)],
        [((2 * LATERAL, SPAN), F32)],
    )(*ring(block), own_high, own_low, pre, rev1, small, met)

    other = other_core(edge)
    both = chip_edges(edge, other, small)
    r1, r2, r3 = (to_time(both, k, True) for k in (1, 2, 3))
    lag, inside, entry = call(overlap_kernel, [lag_shape, inside_shape, entry_shape], [corr_shape], 6e9)(
        big, fwd1, fwd8, small
    )
    (send,) = call(
        last_finish_kernel, [((2 * OWN + PAD, SPAN), F32)], [kern_shape, big_shape]
    )(params, edge, other, r1, r2, r3, lag, inside, entry, fwd1, fwd8, small)
    (carried,) = call(carried_kernel, [field_shape], (), 4e9)(field, turned, *twice_nat, *twice_perm)

    gathered = [send] + [to_group(send, k, 0) for k in (1, 2, 3)]
    x = lax.axis_index("group") // NZ
    mets = [lax.dynamic_slice(g[2 * OWN :], (0, x * LANES), (PAD, LANES)) for g in gathered]
    block = jnp.concatenate([g[: 2 * OWN] for g in gathered] + [jnp.concatenate(mets, 1)], 0)
    amplified, polar, met = call(
        last_field_kernel,
        [field_shape, field_shape, ((PAD, LATERAL), F32)],
        [((2 * LATERAL, SPAN), F32), ((TOTAL_GROUPS, LANES), F32)],
    )(*ring(block), carried, once_perm[0], once_perm[1], const["place"])
    met = met + other_core(met)
    met = met + to_time(met, 1, True) + to_time(met, 2, True) + to_time(met, 3, True)
    return amplified, polar, occupations * jnp.exp(-SATURATE * met)


def solution(mesh):
    return jax.shard_map(
        on_device,
        mesh=mesh,
        in_specs=(P(None, "tm", None), P("group", None), P("group"), P("group"), P("group")),
        out_specs=(P(None, "tm", None), P(None, "tm", None), P("group", None)),
        check_vma=False,
    )
```

```python
import functools

import jax
import jax.numpy as jnp
import numpy as np
from jax import lax
from jax.experimental import pallas as pl
from jax.experimental.pallas import tpu as pltpu
from jax.sharding import PartitionSpec as P

NCLASS = 32
POL_GAIN = 0.25
SATURATE = 1.5
DIFF_PHASE = 6.0
ANGLE_UNIT = 0.01

NX, NZ, NY = 4, 8, 4
LATERAL = 384
TOTAL_TIME = 4096
TOTAL_GROUPS = 512
SPAN = 512
OWN = 12
PAD = 16
PHASES = 8
ROWS = 64
LANES = 128

F32 = jnp.float32
BF16 = jnp.bfloat16


def split2_np(value):
    import ml_dtypes

    high = value.astype(np.float32).astype(ml_dtypes.bfloat16)
    low = (value - high.astype(np.float64)).astype(np.float32).astype(ml_dtypes.bfloat16)
    return high, low


@functools.cache
def lateral_constants():
    column = np.arange(LATERAL)
    signed = np.where(column < LATERAL // 2, column, column - LATERAL).astype(np.float64)
    phase = DIFF_PHASE * signed**2 / float((LATERAL // 2) ** 2)
    twist = np.exp(-1j * phase)

    def real_form(multiplier):
        kernel = np.fft.ifft(multiplier)
        full = kernel[(column[None, :] - column[:, None]) % LATERAL]
        return np.block([[full.real, full.imag], [-full.imag, full.real]])

    owner = np.arange(NX * NZ)[:, None, None]
    part = np.arange(2)[None, :, None]
    inner = np.arange(OWN)[None, None, :]
    owner = owner.reshape(NX, NZ).T.reshape(-1, 1, 1)
    order = (part * LATERAL + owner * OWN + inner).reshape(-1)
    once = real_form(twist)
    place = np.zeros((2 * LATERAL, 2 * LATERAL))
    place[np.arange(2 * LATERAL), order] = 1.0
    return {
        "natural": split2_np(once),
        "gathered": split2_np(once[order]),
        "place": split2_np(place)[0],
    }


def halves(value):
    high = value.astype(BF16)
    low = (value - high.astype(F32)).astype(BF16)
    return high, low


def thirds(value):
    high = value.astype(BF16)
    rest = value - high.astype(F32)
    mid = rest.astype(BF16)
    low = (rest - mid.astype(F32)).astype(BF16)
    return high, mid, low


def mm(left, right):
    return jnp.dot(left, right, preferred_element_type=F32)


def mm3(left, right):
    (lh, ll), (rh, rl) = left, right
    return mm(lh, rh) + (mm(lh, rl) + mm(ll, rh))


def exact_pick(value, pick):
    high, mid, low = thirds(value)
    return (mm(high, pick) + mm(mid, pick)) + mm(low, pick)


def nt(left, right):
    return lax.dot_general(left, right, (((1,), (1,)), ((), ())), preferred_element_type=F32)


def nt3(left, right):
    (lh, ll), (rh, rl) = left, right
    return nt(lh, rh) + (nt(lh, rl) + nt(ll, rh))


def exact_nt(pick, value):
    high, mid, low = thirds(value)
    return (nt(pick, high) + nt(pick, mid)) + nt(pick, low)


def exact_place(pick, value):
    high, mid, low = thirds(value)
    return (mm(pick, high) + mm(pick, mid)) + mm(pick, low)


def iota(shape, axis):
    return lax.broadcasted_iota(jnp.int32, shape, axis)


def flag(condition):
    return jnp.where(condition, 1.0, 0.0).astype(BF16)


def own_pick():
    first = lax.axis_index("group") * OWN
    lane = iota((LATERAL, LANES), 1) % PAD
    return flag((iota((LATERAL, LANES), 0) == first + lane) & (lane < OWN))


def lane_phase(rows):
    return iota((rows, LANES), 1) // PAD


def times(ar, ai, br, bi):
    return ar * br - ai * bi, ar * bi + ai * br


AV, A64 = 0, 16
MISC = 32
SMALL = 40


def powers(first, step, rate, wave):
    exponent = (iota((8, 1), 0) * step + first).astype(F32)
    magnitude = jnp.exp(-exponent * rate)
    angle = (exponent * wave) * ANGLE_UNIT
    return magnitude * jnp.cos(angle), -magnitude * jnp.sin(angle)


def time_rows(value):
    phase = lane_phase(ROWS)
    out = value[:ROWS]
    for q in range(1, PHASES):
        out = jnp.where(phase == q, value[q * ROWS : (q + 1) * ROWS], out)
    return out


def against(re, im, table):
    left = jnp.concatenate([jnp.concatenate([re, -im], 0), jnp.concatenate([im, re], 0)], 1).T
    out = mm3(halves(left), table)
    return out[:LANES], out[LANES:]


def run_edges(s, z, small_ref):
    step_r, step_i = small_ref[A64 + 1 : A64 + 2], small_ref[A64 + 9 : A64 + 10]
    states = []
    for q in range(PHASES):
        part = slice(q * PAD, (q + 1) * PAD)
        if s is None:
            states.append((jnp.zeros((PAD, TOTAL_GROUPS), F32),) * 2)
            s = z[0][part], z[1][part]
        else:
            states.append(s)
            r, i = times(step_r, step_i, *s)
            s = r + z[0][part], i + z[1][part]
    return states, s


def stacked(states):
    return jnp.concatenate([r for r, _ in states], 0), jnp.concatenate([i for _, i in states], 0)


def own_rows(real, imag, rows_ref):
    pick = own_pick()
    rows_ref[:ROWS] = time_rows(exact_pick(real, pick))
    rows_ref[ROWS:] = time_rows(exact_pick(imag, pick))


def own_field_kernel(field_ref, rows_ref):
    own_rows(field_ref[0], field_ref[1], rows_ref)


def pieces_kernel(occupied_ref, rate_ref, class_ref, count_ref, out_ref):
    groups = occupied_ref.shape[0]
    spread = flag(iota((groups, PAD * groups), 1) % groups == iota((groups, PAD * groups), 0))
    tiled = exact_pick(occupied_ref[...].T, spread)
    column = iota((LATERAL, PAD * groups), 0)
    tiled = jnp.where(column % OWN == iota((LATERAL, PAD * groups), 1) // groups, tiled, 0.0)
    owner = iota((NX * NZ, LATERAL), 0)
    out = exact_place(flag(iota((NX * NZ, LATERAL), 1) // OWN == owner), tiled)
    rates = [rate_ref[...], class_ref[...].astype(F32), count_ref[...].astype(F32)]
    lane = iota((8, PAD * groups), 1) // groups
    for k, value in enumerate(rates):
        row = exact_pick(jnp.broadcast_to(value.reshape(1, groups), (8, groups)), spread)
        out = out + jnp.where(lane == OWN + k, row, 0.0)[:1]
    out_ref[...] = out


def turn_kernel(field_ref, high_ref, low_ref, out_ref):
    real, imag = halves(field_ref[0]), halves(field_ref[1])
    for c in range(2):
        cols = slice(c * LATERAL, (c + 1) * LATERAL)
        out_ref[c] = mm3(real, (high_ref[:LATERAL, cols], low_ref[:LATERAL, cols])) + mm3(
            imag, (high_ref[LATERAL:, cols], low_ref[LATERAL:, cols])
        )


def make_tables(params_ref, fwd_ref, rev_ref, small_ref):
    rate = params_ref[12:13]
    wave = 2.0 * params_ref[13:14] - (NCLASS - 1)
    count = params_ref[14:15]
    av_r, av_i = powers(0, 1, rate, wave)
    back_r, back_i = powers(7, -1, rate, wave)
    a8_r, a8_i = powers(0, 8, rate, wave)
    a64_r, a64_i = powers(0, 64, rate, wave)
    far_r, far_i = powers(0, SPAN, rate, wave)
    for u in range(8):
        top = slice(8 * u, 8 * u + 8)
        bottom = slice(ROWS + 8 * u, ROWS + 8 * u + 8)
        fwd_ref[top], fwd_ref[bottom] = times(a8_r[u : u + 1], a8_i[u : u + 1], av_r, av_i)
        rev_ref[top], rev_ref[bottom] = times(
            a8_r[7 - u : 8 - u], a8_i[7 - u : 8 - u], back_r, back_i
        )
    small_ref[AV : AV + 8] = av_r
    small_ref[AV + 8 : AV + 16] = av_i
    small_ref[A64 : A64 + 8] = a64_r
    small_ref[A64 + 8 : A64 + 16] = a64_i
    drive = jnp.sqrt((1.0 - av_r[1:2]) ** 2 + av_i[1:2] ** 2)
    small_ref[MISC : MISC + 1] = far_r[1:2]
    small_ref[MISC + 1 : MISC + 2] = far_i[1:2]
    small_ref[MISC + 2 : MISC + 3] = far_r[2:3]
    small_ref[MISC + 3 : MISC + 4] = far_i[2:3]
    small_ref[MISC + 4 : MISC + 5] = POL_GAIN / TOTAL_GROUPS * count * drive
    small_ref[MISC + 5 : MISC + 6] = drive / TOTAL_TIME
    small_ref[MISC + 6 : MISC + 8] = jnp.zeros((2, TOTAL_GROUPS), F32)


def coupling_of(params_ref, small_ref):
    occupied = jnp.concatenate([params_ref[:OWN], jnp.zeros((PAD - OWN, TOTAL_GROUPS), F32)], 0)
    return small_ref[MISC + 4 : MISC + 5] * occupied


def shifts(rows_ref, shift_ref):
    row = iota((ROWS, LANES), 0)
    for c in range(2):
        value = rows_ref[c * ROWS : (c + 1) * ROWS]
        shift_ref[c, 0] = value
        for v in range(1, 8):
            shift_ref[c, v] = jnp.where(row >= v, pltpu.roll(value, v, 0), 0.0)


def inside_response(coupling, shift_ref, fwd_ref, kern_ref, polar_ref):
    weight = jnp.concatenate([coupling] * PHASES, 0)
    kern_ref[...] = nt3(halves(fwd_ref[...]), halves(weight))
    for j in range(8):
        acc_r = acc_i = None
        for u in range(j + 1):
            at = slice(8 * (j - u), 8 * (j - u) + 8)
            for v in range(8):
                k_r = kern_ref[8 * u + v : 8 * u + v + 1]
                k_i = kern_ref[ROWS + 8 * u + v : ROWS + 8 * u + v + 1]
                e_r, e_i = shift_ref[0, v, at], shift_ref[1, v, at]
                r, i = times(k_r, k_i, e_r, e_i)
                acc_r, acc_i = (r, i) if acc_r is None else (acc_r + r, acc_i + i)
        polar_ref[8 * j : 8 * j + 8] = acc_r
        polar_ref[ROWS + 8 * j : ROWS + 8 * j + 8] = acc_i


def entered_response(coupling, states_r, states_i, polar_ref, fwd_ref, small_ref, send_ref):
    weight = jnp.concatenate([coupling] * PHASES, 0)
    d_r, d_i = times(small_ref[AV + 1 : AV + 2], small_ref[AV + 9 : AV + 10], states_r, states_i)
    table = halves(fwd_ref[...])
    by_r = nt3(table, halves(weight * d_r))
    by_i = nt3(table, halves(weight * d_i))
    real = polar_ref[:ROWS] + (by_r[:ROWS] - by_i[ROWS:])
    imag = polar_ref[ROWS:] + (by_r[ROWS:] + by_i[:ROWS])
    for c, value in enumerate((real, imag)):
        turned = value.T
        parts = [turned[q * PAD : q * PAD + OWN] for q in range(PHASES)]
        send_ref[c * OWN : (c + 1) * OWN] = jnp.concatenate(parts, 1)


def first_kernel(
    params_ref, rows_ref, other_ref, p1, p2, p3,
    fwd_ref, rev_ref, small_ref, send_ref, states_ref, kern_ref, polar_ref, shift_ref,
):
    make_tables(params_ref, fwd_ref, rev_ref, small_ref)
    shifts(rows_ref, shift_ref)
    coupling = coupling_of(params_ref, small_ref)
    inside_response(coupling, shift_ref, fwd_ref, kern_ref, polar_ref)
    rev = halves(rev_ref[...])
    odd = (lax.axis_index("tm") % 2) == 1
    s = None
    for pair in (p3, p2, p1):
        mine, other = pair[: 2 * ROWS], pair[2 * ROWS :]
        for rows in (jnp.where(odd, other, mine), jnp.where(odd, mine, other)):
            _, s = run_edges(s, against(rows[:ROWS], rows[ROWS:], rev), small_ref)
    _, later = run_edges(s, against(other_ref[:ROWS], other_ref[ROWS:], rev), small_ref)
    s = jnp.where(odd, later[0], s[0]), jnp.where(odd, later[1], s[1])
    states, _ = run_edges(s, against(rows_ref[:ROWS], rows_ref[ROWS:], rev), small_ref)
    states_r, states_i = stacked(states)
    states_ref[:LANES] = states_r
    states_ref[LANES:] = states_i
    entered_response(coupling, states_r, states_i, polar_ref, fwd_ref, small_ref, send_ref)


def inside_overlap(rows_ref, shift_ref, fwd_ref):
    corr_r, corr_i = [], []
    for u in range(8):
        sum_r, sum_i = [], []
        for v in range(8):
            acc_r = acc_i = None
            for j in range(u, 8):
                e_r = rows_ref[8 * j : 8 * j + 8]
                e_i = rows_ref[ROWS + 8 * j : ROWS + 8 * j + 8]
                at = slice(8 * (j - u), 8 * (j - u) + 8)
                r, i = times(e_r, -e_i, shift_ref[0, v, at], shift_ref[1, v, at])
                acc_r, acc_i = (r, i) if acc_r is None else (acc_r + r, acc_i + i)
            sum_r.append(jnp.sum(acc_r, axis=0, keepdims=True))
            sum_i.append(jnp.sum(acc_i, axis=0, keepdims=True))
        corr_r += sum_r
        corr_i += sum_i
    left = jnp.concatenate(corr_r + [-value for value in corr_i], 0).T
    z = mm3(halves(left), halves(fwd_ref[...]))
    return functools.reduce(lambda a, b: a + b, [z[q * PAD : (q + 1) * PAD] for q in range(PHASES)])


def entry_overlap(rows_ref, fwd_ref):
    return against(rows_ref[:ROWS], -rows_ref[ROWS:], halves(fwd_ref[...]))


def met_of(inside, z_r, z_i, states_r, states_i, small_ref):
    r, i = times(states_r, states_i, z_r, z_i)
    sum_r, sum_i = inside, jnp.zeros((PAD, TOTAL_GROUPS), F32)
    one_r, one_i = small_ref[AV + 1 : AV + 2], small_ref[AV + 9 : AV + 10]
    for q in range(PHASES):
        part = slice(q * PAD, (q + 1) * PAD)
        sum_r = sum_r + (one_r * r[part] - one_i * i[part])
    return sum_r * small_ref[MISC + 5 : MISC + 6]


def first_overlap_kernel(rows_ref, fwd_ref, small_ref, states_ref, met_ref, shift_ref):
    shifts(rows_ref, shift_ref)
    inside = inside_overlap(rows_ref, shift_ref, fwd_ref)
    z_r, z_i = entry_overlap(rows_ref, fwd_ref)
    met_ref[...] = met_of(inside, z_r, z_i, states_ref[:LANES], states_ref[LANES:], small_ref)


def second_overlap_kernel(rows_ref, fwd_ref, inside_ref, entry_ref, shift_ref):
    shifts(rows_ref, shift_ref)
    inside_ref[...] = inside_overlap(rows_ref, shift_ref, fwd_ref)
    entry_ref[:LANES], entry_ref[LANES:] = entry_overlap(rows_ref, fwd_ref)


def second_inside_kernel(
    rows_ref, params_ref, m0, m1, fwd_ref, small_ref, polar_ref, coupling_ref, kern_ref, shift_ref
):
    coupling = coupling_of(params_ref, small_ref) * jnp.exp(-SATURATE * (m0[...] + m1[...]))
    coupling_ref[...] = coupling
    shifts(rows_ref, shift_ref)
    inside_response(coupling, shift_ref, fwd_ref, kern_ref, polar_ref)


def chip_kernel(edge_ref, other_ref, small_ref, out_ref):
    odd = (lax.axis_index("tm") % 2) == 1
    early = jnp.where(odd, other_ref[...], edge_ref[...])
    late = jnp.where(odd, edge_ref[...], other_ref[...])
    r, i = times(small_ref[MISC : MISC + 1], small_ref[MISC + 1 : MISC + 2], early[:PAD], early[PAD:])
    out_ref[:PAD] = r + late[:PAD]
    out_ref[PAD:] = i + late[PAD:]


def chips_kernel(own_ref, near_ref, small_ref, out_ref):
    far_r, far_i = small_ref[MISC + 2 : MISC + 3], small_ref[MISC + 3 : MISC + 4]
    r, i = times(far_r, far_i, near_ref[:PAD], near_ref[PAD:])
    out_ref[:PAD] = r + own_ref[:PAD]
    out_ref[PAD:] = i + own_ref[PAD:]


def second_finish_kernel(
    coupling_ref, other_ref, near_ref, far_ref, part_ref, inside_ref, entry_ref, met_ref, states_ref,
    fwd_ref, small_ref, send_ref,
):
    s_r, s_i = times(
        small_ref[MISC + 2 : MISC + 3], small_ref[MISC + 3 : MISC + 4], far_ref[:PAD], far_ref[PAD:]
    )
    s_r, s_i = s_r + near_ref[:PAD], s_i + near_ref[PAD:]
    later_r, later_i = times(small_ref[MISC : MISC + 1], small_ref[MISC + 1 : MISC + 2], s_r, s_i)
    odd = (lax.axis_index("tm") % 2) == 1
    s_r = jnp.where(odd, later_r + other_ref[:PAD], s_r)
    s_i = jnp.where(odd, later_i + other_ref[PAD:], s_i)
    states_r, states_i = stacked(
        [
            times(small_ref[A64 + q : A64 + q + 1], small_ref[A64 + 8 + q : A64 + 9 + q], s_r, s_i)
            for q in range(PHASES)
        ]
    )
    states_r = states_r + states_ref[:LANES]
    states_i = states_i + states_ref[LANES:]
    met = met_of(inside_ref[...], entry_ref[:LANES], entry_ref[LANES:], states_r, states_i, small_ref)
    send_ref[2 * OWN :] = met_ref[...] + met
    entered_response(coupling_ref[...], states_r, states_i, part_ref, fwd_ref, small_ref, send_ref)


class Planes:
    def __init__(self, distances, refs):
        refs = list(refs)
        self.blocks = {d: [refs.pop(0) for _ in range(2 if d == 4 else 1)] for d in distances}

    @staticmethod
    def count(distances):
        return sum(2 if d == 4 else 1 for d in distances)

    def turned(self, distances, whole_ref):
        x = lax.axis_index("group") // NZ
        for n, d in enumerate(distances):
            for r in range(NX):
                at = pl.multiple_of(n * 96 + lax.rem(x - r + NX, NX) * 24, 8)
                block, low = self.blocks[d][0], 24 * r
                if d == 4 and r >= 2:
                    block, low = self.blocks[d][1], 24 * (r - 2)
                whole_ref[pl.ds(at, 24)] = block[low : low + 24]
        return whole_ref[: 96 * len(distances)].T

    @staticmethod
    def rows(distances, table_ref, cols):
        z = lax.axis_index("group") % NZ
        starts = [pl.multiple_of(lax.rem(z + d + NZ, NZ) * 96, 32) for d in distances]
        return jnp.concatenate([table_ref[pl.ds(at, 96), cols] for at in starts], 0)


def next_field_kernel(*refs):
    planes, refs = Planes(RING[7:], refs[:2]), refs[2:]
    field_in, high_ref, low_ref, rev_ref, small_ref = refs[:5]
    field_ref, rows_ref, states_ref, edge_ref, whole_ref = refs[5:]
    turned = halves(planes.turned(RING[7:], whole_ref))
    for c in range(2):
        cols = slice(c * LATERAL, (c + 1) * LATERAL)
        table = [Planes.rows(RING[7:], ref, cols) for ref in (high_ref, low_ref)]
        field_ref[c] = field_in[c] + mm3(turned, table)
    own_rows(field_ref[0], field_ref[1], rows_ref)
    z = against(rows_ref[:ROWS], rows_ref[ROWS:], halves(rev_ref[...]))
    states, (s_r, s_i) = run_edges(None, z, small_ref)
    states_ref[:LANES], states_ref[LANES:] = stacked(states)
    edge_ref[:PAD] = s_r
    edge_ref[PAD:] = s_i


def spread_kernel(distances, field_at, polar_at, start, *refs):
    count = Planes.count(distances)
    planes, refs = Planes(distances, refs[:count]), list(refs[count:])
    whole_ref = refs.pop()
    field_in = field_tables = polar_in = place_ref = None
    if field_at:
        field_in, field_tables = refs.pop(0), (refs.pop(0), refs.pop(0))
    if polar_at:
        polar_in = None if start else refs.pop(0)
        place_ref = refs.pop(0)
    if field_at:
        out_ref = refs.pop(0)
        turned = halves(planes.turned(field_at, whole_ref))
        for c in range(2):
            cols = slice(c * LATERAL, (c + 1) * LATERAL)
            table = [Planes.rows(field_at, ref, cols) for ref in field_tables]
            out_ref[c] = field_in[c] + mm3(turned, table)
    if polar_at:
        out_ref = refs.pop(0)
        turned = planes.turned(polar_at, whole_ref)
        for c in range(2):
            cols = slice(c * LATERAL, (c + 1) * LATERAL)
            value = exact_pick(turned, Planes.rows(polar_at, place_ref, cols))
            out_ref[c] = value if start else polar_in[c] + value


def met_kernel(*refs):
    planes, (met_ref, gathered_ref) = Planes(RING, refs[:9]), refs[9:]
    me = lax.axis_index("group")
    x, z = me // NZ, me % NZ
    for d in RING:
        for r in range(NX):
            owner = lax.rem(x - r + NX, NX) * NZ + lax.rem(z + d + NZ, NZ)
            at = pl.multiple_of(owner * PAD, 8)
            block, low = (planes.blocks[d][1], 48) if d == 4 else (planes.blocks[d][0], 96)
            gathered_ref[pl.ds(at, PAD)] = block[low:, LANES * r : LANES * r + LANES]
    mine = flag(iota((PAD, LANES), 1) == iota((PAD, LANES), 0) + PAD * z)
    turned = exact_nt(mine, gathered_ref[...])
    row = iota((TOTAL_GROUPS, LATERAL), 0)
    inner = row % PAD
    col = iota((TOTAL_GROUPS, LATERAL), 1)
    met_ref[...] = exact_pick(turned, flag((inner < OWN) & (col == (row // PAD) * OWN + inner)))


RING = (0, -1, 1, -2, 2, -3, 3, 4)


def call(kernel, outs, scratch=(), cost=2e9):
    return pl.pallas_call(
        kernel,
        out_shape=[jax.ShapeDtypeStruct(shape, dtype) for shape, dtype in outs],
        scratch_shapes=[pltpu.VMEM(shape, dtype) for shape, dtype in scratch],
        compiler_params=pltpu.CompilerParams(vmem_limit_bytes=28 * 1024 * 1024),
        cost_estimate=pl.CostEstimate(flops=int(cost), bytes_accessed=1 << 20, transcendentals=0),
    )


def to_group(value, dx, dz):
    pairs = [
        (x * NZ + z, ((x + dx) % NX) * NZ + (z + dz) % NZ) for x in range(NX) for z in range(NZ)
    ]
    return lax.ppermute(value, "group", pairs)


def to_time(value, dy, wrap):
    pairs = [
        (2 * y + c, 2 * ((y + dy) % NY) + c)
        for y in range(NY)
        for c in range(2)
        if wrap or y + dy < NY
    ]
    return lax.ppermute(value, "tm", pairs)


def to_chip(value, bit):
    pairs = [(2 * y + c, 2 * (y ^ bit) + c) for y in range(NY) for c in range(2)]
    return lax.ppermute(value, "tm", pairs)


def other_core(value):
    return lax.ppermute(value, "tm", [(i, i ^ 1) for i in range(2 * NY)])


def together(*values):
    return lax.optimization_barrier(values)


def step_on(blocks, d):
    if d == 4:
        return to_group(blocks[-3][0][:48], 0, 1), to_group(blocks[3][0][48:], 0, -1)
    near = (blocks[0][0], blocks[0][0]) if d == 1 else (blocks[1 - d][0], blocks[d - 1][0])
    return to_group(near[0], 0, 1), to_group(near[1], 0, -1)


def listed(blocks, distances):
    return [block for d in distances for block in blocks[d]]


def on_device(field, occupations, dephase, detune_class, dot_count):
    const = lateral_constants()
    natural, gathered = const["natural"], const["gathered"]
    table = ((2 * ROWS, TOTAL_GROUPS), F32)
    rows_shape = ((2 * ROWS, LANES), F32)
    shift_shape = ((2, 8, ROWS, LANES), F32)
    states_shape = ((2 * LANES, TOTAL_GROUPS), F32)
    edge_shape = ((2 * PAD, TOTAL_GROUPS), F32)
    met_shape = ((PAD, TOTAL_GROUPS), F32)
    field_shape = ((2, SPAN, LATERAL), F32)
    whole_shape = ((2 * LATERAL, SPAN), F32)

    def spread(blocks, field_at, polar_at, field_in=None, polar_in=None):
        distances = [d for d in RING if d in field_at or d in polar_at]
        extra = [field_in, *gathered] if field_at else []
        if polar_at:
            extra += ([] if polar_in is None else [polar_in]) + [const["place"]]
        outs = [field_shape] * (bool(field_at) + bool(polar_at))
        kernel = functools.partial(spread_kernel, distances, field_at, polar_at, polar_in is None)
        return call(kernel, outs, [whole_shape], 3e9)(*listed(blocks, distances), *extra)

    (pieces,) = call(pieces_kernel, [((NX * NZ, PAD * occupations.shape[0]), F32)])(
        occupations, dephase, detune_class, dot_count
    )
    params = lax.all_to_all(pieces, "group", 0, 0, tiled=True)
    (rows,) = call(own_field_kernel, [rows_shape])(field)
    other = other_core(rows)
    pair = jnp.concatenate([rows, other], 0)
    p1, p2, p3 = (to_time(pair, k, False) for k in (1, 2, 3))
    (turned,) = call(turn_kernel, [field_shape], (), 4e9)(field, *natural)
    params, turned = together(params, turned)
    params = params.reshape(NX * NZ, PAD, -1).transpose(1, 0, 2).reshape(PAD, TOTAL_GROUPS)
    fwd, rev, small, send, states = call(
        first_kernel,
        [table, table, ((SMALL, TOTAL_GROUPS), F32), ((2 * OWN, SPAN), F32), states_shape],
        [rows_shape, rows_shape, shift_shape],
        4e9,
    )(params, rows, other, p1, p2, p3)

    near = [to_group(send, k, 0) for k in (1, 2, 3)]
    (met,) = call(first_overlap_kernel, [met_shape], [shift_shape])(rows, fwd, small, states)
    send, met, *near = together(send, met, *near)
    blocks = {0: [jnp.concatenate([send] + near, 0)]}
    f, b = step_on(blocks, 1)
    met_two = met + other_core(met)
    f, b, met_two = together(f, b, met_two)
    blocks[-1], blocks[1] = [f], [b]
    f, b = step_on(blocks, 2)
    met_four = met_two + to_chip(met_two, 1)
    (turned,) = spread(blocks, RING[:3], (), turned)
    f, b, met_four, turned = together(f, b, met_four, turned)
    blocks[-2], blocks[2] = [f], [b]
    f, b = step_on(blocks, 3)
    met_rest = to_chip(met_four, 2)
    (turned,) = spread(blocks, RING[3:5], (), turned)
    f, b, met_rest, turned = together(f, b, met_rest, turned)
    blocks[-3], blocks[3] = [f], [b]
    f, b = step_on(blocks, 4)
    (turned,) = spread(blocks, RING[5:7], (), turned)
    f, b, turned = together(f, b, turned)
    blocks[4] = [f, b]
    field, rows, states, edge = call(
        next_field_kernel, [field_shape, rows_shape, states_shape, edge_shape], [whole_shape]
    )(*blocks[4], turned, *gathered, rev, small)

    other = other_core(edge)
    (chip,) = call(chip_kernel, [edge_shape])(edge, other, small)
    near_chip = to_time(chip, 1, False)
    inside, entry = call(second_overlap_kernel, [met_shape, states_shape], [shift_shape])(rows, fwd)
    near_chip, inside, entry = together(near_chip, inside, entry)
    (chips,) = call(chips_kernel, [edge_shape])(chip, near_chip, small)
    far_chip = to_time(chips, 2, False)
    part, coupling = call(second_inside_kernel, [rows_shape, met_shape], [rows_shape, shift_shape])(
        rows, params, met_four, met_rest, fwd, small
    )
    far_chip, part, coupling = together(far_chip, part, coupling)
    (send,) = call(second_finish_kernel, [((2 * OWN + PAD, SPAN), F32)])(
        coupling, other, near_chip, far_chip, part, inside, entry, met, states, fwd, small
    )

    near = [to_group(send, k, 0) for k in (1, 2, 3)]
    (turned,) = call(turn_kernel, [field_shape], (), 4e9)(field, *natural)
    send, turned, *near = together(send, turned, *near)
    x = lax.axis_index("group") // NZ
    sent = [send] + near
    mets = [lax.dynamic_slice(g[2 * OWN :], (0, x * LANES), (PAD, LANES)) for g in sent]
    blocks = {0: [jnp.concatenate([g[: 2 * OWN] for g in sent] + [jnp.concatenate(mets, 1)], 0)]}
    f, b = step_on(blocks, 1)
    f, b = together(f, b)
    blocks[-1], blocks[1] = [f], [b]
    f, b = step_on(blocks, 2)
    (polar,) = spread(blocks, (), RING[:3])
    f, b, polar = together(f, b, polar)
    blocks[-2], blocks[2] = [f], [b]
    f, b = step_on(blocks, 3)
    (amplified,) = spread(blocks, RING[:5], (), turned)
    f, b, amplified = together(f, b, amplified)
    blocks[-3], blocks[3] = [f], [b]
    f, b = step_on(blocks, 4)
    amplified, polar = spread(blocks, RING[5:7], RING[3:7], amplified, polar)
    f, b, polar, amplified = together(f, b, polar, amplified)
    blocks[4] = [f, b]
    (met,) = call(met_kernel, [((PAD, LATERAL), F32)], [((TOTAL_GROUPS, LANES), F32)])(*listed(blocks, RING))
    met = met + other_core(met)
    far = [to_time(met, k, True) for k in (1, 2, 3)]
    amplified, polar = spread(blocks, RING[7:], RING[7:], amplified, polar)
    met = met + (far[0] + far[1] + far[2])
    return amplified, polar, occupations * jnp.exp(-SATURATE * met)


def solution(mesh):
    return jax.shard_map(
        on_device,
        mesh=mesh,
        in_specs=(P(None, "tm", None), P("group", None), P("group"), P("group"), P("group")),
        out_specs=(P(None, "tm", None), P(None, "tm", None), P("group", None)),
        check_vma=False,
    )
```

```python
import functools

import jax
import jax.numpy as jnp
import numpy as np
from jax import lax
from jax.experimental import pallas as pl
from jax.experimental.pallas import tpu as pltpu
from jax.sharding import PartitionSpec as P

NCLASS = 32
POL_GAIN = 0.25
SATURATE = 1.5
DIFF_PHASE = 6.0
ANGLE_UNIT = 0.01

NX, NZ, NY = 4, 8, 4
LATERAL = 384
TOTAL_TIME = 4096
TOTAL_GROUPS = 512
SPAN = 512
OWN = 12
PAD = 16
PHASES = 8
ROWS = 64
LANES = 128

F32 = jnp.float32
BF16 = jnp.bfloat16


def split2_np(value):
    import ml_dtypes

    high = value.astype(np.float32).astype(ml_dtypes.bfloat16)
    low = (value - high.astype(np.float64)).astype(np.float32).astype(ml_dtypes.bfloat16)
    return high, low


@functools.cache
def lateral_constants():
    column = np.arange(LATERAL)
    signed = np.where(column < LATERAL // 2, column, column - LATERAL).astype(np.float64)
    phase = DIFF_PHASE * signed**2 / float((LATERAL // 2) ** 2)
    twist = np.exp(-1j * phase)

    def real_form(multiplier):
        kernel = np.fft.ifft(multiplier)
        full = kernel[(column[None, :] - column[:, None]) % LATERAL]
        return np.block([[full.real, full.imag], [-full.imag, full.real]])

    owner = np.arange(NX * NZ)[:, None, None]
    part = np.arange(2)[None, :, None]
    inner = np.arange(OWN)[None, None, :]
    owner = owner.reshape(NX, NZ).T.reshape(-1, 1, 1)
    order = (part * LATERAL + owner * OWN + inner).reshape(-1)
    once = real_form(twist)
    place = np.zeros((2 * LATERAL, 2 * LATERAL))
    place[np.arange(2 * LATERAL), order] = 1.0
    return {
        "natural": split2_np(once),
        "gathered": split2_np(once[order]),
        "place": split2_np(place)[0],
    }


def halves(value):
    high = value.astype(BF16)
    low = (value - high.astype(F32)).astype(BF16)
    return high, low


def thirds(value):
    high = value.astype(BF16)
    rest = value - high.astype(F32)
    mid = rest.astype(BF16)
    low = (rest - mid.astype(F32)).astype(BF16)
    return high, mid, low


def mm(left, right):
    return jnp.dot(left, right, preferred_element_type=F32)


def mm3(left, right):
    (lh, ll), (rh, rl) = left, right
    return mm(lh, rh) + (mm(lh, rl) + mm(ll, rh))


def exact_pick(value, pick):
    high, mid, low = thirds(value)
    return (mm(high, pick) + mm(mid, pick)) + mm(low, pick)


def nt(left, right):
    return lax.dot_general(left, right, (((1,), (1,)), ((), ())), preferred_element_type=F32)


def nt3(left, right):
    (lh, ll), (rh, rl) = left, right
    return nt(lh, rh) + (nt(lh, rl) + nt(ll, rh))


def exact_nt(pick, value):
    high, mid, low = thirds(value)
    return (nt(pick, high) + nt(pick, mid)) + nt(pick, low)


def exact_place(pick, value):
    high, mid, low = thirds(value)
    return (mm(pick, high) + mm(pick, mid)) + mm(pick, low)


def iota(shape, axis):
    return lax.broadcasted_iota(jnp.int32, shape, axis)


def flag(condition):
    return jnp.where(condition, 1.0, 0.0).astype(BF16)


def own_pick():
    first = lax.axis_index("group") * OWN
    lane = iota((LATERAL, LANES), 1) % PAD
    return flag((iota((LATERAL, LANES), 0) == first + lane) & (lane < OWN))


def lane_phase(rows):
    return iota((rows, LANES), 1) // PAD


def times(ar, ai, br, bi):
    return ar * br - ai * bi, ar * bi + ai * br


AV, A64 = 0, 16
MISC = 32
SMALL = 40


def powers(first, step, rate, wave):
    exponent = (iota((8, 1), 0) * step + first).astype(F32)
    magnitude = jnp.exp(-exponent * rate)
    angle = (exponent * wave) * ANGLE_UNIT
    return magnitude * jnp.cos(angle), -magnitude * jnp.sin(angle)


def time_rows(value):
    phase = lane_phase(ROWS)
    out = value[:ROWS]
    for q in range(1, PHASES):
        out = jnp.where(phase == q, value[q * ROWS : (q + 1) * ROWS], out)
    return out


def against(re, im, table):
    left = jnp.concatenate([jnp.concatenate([re, -im], 0), jnp.concatenate([im, re], 0)], 1).T
    out = mm3(halves(left), table)
    return out[:LANES], out[LANES:]


def run_edges(s, z, small_ref):
    step_r, step_i = small_ref[A64 + 1 : A64 + 2], small_ref[A64 + 9 : A64 + 10]
    states = []
    for q in range(PHASES):
        part = slice(q * PAD, (q + 1) * PAD)
        if s is None:
            states.append((jnp.zeros((PAD, TOTAL_GROUPS), F32),) * 2)
            s = z[0][part], z[1][part]
        else:
            states.append(s)
            r, i = times(step_r, step_i, *s)
            s = r + z[0][part], i + z[1][part]
    return states, s


def stacked(states):
    return jnp.concatenate([r for r, _ in states], 0), jnp.concatenate([i for _, i in states], 0)


def own_rows(real, imag, rows_ref):
    pick = own_pick()
    rows_ref[:ROWS] = time_rows(exact_pick(real, pick))
    rows_ref[ROWS:] = time_rows(exact_pick(imag, pick))


def own_field_kernel(field_ref, rows_ref):
    own_rows(field_ref[0], field_ref[1], rows_ref)


def pieces_kernel(occupied_ref, rate_ref, class_ref, count_ref, out_ref):
    groups = occupied_ref.shape[0]
    spread = flag(iota((groups, PAD * groups), 1) % groups == iota((groups, PAD * groups), 0))
    tiled = exact_pick(occupied_ref[...].T, spread)
    column = iota((LATERAL, PAD * groups), 0)
    tiled = jnp.where(column % OWN == iota((LATERAL, PAD * groups), 1) // groups, tiled, 0.0)
    owner = iota((NX * NZ, LATERAL), 0)
    out = exact_place(flag(iota((NX * NZ, LATERAL), 1) // OWN == owner), tiled)
    rates = [rate_ref[...], class_ref[...].astype(F32), count_ref[...].astype(F32)]
    lane = iota((8, PAD * groups), 1) // groups
    for k, value in enumerate(rates):
        row = exact_pick(jnp.broadcast_to(value.reshape(1, groups), (8, groups)), spread)
        out = out + jnp.where(lane == OWN + k, row, 0.0)[:1]
    out_ref[...] = out


def turn_kernel(field_ref, high_ref, low_ref, out_ref):
    real, imag = halves(field_ref[0]), halves(field_ref[1])
    for c in range(2):
        cols = slice(c * LATERAL, (c + 1) * LATERAL)
        out_ref[c] = mm3(real, (high_ref[:LATERAL, cols], low_ref[:LATERAL, cols])) + mm3(
            imag, (high_ref[LATERAL:, cols], low_ref[LATERAL:, cols])
        )


def make_tables(params_ref, fwd_ref, rev_ref, small_ref):
    rate = params_ref[12:13]
    wave = 2.0 * params_ref[13:14] - (NCLASS - 1)
    count = params_ref[14:15]
    av_r, av_i = powers(0, 1, rate, wave)
    back_r, back_i = powers(7, -1, rate, wave)
    a8_r, a8_i = powers(0, 8, rate, wave)
    a64_r, a64_i = powers(0, 64, rate, wave)
    far_r, far_i = powers(0, SPAN, rate, wave)
    for u in range(8):
        top = slice(8 * u, 8 * u + 8)
        bottom = slice(ROWS + 8 * u, ROWS + 8 * u + 8)
        fwd_ref[top], fwd_ref[bottom] = times(a8_r[u : u + 1], a8_i[u : u + 1], av_r, av_i)
        rev_ref[top], rev_ref[bottom] = times(
            a8_r[7 - u : 8 - u], a8_i[7 - u : 8 - u], back_r, back_i
        )
    small_ref[AV : AV + 8] = av_r
    small_ref[AV + 8 : AV + 16] = av_i
    small_ref[A64 : A64 + 8] = a64_r
    small_ref[A64 + 8 : A64 + 16] = a64_i
    drive = jnp.sqrt((1.0 - av_r[1:2]) ** 2 + av_i[1:2] ** 2)
    small_ref[MISC : MISC + 1] = far_r[1:2]
    small_ref[MISC + 1 : MISC + 2] = far_i[1:2]
    small_ref[MISC + 2 : MISC + 3] = far_r[2:3]
    small_ref[MISC + 3 : MISC + 4] = far_i[2:3]
    small_ref[MISC + 4 : MISC + 5] = POL_GAIN / TOTAL_GROUPS * count * drive
    small_ref[MISC + 5 : MISC + 6] = drive / TOTAL_TIME
    small_ref[MISC + 6 : MISC + 8] = jnp.zeros((2, TOTAL_GROUPS), F32)


def coupling_of(params_ref, small_ref):
    occupied = jnp.concatenate([params_ref[:OWN], jnp.zeros((PAD - OWN, TOTAL_GROUPS), F32)], 0)
    return small_ref[MISC + 4 : MISC + 5] * occupied


def shifts(rows_ref, shift_ref):
    row = iota((ROWS, LANES), 0)
    for c in range(2):
        value = rows_ref[c * ROWS : (c + 1) * ROWS]
        shift_ref[c, 0] = value
        for v in range(1, 8):
            shift_ref[c, v] = jnp.where(row >= v, pltpu.roll(value, v, 0), 0.0)


def inside_response(coupling, shift_ref, fwd_ref, kern_ref, polar_ref):
    weight = jnp.concatenate([coupling] * PHASES, 0)
    kern_ref[...] = nt3(halves(fwd_ref[...]), halves(weight))
    for j in range(8):
        acc_r = acc_i = None
        for u in range(j + 1):
            at = slice(8 * (j - u), 8 * (j - u) + 8)
            for v in range(8):
                k_r = kern_ref[8 * u + v : 8 * u + v + 1]
                k_i = kern_ref[ROWS + 8 * u + v : ROWS + 8 * u + v + 1]
                e_r, e_i = shift_ref[0, v, at], shift_ref[1, v, at]
                r, i = times(k_r, k_i, e_r, e_i)
                acc_r, acc_i = (r, i) if acc_r is None else (acc_r + r, acc_i + i)
        polar_ref[8 * j : 8 * j + 8] = acc_r
        polar_ref[ROWS + 8 * j : ROWS + 8 * j + 8] = acc_i


def entered_response(coupling, states_r, states_i, polar_ref, fwd_ref, small_ref, send_ref):
    weight = jnp.concatenate([coupling] * PHASES, 0)
    d_r, d_i = times(small_ref[AV + 1 : AV + 2], small_ref[AV + 9 : AV + 10], states_r, states_i)
    table = halves(fwd_ref[...])
    by_r = nt3(table, halves(weight * d_r))
    by_i = nt3(table, halves(weight * d_i))
    real = polar_ref[:ROWS] + (by_r[:ROWS] - by_i[ROWS:])
    imag = polar_ref[ROWS:] + (by_r[ROWS:] + by_i[:ROWS])
    for c, value in enumerate((real, imag)):
        turned = value.T
        parts = [turned[q * PAD : q * PAD + OWN] for q in range(PHASES)]
        send_ref[c * OWN : (c + 1) * OWN] = jnp.concatenate(parts, 1)


def first_kernel(
    params_ref, rows_ref, other_ref, p1, p2, p3,
    fwd_ref, rev_ref, small_ref, send_ref, states_ref, kern_ref, polar_ref, shift_ref,
):
    make_tables(params_ref, fwd_ref, rev_ref, small_ref)
    shifts(rows_ref, shift_ref)
    coupling = coupling_of(params_ref, small_ref)
    inside_response(coupling, shift_ref, fwd_ref, kern_ref, polar_ref)
    rev = halves(rev_ref[...])
    odd = (lax.axis_index("tm") % 2) == 1
    s = None
    for pair in (p3, p2, p1):
        mine, other = pair[: 2 * ROWS], pair[2 * ROWS :]
        for rows in (jnp.where(odd, other, mine), jnp.where(odd, mine, other)):
            _, s = run_edges(s, against(rows[:ROWS], rows[ROWS:], rev), small_ref)
    _, later = run_edges(s, against(other_ref[:ROWS], other_ref[ROWS:], rev), small_ref)
    s = jnp.where(odd, later[0], s[0]), jnp.where(odd, later[1], s[1])
    states, _ = run_edges(s, against(rows_ref[:ROWS], rows_ref[ROWS:], rev), small_ref)
    states_r, states_i = stacked(states)
    states_ref[:LANES] = states_r
    states_ref[LANES:] = states_i
    entered_response(coupling, states_r, states_i, polar_ref, fwd_ref, small_ref, send_ref)


def stretch_correlation(rows_ref, shift_ref):
    corr_r, corr_i = [], []
    for u in range(8):
        sum_r, sum_i = [], []
        for v in range(8):
            acc_r = acc_i = None
            for j in range(u, 8):
                e_r = rows_ref[8 * j : 8 * j + 8]
                e_i = rows_ref[ROWS + 8 * j : ROWS + 8 * j + 8]
                at = slice(8 * (j - u), 8 * (j - u) + 8)
                r, i = times(e_r, -e_i, shift_ref[0, v, at], shift_ref[1, v, at])
                acc_r, acc_i = (r, i) if acc_r is None else (acc_r + r, acc_i + i)
            sum_r.append(jnp.sum(acc_r, axis=0, keepdims=True))
            sum_i.append(jnp.sum(acc_i, axis=0, keepdims=True))
        corr_r += sum_r
        corr_i += sum_i
    return jnp.concatenate(corr_r + [-value for value in corr_i], 0)


def inside_overlap(corr, fwd_ref):
    z = mm3(halves(corr.T), halves(fwd_ref[...]))
    return functools.reduce(lambda a, b: a + b, [z[q * PAD : (q + 1) * PAD] for q in range(PHASES)])


def entry_overlap(rows_ref, fwd_ref):
    return against(rows_ref[:ROWS], -rows_ref[ROWS:], halves(fwd_ref[...]))


def met_of(inside, z_r, z_i, states_r, states_i, small_ref):
    r, i = times(states_r, states_i, z_r, z_i)
    sum_r, sum_i = inside, jnp.zeros((PAD, TOTAL_GROUPS), F32)
    one_r, one_i = small_ref[AV + 1 : AV + 2], small_ref[AV + 9 : AV + 10]
    for q in range(PHASES):
        part = slice(q * PAD, (q + 1) * PAD)
        sum_r = sum_r + (one_r * r[part] - one_i * i[part])
    return sum_r * small_ref[MISC + 5 : MISC + 6]


def correlation_kernel(rows_ref, corr_ref, shift_ref):
    shifts(rows_ref, shift_ref)
    corr_ref[...] = stretch_correlation(rows_ref, shift_ref)


def first_overlap_kernel(rows_ref, corr_ref, fwd_ref, small_ref, states_ref, met_ref):
    inside = inside_overlap(corr_ref[...], fwd_ref)
    z_r, z_i = entry_overlap(rows_ref, fwd_ref)
    met_ref[...] = met_of(inside, z_r, z_i, states_ref[:LANES], states_ref[LANES:], small_ref)


def unpack(ref):
    return [ref[k * OWN : (k + 1) * OWN] for k in range(ref.shape[0] // OWN)]


def pack(ref, values):
    for k, value in enumerate(values):
        ref[k * OWN : (k + 1) * OWN] = value[:OWN]


def chip_kernel(own_ref, other_ref, states_ref, small_ref, out_ref, entered_ref):
    odd = (lax.axis_index("tm") % 2) == 1
    own, other = unpack(own_ref), unpack(other_ref)
    early = [jnp.where(odd, o, m) for o, m in zip(other, own)]
    late = [jnp.where(odd, m, o) for o, m in zip(other, own)]
    far_r, far_i = small_ref[MISC : MISC + 1], small_ref[MISC + 1 : MISC + 2]
    s_r, s_i = times(far_r, far_i, early[0], early[1])
    f_r, f_i = times(far_r, far_i, late[2], late[3])
    cross = early[0] * late[2] - early[1] * late[3]
    met = early[4] + late[4] + cross * small_ref[MISC + 5 : MISC + 6]
    pack(out_ref, [s_r + late[0], s_i + late[1], f_r + early[2], f_i + early[3], met, early[5] + late[5]])
    fill = jnp.zeros((PAD - OWN, TOTAL_GROUPS), F32)
    r, i = carried(*[jnp.concatenate([jnp.where(odd, v, 0.0), fill], 0) for v in other[:2]], small_ref)
    entered_ref[:LANES] = states_ref[:LANES] + r
    entered_ref[LANES:] = states_ref[LANES:] + i


def carried(s_r, s_i, small_ref):
    return stacked(
        [
            times(small_ref[A64 + q : A64 + q + 1], small_ref[A64 + 8 + q : A64 + 9 + q], s_r, s_i)
            for q in range(PHASES)
        ]
    )


def second_finish_kernel(
    rows_at, params_ref, own_at, below_ref, above_ref, across_ref, states_ref,
    fwd_ref, small_ref, send_ref, kern_ref, polar_ref, shift_ref, chips_ref, rows_ref, sems,
):
    place = lax.axis_index("tm")
    y = place // 2
    rows_copy = pltpu.make_async_copy(rows_at, rows_ref, sems.at[0])
    rows_copy.start()
    own_copy = pltpu.make_async_copy(own_at, chips_ref.at[y], sems.at[1])
    own_copy.start()
    chips_ref[lax.rem(y + 3, NY)] = below_ref[...]
    chips_ref[lax.rem(y + 1, NY)] = above_ref[...]
    chips_ref[lax.rem(y + 2, NY)] = across_ref[...]
    rows_copy.wait()
    shifts(rows_ref, shift_ref)
    own_copy.wait()
    far_r, far_i = small_ref[MISC + 2 : MISC + 3], small_ref[MISC + 3 : MISC + 4]
    scale = small_ref[MISC + 5 : MISC + 6]
    x_r = x_i = s_r = s_i = before = met = jnp.zeros((OWN, TOTAL_GROUPS), F32)
    for k in range(NY):
        e_r, e_i, f_r, f_i, here, first = unpack(chips_ref.at[k])
        s_r = jnp.where(y == k, x_r, s_r)
        s_i = jnp.where(y == k, x_i, s_i)
        before = before + first
        met = met + (here + (x_r * f_r - x_i * f_i) * scale)
        x_r, x_i = times(far_r, far_i, x_r, x_i)
        x_r, x_i = x_r + e_r, x_i + e_i
    send_ref[2 * OWN : 3 * OWN] = before + met
    send_ref[3 * OWN :] = jnp.zeros((PAD - OWN, TOTAL_GROUPS), F32)
    coupling = coupling_of(params_ref, small_ref)
    fill = jnp.zeros((PAD - OWN, TOTAL_GROUPS), F32)
    coupling = coupling * jnp.exp(-SATURATE * jnp.concatenate([before, fill], 0))
    inside_response(coupling, shift_ref, fwd_ref, kern_ref, polar_ref)
    odd = (place % 2) == 1
    later_r, later_i = times(small_ref[MISC : MISC + 1], small_ref[MISC + 1 : MISC + 2], s_r, s_i)
    s_r, s_i = jnp.where(odd, later_r, s_r), jnp.where(odd, later_i, s_i)
    s_r, s_i = jnp.concatenate([s_r, fill], 0), jnp.concatenate([s_i, fill], 0)
    states_r, states_i = carried(s_r, s_i, small_ref)
    states_r = states_r + states_ref[:LANES]
    states_i = states_i + states_ref[LANES:]
    entered_response(coupling, states_r, states_i, polar_ref, fwd_ref, small_ref, send_ref)


class Planes:
    def __init__(self, distances, refs):
        refs = list(refs)
        self.blocks = {d: [refs.pop(0) for _ in range(2 if d == 4 else 1)] for d in distances}

    @staticmethod
    def count(distances):
        return sum(2 if d == 4 else 1 for d in distances)

    def turned(self, distances, whole_ref):
        x = lax.axis_index("group") // NZ
        for n, d in enumerate(distances):
            for r in range(NX):
                at = pl.multiple_of(n * 96 + lax.rem(x - r + NX, NX) * 24, 8)
                block, low = self.blocks[d][0], 24 * r
                if d == 4 and r >= 2:
                    block, low = self.blocks[d][1], 24 * (r - 2)
                whole_ref[pl.ds(at, 24)] = block[low : low + 24]
        return whole_ref[: 96 * len(distances)].T

    @staticmethod
    def rows(distances, table_ref, cols):
        z = lax.axis_index("group") % NZ
        starts = [pl.multiple_of(lax.rem(z + d + NZ, NZ) * 96, 32) for d in distances]
        return jnp.concatenate([table_ref[pl.ds(at, 96), cols] for at in starts], 0)


def next_field_kernel(*refs):
    planes, refs = Planes(RING[7:], refs[:2]), refs[2:]
    field_in, high_ref, low_ref, fwd_ref, rev_ref, small_ref, met_ref = refs[:7]
    field_out, rows_out, states_ref, edge_ref, whole_ref, shift_ref, field_ref, rows_ref, sems = refs[7:]
    turned = halves(planes.turned(RING[7:], whole_ref))
    for c in range(2):
        cols = slice(c * LATERAL, (c + 1) * LATERAL)
        table = [Planes.rows(RING[7:], ref, cols) for ref in (high_ref, low_ref)]
        field_ref[c] = field_in[c] + mm3(turned, table)
    field_copy = pltpu.make_async_copy(field_ref, field_out, sems.at[0])
    field_copy.start()
    own_rows(field_ref[0], field_ref[1], rows_ref)
    rows_copy = pltpu.make_async_copy(rows_ref, rows_out, sems.at[1])
    rows_copy.start()
    z = against(rows_ref[:ROWS], rows_ref[ROWS:], halves(rev_ref[...]))
    states, (s_r, s_i) = run_edges(None, z, small_ref)
    states_r, states_i = stacked(states)
    states_ref[:LANES] = states_r
    states_ref[LANES:] = states_i
    shifts(rows_ref, shift_ref)
    inside = inside_overlap(stretch_correlation(rows_ref, shift_ref), fwd_ref)
    z_r, z_i = entry_overlap(rows_ref, fwd_ref)
    met = met_of(inside, z_r, z_i, states_r, states_i, small_ref)
    f_r = f_i = jnp.zeros((PAD, TOTAL_GROUPS), F32)
    for q in range(PHASES):
        part = slice(q * PAD, (q + 1) * PAD)
        r, i = times(
            small_ref[A64 + q : A64 + q + 1], small_ref[A64 + 8 + q : A64 + 9 + q], z_r[part], z_i[part]
        )
        f_r, f_i = f_r + r, f_i + i
    f_r, f_i = times(small_ref[AV + 1 : AV + 2], small_ref[AV + 9 : AV + 10], f_r, f_i)
    pack(edge_ref, [s_r, s_i, f_r, f_i, met, met_ref[...]])
    field_copy.wait()
    rows_copy.wait()


def spread_kernel(distances, field_at, polar_at, start, *refs):
    count = Planes.count(distances)
    planes, refs = Planes(distances, refs[:count]), list(refs[count:])
    whole_ref = refs.pop()
    field_in = field_tables = polar_in = place_ref = None
    if field_at:
        field_in, field_tables = refs.pop(0), (refs.pop(0), refs.pop(0))
    if polar_at:
        polar_in = None if start else refs.pop(0)
        place_ref = refs.pop(0)
    if field_at:
        out_ref = refs.pop(0)
        turned = halves(planes.turned(field_at, whole_ref))
        for c in range(2):
            cols = slice(c * LATERAL, (c + 1) * LATERAL)
            table = [Planes.rows(field_at, ref, cols) for ref in field_tables]
            out_ref[c] = field_in[c] + mm3(turned, table)
    if polar_at:
        out_ref = refs.pop(0)
        turned = planes.turned(polar_at, whole_ref)
        for c in range(2):
            cols = slice(c * LATERAL, (c + 1) * LATERAL)
            value = exact_pick(turned, Planes.rows(polar_at, place_ref, cols))
            out_ref[c] = value if start else polar_in[c] + value


def met_kernel(*refs):
    planes, (occupied_ref, out_ref, gathered_ref) = Planes(RING, refs[:9]), refs[9:]
    me = lax.axis_index("group")
    x, z = me // NZ, me % NZ
    for d in RING:
        for r in range(NX):
            owner = lax.rem(x - r + NX, NX) * NZ + lax.rem(z + d + NZ, NZ)
            at = pl.multiple_of(owner * PAD, 8)
            block, low = (planes.blocks[d][1], 48) if d == 4 else (planes.blocks[d][0], 96)
            gathered_ref[pl.ds(at, PAD)] = block[low:, LANES * r : LANES * r + LANES]
    mine = flag(iota((PAD, LANES), 1) == iota((PAD, LANES), 0) + PAD * z)
    turned = exact_nt(mine, gathered_ref[...])
    row = iota((TOTAL_GROUPS, LATERAL), 0)
    inner = row % PAD
    col = iota((TOTAL_GROUPS, LATERAL), 1)
    met = exact_pick(turned, flag((inner < OWN) & (col == (row // PAD) * OWN + inner)))
    out_ref[...] = occupied_ref[...] * jnp.exp(-SATURATE * met)


RING = (0, -1, 1, -2, 2, -3, 3, 4)


VMEM = pl.BlockSpec(memory_space=pltpu.VMEM)
ANY = pl.BlockSpec(memory_space=pl.ANY)


def call(kernel, outs, scratch=(), cost=1e9, copied=0, at=None, to=()):
    specs = {"out_specs": [ANY if n in to else VMEM for n in range(len(outs))]}
    if at is not None:
        specs["in_specs"] = [ANY if n in at[1] else VMEM for n in range(at[0])]
    sems = [pltpu.SemaphoreType.DMA((copied,))] if copied else []
    return pl.pallas_call(
        kernel,
        out_shape=[jax.ShapeDtypeStruct(shape, dtype) for shape, dtype in outs],
        scratch_shapes=[pltpu.VMEM(shape, dtype) for shape, dtype in scratch] + sems,
        compiler_params=pltpu.CompilerParams(vmem_limit_bytes=16 * 1024 * 1024),
        cost_estimate=pl.CostEstimate(flops=int(cost), bytes_accessed=1 << 20, transcendentals=0),
        **specs,
    )


def to_group(value, dx, dz):
    pairs = [
        (x * NZ + z, ((x + dx) % NX) * NZ + (z + dz) % NZ) for x in range(NX) for z in range(NZ)
    ]
    return lax.ppermute(value, "group", pairs)


def to_time(value, dy, wrap):
    pairs = [
        (2 * y + c, 2 * ((y + dy) % NY) + c)
        for y in range(NY)
        for c in range(2)
        if wrap or y + dy < NY
    ]
    return lax.ppermute(value, "tm", pairs)


def other_core(value):
    return lax.ppermute(value, "tm", [(i, i ^ 1) for i in range(2 * NY)])


def together(*values):
    return lax.optimization_barrier(values)


def step_on(blocks, d):
    if d == 4:
        return to_group(blocks[-3][0][:48], 0, 1), to_group(blocks[3][0][48:], 0, -1)
    near = (blocks[0][0], blocks[0][0]) if d == 1 else (blocks[1 - d][0], blocks[d - 1][0])
    return to_group(near[0], 0, 1), to_group(near[1], 0, -1)


def listed(blocks, distances):
    return [block for d in distances for block in blocks[d]]


def on_device(field, occupations, dephase, detune_class, dot_count):
    const = lateral_constants()
    natural, gathered = const["natural"], const["gathered"]
    table = ((2 * ROWS, TOTAL_GROUPS), F32)
    rows_shape = ((2 * ROWS, LANES), F32)
    shift_shape = ((2, 8, ROWS, LANES), F32)
    states_shape = ((2 * LANES, TOTAL_GROUPS), F32)
    edge_shape = ((6 * OWN, TOTAL_GROUPS), F32)
    met_shape = ((PAD, TOTAL_GROUPS), F32)
    field_shape = ((2, SPAN, LATERAL), F32)
    whole_shape = ((2 * LATERAL, SPAN), F32)

    def spread(blocks, field_at, polar_at, field_in=None, polar_in=None):
        distances = [d for d in RING if d in field_at or d in polar_at]
        extra = [field_in, *gathered] if field_at else []
        if polar_at:
            extra += ([] if polar_in is None else [polar_in]) + [const["place"]]
        outs = [field_shape] * (bool(field_at) + bool(polar_at))
        kernel = functools.partial(spread_kernel, distances, field_at, polar_at, polar_in is None)
        return call(kernel, outs, [whole_shape], 3e9)(*listed(blocks, distances), *extra)

    (pieces,) = call(pieces_kernel, [((NX * NZ, PAD * occupations.shape[0]), F32)])(
        occupations, dephase, detune_class, dot_count
    )
    params = lax.all_to_all(pieces, "group", 0, 0, tiled=True)
    (rows,) = call(own_field_kernel, [rows_shape])(field)
    other = other_core(rows)
    pair = jnp.concatenate([rows, other], 0)
    p1, p2, p3 = (to_time(pair, k, False) for k in (1, 2, 3))
    (corr,) = call(correlation_kernel, [rows_shape], [shift_shape], 4e9)(rows)
    params, corr = together(params, corr)
    params = params.reshape(NX * NZ, PAD, -1).transpose(1, 0, 2).reshape(PAD, TOTAL_GROUPS)
    fwd, rev, small, send, states = call(
        first_kernel,
        [table, table, ((SMALL, TOTAL_GROUPS), F32), ((2 * OWN, SPAN), F32), states_shape],
        [rows_shape, rows_shape, shift_shape],
        3e9,
    )(params, rows, other, p1, p2, p3)

    near = [to_group(send, k, 0) for k in (1, 2, 3)]
    (met,) = call(first_overlap_kernel, [met_shape])(rows, corr, fwd, small, states)
    send, met, *near = together(send, met, *near)
    blocks = {0: [jnp.concatenate([send] + near, 0)]}
    f, b = step_on(blocks, 1)
    (turned,) = call(turn_kernel, [field_shape], (), 3e9)(field, *natural)
    f, turned = together(f, turned)
    blocks[-1], blocks[1] = [f], [b]
    f, b = step_on(blocks, 2)
    (turned,) = spread(blocks, RING[:3], (), turned)
    f, turned = together(f, turned)
    blocks[-2], blocks[2] = [f], [b]
    f, b = step_on(blocks, 3)
    (turned,) = spread(blocks, RING[3:5], (), turned)
    f, turned = together(f, turned)
    blocks[-3], blocks[3] = [f], [b]
    f, b = step_on(blocks, 4)
    (turned,) = spread(blocks, RING[5:7], (), turned)
    f, turned = together(f, turned)
    blocks[4] = [f, b]
    field, rows, states, edge = call(
        next_field_kernel,
        [field_shape, rows_shape, states_shape, edge_shape],
        [whole_shape, shift_shape, field_shape, rows_shape],
        copied=2,
        to=(0, 1),
    )(*blocks[4], turned, *gathered, fwd, rev, small, met)

    other = other_core(edge)
    chip, states = call(chip_kernel, [edge_shape, states_shape])(edge, other, states, small)
    below, above = to_time(chip, 1, True), to_time(chip, -1, True)
    across = to_time(above, -1, True)
    field, below, above = together(field, below, above)
    (turned,) = call(turn_kernel, [field_shape], (), 3e9)(field, *natural)
    across, turned = together(across, turned)
    (send,) = call(
        second_finish_kernel,
        [((2 * OWN + PAD, SPAN), F32)],
        [rows_shape, rows_shape, shift_shape, ((NY, 6 * OWN, TOTAL_GROUPS), F32), rows_shape],
        copied=2,
        at=(9, (0, 2)),
    )(rows, params, chip, below, above, across, states, fwd, small)

    sent = [send] + [to_group(send, k, 0) for k in (1, 2, 3)]
    x = lax.axis_index("group") // NZ
    mets = [lax.dynamic_slice(g[2 * OWN :], (0, x * LANES), (PAD, LANES)) for g in sent]
    blocks = {0: [jnp.concatenate([g[: 2 * OWN] for g in sent] + [jnp.concatenate(mets, 1)], 0)]}
    f, b = step_on(blocks, 1)
    blocks[-1], blocks[1] = [f], [b]
    f, b = step_on(blocks, 2)
    (polar,) = spread(blocks, (), RING[:3])
    f, polar = together(f, polar)
    blocks[-2], blocks[2] = [f], [b]
    f, b = step_on(blocks, 3)
    (amplified,) = spread(blocks, RING[:5], (), turned)
    f, amplified = together(f, amplified)
    blocks[-3], blocks[3] = [f], [b]
    f, b = step_on(blocks, 4)
    amplified, polar = spread(blocks, RING[5:7], RING[3:7], amplified, polar)
    f, polar, amplified = together(f, polar, amplified)
    blocks[4] = [f, b]
    (occupied,) = call(met_kernel, [((PAD, LATERAL), F32)], [((TOTAL_GROUPS, LANES), F32)])(
        *listed(blocks, RING), occupations
    )
    amplified, polar = spread(blocks, RING[7:], RING[7:], amplified, polar)
    return amplified, polar, occupied


def solution(mesh):
    return jax.shard_map(
        on_device,
        mesh=mesh,
        in_specs=(P(None, "tm", None), P("group", None), P("group"), P("group"), P("group")),
        out_specs=(P(None, "tm", None), P(None, "tm", None), P("group", None)),
        check_vma=False,
    )
```

```python
import functools

import jax
import jax.numpy as jnp
import numpy as np
from jax import lax
from jax.experimental import pallas as pl
from jax.experimental.pallas import tpu as pltpu
from jax.sharding import PartitionSpec as P

NCLASS = 32
POL_GAIN = 0.25
SATURATE = 1.5
DIFF_PHASE = 6.0
ANGLE_UNIT = 0.01

NX, NZ, NY = 4, 8, 4
LATERAL = 384
TOTAL_TIME = 4096
TOTAL_GROUPS = 512
SPAN = 512
OWN = 12
PAD = 16
PHASES = 8
ROWS = 64
LANES = 128

F32 = jnp.float32
BF16 = jnp.bfloat16


def split2_np(value):
    import ml_dtypes

    high = value.astype(np.float32).astype(ml_dtypes.bfloat16)
    low = (value - high.astype(np.float64)).astype(np.float32).astype(ml_dtypes.bfloat16)
    return high, low


@functools.cache
def lateral_constants():
    column = np.arange(LATERAL)
    signed = np.where(column < LATERAL // 2, column, column - LATERAL).astype(np.float64)
    phase = DIFF_PHASE * signed**2 / float((LATERAL // 2) ** 2)
    twist = np.exp(-1j * phase)

    def real_form(multiplier):
        kernel = np.fft.ifft(multiplier)
        full = kernel[(column[None, :] - column[:, None]) % LATERAL]
        return np.block([[full.real, full.imag], [-full.imag, full.real]])

    owner = np.arange(NX * NZ)[:, None, None]
    part = np.arange(2)[None, :, None]
    inner = np.arange(OWN)[None, None, :]
    owner = owner.reshape(NX, NZ).T.reshape(-1, 1, 1)
    order = (part * LATERAL + owner * OWN + inner).reshape(-1)
    once = real_form(twist)
    place = np.zeros((2 * LATERAL, 2 * LATERAL))
    place[np.arange(2 * LATERAL), order] = 1.0
    return {
        "natural": split2_np(once),
        "gathered": split2_np(once[order]),
        "place": split2_np(place)[0],
    }


def halves(value):
    high = value.astype(BF16)
    low = (value - high.astype(F32)).astype(BF16)
    return high, low


def thirds(value):
    high = value.astype(BF16)
    rest = value - high.astype(F32)
    mid = rest.astype(BF16)
    low = (rest - mid.astype(F32)).astype(BF16)
    return high, mid, low


def mm(left, right):
    return jnp.dot(left, right, preferred_element_type=F32)


def mm3(left, right):
    (lh, ll), (rh, rl) = left, right
    return mm(lh, rh) + (mm(lh, rl) + mm(ll, rh))


def exact_pick(value, pick):
    high, mid, low = thirds(value)
    return (mm(high, pick) + mm(mid, pick)) + mm(low, pick)


def nt(left, right):
    return lax.dot_general(left, right, (((1,), (1,)), ((), ())), preferred_element_type=F32)


def nt3(left, right):
    (lh, ll), (rh, rl) = left, right
    return nt(lh, rh) + (nt(lh, rl) + nt(ll, rh))


def exact_nt(pick, value):
    high, mid, low = thirds(value)
    return (nt(pick, high) + nt(pick, mid)) + nt(pick, low)


def exact_place(pick, value):
    high, mid, low = thirds(value)
    return (mm(pick, high) + mm(pick, mid)) + mm(pick, low)


def iota(shape, axis):
    return lax.broadcasted_iota(jnp.int32, shape, axis)


def flag(condition):
    return jnp.where(condition, 1.0, 0.0).astype(BF16)


def own_pick():
    first = lax.axis_index("group") * OWN
    lane = iota((LATERAL, LANES), 1) % PAD
    return flag((iota((LATERAL, LANES), 0) == first + lane) & (lane < OWN))


def lane_phase(rows):
    return iota((rows, LANES), 1) // PAD


def times(ar, ai, br, bi):
    return ar * br - ai * bi, ar * bi + ai * br


AV, A64 = 0, 16
MISC = 32
SMALL = 40
PIECE = 40


def powers(first, step, rate, wave):
    exponent = (iota((8, 1), 0) * step + first).astype(F32)
    magnitude = jnp.exp(-exponent * rate)
    angle = (exponent * wave) * ANGLE_UNIT
    return magnitude * jnp.cos(angle), -magnitude * jnp.sin(angle)


def time_rows(value):
    phase = lane_phase(ROWS)
    out = value[:ROWS]
    for q in range(1, PHASES):
        out = jnp.where(phase == q, value[q * ROWS : (q + 1) * ROWS], out)
    return out


def against(re, im, table):
    left = jnp.concatenate([jnp.concatenate([re, -im], 0), jnp.concatenate([im, re], 0)], 1).T
    out = mm3(halves(left), table)
    return out[:LANES], out[LANES:]


def run_edges(s, z, small_ref):
    step_r, step_i = small_ref[A64 + 1 : A64 + 2], small_ref[A64 + 9 : A64 + 10]
    states = []
    for q in range(PHASES):
        part = slice(q * PAD, (q + 1) * PAD)
        if s is None:
            states.append((jnp.zeros((PAD, TOTAL_GROUPS), F32),) * 2)
            s = z[0][part], z[1][part]
        else:
            states.append(s)
            r, i = times(step_r, step_i, *s)
            s = r + z[0][part], i + z[1][part]
    return states, s


def stacked(states):
    return jnp.concatenate([r for r, _ in states], 0), jnp.concatenate([i for _, i in states], 0)


def own_field_kernel(field_ref, rows_ref):
    pick = own_pick()
    rows_ref[:ROWS] = time_rows(exact_pick(field_ref[0], pick))
    rows_ref[ROWS:] = time_rows(exact_pick(field_ref[1], pick))


def pieces_kernel(occupied_ref, rate_ref, class_ref, count_ref, out_ref):
    groups = occupied_ref.shape[0]
    spread = flag(iota((groups, PAD * groups), 1) % groups == iota((groups, PAD * groups), 0))
    tiled = exact_pick(occupied_ref[...].T, spread)
    column = iota((LATERAL, PAD * groups), 0)
    tiled = jnp.where(column % OWN == iota((LATERAL, PAD * groups), 1) // groups, tiled, 0.0)
    owner = iota((NX * NZ, LATERAL), 0)
    out = exact_place(flag(iota((NX * NZ, LATERAL), 1) // OWN == owner), tiled)
    rates = [rate_ref[...], class_ref[...].astype(F32), count_ref[...].astype(F32)]
    lane = iota((8, PAD * groups), 1) // groups
    for k, value in enumerate(rates):
        row = exact_pick(jnp.broadcast_to(value.reshape(1, groups), (8, groups)), spread)
        out = out + jnp.where(lane == OWN + k, row, 0.0)[:1]
    out_ref[...] = out


def turn_kernel(field_ref, high_ref, low_ref, out_ref):
    real, imag = halves(field_ref[0]), halves(field_ref[1])
    for c in range(2):
        cols = slice(c * LATERAL, (c + 1) * LATERAL)
        out_ref[c] = mm3(real, (high_ref[:LATERAL, cols], low_ref[:LATERAL, cols])) + mm3(
            imag, (high_ref[LATERAL:, cols], low_ref[LATERAL:, cols])
        )


def make_tables(params_ref, fwd_ref, rev_ref, small_ref):
    rate = params_ref[12:13]
    wave = 2.0 * params_ref[13:14] - (NCLASS - 1)
    count = params_ref[14:15]
    av_r, av_i = powers(0, 1, rate, wave)
    back_r, back_i = powers(7, -1, rate, wave)
    a8_r, a8_i = powers(0, 8, rate, wave)
    a64_r, a64_i = powers(0, 64, rate, wave)
    far_r, far_i = powers(0, SPAN, rate, wave)
    for u in range(8):
        top = slice(8 * u, 8 * u + 8)
        bottom = slice(ROWS + 8 * u, ROWS + 8 * u + 8)
        fwd_ref[top], fwd_ref[bottom] = times(a8_r[u : u + 1], a8_i[u : u + 1], av_r, av_i)
        rev_ref[top], rev_ref[bottom] = times(
            a8_r[7 - u : 8 - u], a8_i[7 - u : 8 - u], back_r, back_i
        )
    small_ref[AV : AV + 8] = av_r
    small_ref[AV + 8 : AV + 16] = av_i
    small_ref[A64 : A64 + 8] = a64_r
    small_ref[A64 + 8 : A64 + 16] = a64_i
    drive = jnp.sqrt((1.0 - av_r[1:2]) ** 2 + av_i[1:2] ** 2)
    small_ref[MISC : MISC + 1] = far_r[1:2]
    small_ref[MISC + 1 : MISC + 2] = far_i[1:2]
    small_ref[MISC + 2 : MISC + 3] = far_r[2:3]
    small_ref[MISC + 3 : MISC + 4] = far_i[2:3]
    small_ref[MISC + 4 : MISC + 5] = POL_GAIN / TOTAL_GROUPS * count * drive
    small_ref[MISC + 5 : MISC + 6] = drive / TOTAL_TIME
    small_ref[MISC + 6 : MISC + 8] = jnp.zeros((2, TOTAL_GROUPS), F32)


def coupling_of(params_ref, small_ref):
    occupied = jnp.concatenate([params_ref[:OWN], jnp.zeros((PAD - OWN, TOTAL_GROUPS), F32)], 0)
    return small_ref[MISC + 4 : MISC + 5] * occupied


def shifts(rows_ref, shift_ref):
    row = iota((ROWS, LANES), 0)
    for c in range(2):
        value = rows_ref[c * ROWS : (c + 1) * ROWS]
        shift_ref[c, 0] = value
        for v in range(1, 8):
            shift_ref[c, v] = jnp.where(row >= v, pltpu.roll(value, v, 0), 0.0)


def inside_response(coupling, shift_ref, fwd_ref, kern_ref, polar_ref):
    weight = jnp.concatenate([coupling] * PHASES, 0)
    kern_ref[...] = nt3(halves(fwd_ref[...]), halves(weight))
    for j in range(8):
        acc_r = acc_i = None
        for u in range(j + 1):
            at = slice(8 * (j - u), 8 * (j - u) + 8)
            for v in range(8):
                k_r = kern_ref[8 * u + v : 8 * u + v + 1]
                k_i = kern_ref[ROWS + 8 * u + v : ROWS + 8 * u + v + 1]
                e_r, e_i = shift_ref[0, v, at], shift_ref[1, v, at]
                r, i = times(k_r, k_i, e_r, e_i)
                acc_r, acc_i = (r, i) if acc_r is None else (acc_r + r, acc_i + i)
        polar_ref[8 * j : 8 * j + 8] = acc_r
        polar_ref[ROWS + 8 * j : ROWS + 8 * j + 8] = acc_i


def entered_response(coupling, states_r, states_i, polar_ref, fwd_ref, small_ref, send_ref):
    weight = jnp.concatenate([coupling] * PHASES, 0)
    d_r, d_i = times(small_ref[AV + 1 : AV + 2], small_ref[AV + 9 : AV + 10], states_r, states_i)
    table = halves(fwd_ref[...])
    by_r = nt3(table, halves(weight * d_r))
    by_i = nt3(table, halves(weight * d_i))
    real = polar_ref[:ROWS] + (by_r[:ROWS] - by_i[ROWS:])
    imag = polar_ref[ROWS:] + (by_r[ROWS:] + by_i[:ROWS])
    for c, value in enumerate((real, imag)):
        turned = value.T
        parts = [turned[q * PAD : q * PAD + OWN] for q in range(PHASES)]
        send_ref[c * OWN : (c + 1) * OWN] = jnp.concatenate(parts, 1)


def by_chip(chips_ref, near_ref, swapped_ref):
    place = lax.axis_index("tm")
    y, odd = place // 2, place % 2
    chips_ref[lax.rem(y + 3 - 2 * odd, NY)] = near_ref[...]
    chips_ref[lax.rem(y + 1 + 2 * odd, NY)] = swapped_ref[...]


def first_kernel(
    params_ref, rows_ref, own_ref, near_ref, far_ref, swapped_ref,
    fwd_ref, rev_ref, small_ref, send_ref, states_ref, kern_ref, polar_ref, shift_ref, chips_ref,
):
    make_tables(params_ref, fwd_ref, rev_ref, small_ref)
    shifts(rows_ref, shift_ref)
    coupling = coupling_of(params_ref, small_ref)
    inside_response(coupling, shift_ref, fwd_ref, kern_ref, polar_ref)
    rev = halves(rev_ref[...])
    place = lax.axis_index("tm")
    by_chip(chips_ref, near_ref, swapped_ref)
    chips_ref[lax.rem(place // 2 + 2, NY)] = far_ref[...]
    chips_ref[place // 2] = own_ref[...]
    zero = jnp.zeros((PAD, TOTAL_GROUPS), F32)
    s = zero, zero
    for span in range(2 * NY):
        start = 2 * ROWS * (span % 2)
        rows = chips_ref[span // 2, start : start + 2 * ROWS]
        _, later = run_edges(s, against(rows[:ROWS], rows[ROWS:], rev), small_ref)
        before = span < lax.axis_index("tm")
        s = jnp.where(before, later[0], s[0]), jnp.where(before, later[1], s[1])
    states, _ = run_edges(s, against(rows_ref[:ROWS], rows_ref[ROWS:], rev), small_ref)
    states_r, states_i = stacked(states)
    states_ref[:LANES] = states_r
    states_ref[LANES:] = states_i
    entered_response(coupling, states_r, states_i, polar_ref, fwd_ref, small_ref, send_ref)


def stretch_correlation(rows_ref, shift_ref):
    corr_r, corr_i = [], []
    for u in range(8):
        sum_r, sum_i = [], []
        for v in range(8):
            acc_r = acc_i = None
            for j in range(u, 8):
                e_r = rows_ref[8 * j : 8 * j + 8]
                e_i = rows_ref[ROWS + 8 * j : ROWS + 8 * j + 8]
                at = slice(8 * (j - u), 8 * (j - u) + 8)
                r, i = times(e_r, -e_i, shift_ref[0, v, at], shift_ref[1, v, at])
                acc_r, acc_i = (r, i) if acc_r is None else (acc_r + r, acc_i + i)
            sum_r.append(jnp.sum(acc_r, axis=0, keepdims=True))
            sum_i.append(jnp.sum(acc_i, axis=0, keepdims=True))
        corr_r += sum_r
        corr_i += sum_i
    return jnp.concatenate(corr_r + [-value for value in corr_i], 0)


def inside_overlap(corr, fwd_ref):
    z = mm3(halves(corr.T), halves(fwd_ref[...]))
    return functools.reduce(lambda a, b: a + b, [z[q * PAD : (q + 1) * PAD] for q in range(PHASES)])


def entry_overlap(rows_ref, fwd_ref):
    return against(rows_ref[:ROWS], -rows_ref[ROWS:], halves(fwd_ref[...]))


def met_of(inside, z_r, z_i, states_r, states_i, small_ref):
    r, i = times(states_r, states_i, z_r, z_i)
    sum_r, sum_i = inside, jnp.zeros((PAD, TOTAL_GROUPS), F32)
    one_r, one_i = small_ref[AV + 1 : AV + 2], small_ref[AV + 9 : AV + 10]
    for q in range(PHASES):
        part = slice(q * PAD, (q + 1) * PAD)
        sum_r = sum_r + (one_r * r[part] - one_i * i[part])
    return sum_r * small_ref[MISC + 5 : MISC + 6]


def correlation_kernel(rows_ref, corr_ref, shift_ref):
    shifts(rows_ref, shift_ref)
    corr_ref[...] = stretch_correlation(rows_ref, shift_ref)


def first_overlap_kernel(rows_ref, corr_ref, fwd_ref, small_ref, states_ref, met_ref):
    inside = inside_overlap(corr_ref[...], fwd_ref)
    z_r, z_i = entry_overlap(rows_ref, fwd_ref)
    met_ref[...] = met_of(inside, z_r, z_i, states_ref[:LANES], states_ref[LANES:], small_ref)


def unpack(ref):
    return [ref[k * OWN : (k + 1) * OWN] for k in range(ref.shape[0] // OWN)]


def pack(ref, values):
    for k, value in enumerate(values):
        ref[k * OWN : (k + 1) * OWN] = value[:OWN]


def chip_kernel(own_ref, other_ref, states_ref, small_ref, out_ref, piece_ref, entered_ref):
    odd = (lax.axis_index("tm") % 2) == 1
    own, other = unpack(own_ref), unpack(other_ref)
    early = [jnp.where(odd, o, m) for o, m in zip(other, own)]
    late = [jnp.where(odd, m, o) for o, m in zip(other, own)]
    far_r, far_i = small_ref[MISC : MISC + 1], small_ref[MISC + 1 : MISC + 2]
    s_r, s_i = times(far_r, far_i, early[0], early[1])
    f_r, f_i = times(far_r, far_i, late[2], late[3])
    cross = early[0] * late[2] - early[1] * late[3]
    met = early[4] + late[4] + cross * small_ref[MISC + 5 : MISC + 6]
    pack(out_ref, [s_r + late[0], s_i + late[1], f_r + early[2], f_i + early[3], met, early[5] + late[5]])
    piece_ref[...] = jnp.where(odd, out_ref[6 * OWN - PIECE :], out_ref[:PIECE])
    fill = jnp.zeros((PAD - OWN, TOTAL_GROUPS), F32)
    r, i = carried(*[jnp.concatenate([jnp.where(odd, v, 0.0), fill], 0) for v in other[:2]], small_ref)
    entered_ref[:LANES] = states_ref[:LANES] + r
    entered_ref[LANES:] = states_ref[LANES:] + i


def carried(s_r, s_i, small_ref):
    return stacked(
        [
            times(small_ref[A64 + q : A64 + q + 1], small_ref[A64 + 8 + q : A64 + 9 + q], s_r, s_i)
            for q in range(PHASES)
        ]
    )


def second_finish_kernel(
    rows_at, params_ref, own_at, near_ref, swapped_ref, piece_ref, other_piece_ref, states_ref,
    fwd_ref, small_ref, send_ref, kern_ref, polar_ref, shift_ref, chips_ref, rows_ref, sems,
):
    place = lax.axis_index("tm")
    y = place // 2
    rows_copy = pltpu.make_async_copy(rows_at, rows_ref, sems.at[0])
    rows_copy.start()
    own_copy = pltpu.make_async_copy(own_at, chips_ref.at[y], sems.at[1])
    own_copy.start()
    odd = (place % 2) == 1
    by_chip(chips_ref, near_ref, swapped_ref)
    across = lax.rem(y + 2, NY)
    chips_ref[across, :PIECE] = jnp.where(odd, other_piece_ref[...], piece_ref[...])
    chips_ref[across, 6 * OWN - PIECE :] = jnp.where(odd, piece_ref[...], other_piece_ref[...])
    rows_copy.wait()
    shifts(rows_ref, shift_ref)
    own_copy.wait()
    far_r, far_i = small_ref[MISC + 2 : MISC + 3], small_ref[MISC + 3 : MISC + 4]
    scale = small_ref[MISC + 5 : MISC + 6]
    x_r = x_i = s_r = s_i = before = met = jnp.zeros((OWN, TOTAL_GROUPS), F32)
    for k in range(NY):
        e_r, e_i, f_r, f_i, here, first = unpack(chips_ref.at[k])
        s_r = jnp.where(y == k, x_r, s_r)
        s_i = jnp.where(y == k, x_i, s_i)
        before = before + first
        met = met + (here + (x_r * f_r - x_i * f_i) * scale)
        x_r, x_i = times(far_r, far_i, x_r, x_i)
        x_r, x_i = x_r + e_r, x_i + e_i
    send_ref[2 * OWN : 3 * OWN] = before + met
    send_ref[3 * OWN :] = jnp.zeros((PAD - OWN, TOTAL_GROUPS), F32)
    coupling = coupling_of(params_ref, small_ref)
    fill = jnp.zeros((PAD - OWN, TOTAL_GROUPS), F32)
    coupling = coupling * jnp.exp(-SATURATE * jnp.concatenate([before, fill], 0))
    inside_response(coupling, shift_ref, fwd_ref, kern_ref, polar_ref)
    later_r, later_i = times(small_ref[MISC : MISC + 1], small_ref[MISC + 1 : MISC + 2], s_r, s_i)
    s_r, s_i = jnp.where(odd, later_r, s_r), jnp.where(odd, later_i, s_i)
    s_r, s_i = jnp.concatenate([s_r, fill], 0), jnp.concatenate([s_i, fill], 0)
    states_r, states_i = carried(s_r, s_i, small_ref)
    states_r = states_r + states_ref[:LANES]
    states_i = states_i + states_ref[LANES:]
    entered_response(coupling, states_r, states_i, polar_ref, fwd_ref, small_ref, send_ref)


class Planes:
    def __init__(self, distances, refs):
        refs = list(refs)
        self.blocks = {d: [refs.pop(0) for _ in range(2 if d == 4 else 1)] for d in distances}

    @staticmethod
    def count(distances):
        return sum(2 if d == 4 else 1 for d in distances)

    def turned(self, distances, whole_ref):
        x = lax.axis_index("group") // NZ
        for n, d in enumerate(distances):
            for r in range(NX):
                at = pl.multiple_of(n * 96 + lax.rem(x - r + NX, NX) * 24, 8)
                block, low = self.blocks[d][0], 24 * r
                if d == 4 and r >= 2:
                    block, low = self.blocks[d][1], 24 * (r - 2)
                whole_ref[pl.ds(at, 24)] = block[low : low + 24]
        return whole_ref[: 96 * len(distances)].T

    @staticmethod
    def rows(distances, table_ref, cols):
        z = lax.axis_index("group") % NZ
        starts = [pl.multiple_of(lax.rem(z + d + NZ, NZ) * 96, 32) for d in distances]
        return jnp.concatenate([table_ref[pl.ds(at, 96), cols] for at in starts], 0)


def next_field_kernel(*refs):
    planes, refs = Planes(RING[7:], refs[:2]), refs[2:]
    field_in, high_ref, low_ref, fwd_ref, rev_ref, small_ref, met_ref = refs[:7]
    rows_out, states_ref, edge_ref, whole_ref, shift_ref, rows_ref, sems = refs[7:]
    pick = own_pick()
    turned = halves(planes.turned(RING[7:], whole_ref))
    for c in range(2):
        cols = slice(c * LATERAL, (c + 1) * LATERAL)
        table = [mm(Planes.rows(RING[7:], ref, cols), pick).astype(BF16) for ref in (high_ref, low_ref)]
        value = exact_pick(field_in[c], pick) + mm3(turned, table)
        rows_ref[c * ROWS : (c + 1) * ROWS] = time_rows(value)
    rows_copy = pltpu.make_async_copy(rows_ref, rows_out, sems.at[0])
    rows_copy.start()
    z = against(rows_ref[:ROWS], rows_ref[ROWS:], halves(rev_ref[...]))
    states, (s_r, s_i) = run_edges(None, z, small_ref)
    states_r, states_i = stacked(states)
    states_ref[:LANES] = states_r
    states_ref[LANES:] = states_i
    shifts(rows_ref, shift_ref)
    inside = inside_overlap(stretch_correlation(rows_ref, shift_ref), fwd_ref)
    z_r, z_i = entry_overlap(rows_ref, fwd_ref)
    met = met_of(inside, z_r, z_i, states_r, states_i, small_ref)
    f_r = f_i = jnp.zeros((PAD, TOTAL_GROUPS), F32)
    for q in range(PHASES):
        part = slice(q * PAD, (q + 1) * PAD)
        r, i = times(
            small_ref[A64 + q : A64 + q + 1], small_ref[A64 + 8 + q : A64 + 9 + q], z_r[part], z_i[part]
        )
        f_r, f_i = f_r + r, f_i + i
    f_r, f_i = times(small_ref[AV + 1 : AV + 2], small_ref[AV + 9 : AV + 10], f_r, f_i)
    pack(edge_ref, [s_r, s_i, f_r, f_i, met, met_ref[...]])
    rows_copy.wait()


def spread_kernel(distances, field_at, polar_at, start, *refs):
    count = Planes.count(distances)
    planes, refs = Planes(distances, refs[:count]), list(refs[count:])
    whole_ref = refs.pop()
    field_in = field_tables = polar_in = place_ref = None
    if field_at:
        field_in, field_tables = refs.pop(0), (refs.pop(0), refs.pop(0))
    if polar_at:
        polar_in = None if start else refs.pop(0)
        place_ref = refs.pop(0)
    if field_at:
        out_ref = refs.pop(0)
        turned = halves(planes.turned(field_at, whole_ref))
        for c in range(2):
            cols = slice(c * LATERAL, (c + 1) * LATERAL)
            table = [Planes.rows(field_at, ref, cols) for ref in field_tables]
            out_ref[c] = field_in[c] + mm3(turned, table)
    if polar_at:
        out_ref = refs.pop(0)
        turned = planes.turned(polar_at, whole_ref)
        for c in range(2):
            cols = slice(c * LATERAL, (c + 1) * LATERAL)
            value = exact_pick(turned, Planes.rows(polar_at, place_ref, cols))
            out_ref[c] = value if start else polar_in[c] + value


def last_kernel(*refs):
    planes, refs = Planes(RING, refs[:9]), refs[9:]
    field_in, high_ref, low_ref, polar_in, place_ref, occupied_ref = refs[:6]
    field_out, polar_out, occupied_out, whole_ref, field_ref, polar_ref, gathered_ref, sems = refs[6:]
    turned = planes.turned(RING[7:], whole_ref)
    pair = halves(turned)
    copies = []
    for c in range(2):
        cols = slice(c * LATERAL, (c + 1) * LATERAL)
        table = [Planes.rows(RING[7:], ref, cols) for ref in (high_ref, low_ref)]
        field_ref[c] = field_in[c] + mm3(pair, table)
        copies.append(pltpu.make_async_copy(field_ref.at[c], field_out.at[c], sems.at[c]))
        copies[-1].start()
    for c in range(2):
        cols = slice(c * LATERAL, (c + 1) * LATERAL)
        polar_ref[c] = polar_in[c] + exact_pick(turned, Planes.rows(RING[7:], place_ref, cols))
        copies.append(pltpu.make_async_copy(polar_ref.at[c], polar_out.at[c], sems.at[2 + c]))
        copies[-1].start()
    occupied_out[...] = occupied_ref[...] * jnp.exp(-SATURATE * gathered_met(planes, gathered_ref))
    for copy in copies:
        copy.wait()


def gathered_met(planes, gathered_ref):
    me = lax.axis_index("group")
    x, z = me // NZ, me % NZ
    for d in RING:
        for r in range(NX):
            owner = lax.rem(x - r + NX, NX) * NZ + lax.rem(z + d + NZ, NZ)
            at = pl.multiple_of(owner * PAD, 8)
            block, low = (planes.blocks[d][1], 48) if d == 4 else (planes.blocks[d][0], 96)
            gathered_ref[pl.ds(at, PAD)] = block[low:, LANES * r : LANES * r + LANES]
    mine = flag(iota((PAD, LANES), 1) == iota((PAD, LANES), 0) + PAD * z)
    turned = exact_nt(mine, gathered_ref[...])
    row = iota((TOTAL_GROUPS, LATERAL), 0)
    inner = row % PAD
    col = iota((TOTAL_GROUPS, LATERAL), 1)
    return exact_pick(turned, flag((inner < OWN) & (col == (row // PAD) * OWN + inner)))


RING = (0, -1, 1, -2, 2, -3, 3, 4)


VMEM = pl.BlockSpec(memory_space=pltpu.VMEM)
ANY = pl.BlockSpec(memory_space=pl.ANY)


def call(kernel, outs, scratch=(), cost=1e9, copied=0, at=None, to=()):
    specs = {"out_specs": [ANY if n in to else VMEM for n in range(len(outs))]}
    if at is not None:
        specs["in_specs"] = [ANY if n in at[1] else VMEM for n in range(at[0])]
    sems = [pltpu.SemaphoreType.DMA((copied,))] if copied else []
    return pl.pallas_call(
        kernel,
        out_shape=[jax.ShapeDtypeStruct(shape, dtype) for shape, dtype in outs],
        scratch_shapes=[pltpu.VMEM(shape, dtype) for shape, dtype in scratch] + sems,
        compiler_params=pltpu.CompilerParams(vmem_limit_bytes=16 * 1024 * 1024),
        cost_estimate=pl.CostEstimate(flops=int(cost), bytes_accessed=1 << 20, transcendentals=0),
        **specs,
    )


def to_group(value, dx, dz):
    pairs = [
        (x * NZ + z, ((x + dx) % NX) * NZ + (z + dz) % NZ) for x in range(NX) for z in range(NZ)
    ]
    return lax.ppermute(value, "group", pairs)


def across(value):
    return lax.ppermute(value, "tm", [(2 * y + c, 2 * ((y + 2) % NY) + c) for y in range(NY) for c in range(2)])


def to_side(value):
    pairs = [(2 * y + c, 2 * ((y + 1 - 2 * c) % NY) + c) for y in range(NY) for c in range(2)]
    return lax.ppermute(value, "tm", pairs)


def other_core(value):
    return lax.ppermute(value, "tm", [(i, i ^ 1) for i in range(2 * NY)])


def together(*values):
    return lax.optimization_barrier(values)


def step_on(blocks, d):
    if d == 4:
        return to_group(blocks[-3][0][:48], 0, 1), to_group(blocks[3][0][48:], 0, -1)
    near = (blocks[0][0], blocks[0][0]) if d == 1 else (blocks[1 - d][0], blocks[d - 1][0])
    return to_group(near[0], 0, 1), to_group(near[1], 0, -1)


def listed(blocks, distances):
    return [block for d in distances for block in blocks[d]]


def on_device(field, occupations, dephase, detune_class, dot_count):
    const = lateral_constants()
    natural, gathered = const["natural"], const["gathered"]
    table = ((2 * ROWS, TOTAL_GROUPS), F32)
    rows_shape = ((2 * ROWS, LANES), F32)
    shift_shape = ((2, 8, ROWS, LANES), F32)
    states_shape = ((2 * LANES, TOTAL_GROUPS), F32)
    edge_shape = ((6 * OWN, TOTAL_GROUPS), F32)
    met_shape = ((PAD, TOTAL_GROUPS), F32)
    field_shape = ((2, SPAN, LATERAL), F32)
    whole_shape = ((2 * LATERAL, SPAN), F32)

    def spread(blocks, field_at, polar_at, field_in=None, polar_in=None):
        distances = [d for d in RING if d in field_at or d in polar_at]
        extra = [field_in, *gathered] if field_at else []
        if polar_at:
            extra += ([] if polar_in is None else [polar_in]) + [const["place"]]
        outs = [field_shape] * (bool(field_at) + bool(polar_at))
        kernel = functools.partial(spread_kernel, distances, field_at, polar_at, polar_in is None)
        return call(kernel, outs, [whole_shape], 3e9)(*listed(blocks, distances), *extra)

    (pieces,) = call(pieces_kernel, [((NX * NZ, PAD * occupations.shape[0]), F32)])(
        occupations, dephase, detune_class, dot_count
    )
    params = lax.all_to_all(pieces, "group", 0, 0, tiled=True)
    (rows,) = call(own_field_kernel, [rows_shape])(field)
    other = other_core(rows)
    odd = (lax.axis_index("tm") % 2) == 1
    pair = jnp.concatenate([jnp.where(odd, other, rows), jnp.where(odd, rows, other)], 0)
    near = to_side(pair)
    far, swapped = to_side(near), other_core(near)
    (corr,) = call(correlation_kernel, [rows_shape], [shift_shape], 4e9)(rows)
    params, corr = together(params, corr)
    params = params.reshape(NX * NZ, PAD, -1).transpose(1, 0, 2).reshape(PAD, TOTAL_GROUPS)
    fwd, rev, small, send, states = call(
        first_kernel,
        [table, table, ((SMALL, TOTAL_GROUPS), F32), ((2 * OWN, SPAN), F32), states_shape],
        [rows_shape, rows_shape, shift_shape, ((NY, 4 * ROWS, LANES), F32)],
        3e9,
    )(params, rows, pair, near, far, swapped)

    near = [to_group(send, k, 0) for k in (1, 2, 3)]
    (met,) = call(first_overlap_kernel, [met_shape])(rows, corr, fwd, small, states)
    send, met, *near = together(send, met, *near)
    blocks = {0: [jnp.concatenate([send] + near, 0)]}
    f, b = step_on(blocks, 1)
    (turned,) = call(turn_kernel, [field_shape], (), 3e9)(field, *natural)
    b, turned = together(b, turned)
    blocks[-1], blocks[1] = [f], [b]
    f, b = step_on(blocks, 2)
    (turned,) = spread(blocks, RING[:3], (), turned)
    b, turned = together(b, turned)
    blocks[-2], blocks[2] = [f], [b]
    f, b = step_on(blocks, 3)
    (turned,) = spread(blocks, RING[3:5], (), turned)
    b, turned = together(b, turned)
    blocks[-3], blocks[3] = [f], [b]
    f, b = step_on(blocks, 4)
    (turned,) = spread(blocks, RING[5:7], (), turned)
    b, turned = together(b, turned)
    blocks[4] = [f, b]
    rows, states, edge = call(
        next_field_kernel,
        [rows_shape, states_shape, edge_shape],
        [((96, SPAN), F32), shift_shape, rows_shape],
        copied=1,
        to=(0,),
    )(*blocks[4], turned, *gathered, fwd, rev, small, met)

    other = other_core(edge)
    chip, piece, states = call(
        chip_kernel, [edge_shape, ((PIECE, TOTAL_GROUPS), F32), states_shape]
    )(edge, other, states, small)
    near, piece = to_side(chip), across(piece)
    (field,) = spread(blocks, RING[7:], (), turned)
    near, field = together(near, field)
    swapped, other_piece = other_core(near), other_core(piece)
    (send,) = call(
        second_finish_kernel,
        [((2 * OWN + PAD, SPAN), F32)],
        [rows_shape, rows_shape, shift_shape, ((NY, 6 * OWN, TOTAL_GROUPS), F32), rows_shape],
        copied=2,
        at=(10, (0, 2)),
    )(rows, params, chip, near, swapped, piece, other_piece, states, fwd, small)

    sent = [send] + [to_group(send, k, 0) for k in (1, 2, 3)]
    x = lax.axis_index("group") // NZ
    mets = [lax.dynamic_slice(g[2 * OWN :], (0, x * LANES), (PAD, LANES)) for g in sent]
    blocks = {0: [jnp.concatenate([g[: 2 * OWN] for g in sent] + [jnp.concatenate(mets, 1)], 0)]}
    f, b = step_on(blocks, 1)
    (turned,) = call(turn_kernel, [field_shape], (), 3e9)(field, *natural)
    b, turned = together(b, turned)
    blocks[-1], blocks[1] = [f], [b]
    f, b = step_on(blocks, 2)
    (polar,) = spread(blocks, (), RING[:3])
    b, polar = together(b, polar)
    blocks[-2], blocks[2] = [f], [b]
    f, b = step_on(blocks, 3)
    amplified, polar = spread(blocks, RING[:5], RING[3:5], turned, polar)
    b, amplified, polar = together(b, amplified, polar)
    blocks[-3], blocks[3] = [f], [b]
    f, b = step_on(blocks, 4)
    amplified, polar = spread(blocks, RING[5:7], RING[5:7], amplified, polar)
    b, polar, amplified = together(b, polar, amplified)
    blocks[4] = [f, b]
    amplified, polar, occupied = call(
        last_kernel,
        [field_shape, field_shape, ((PAD, LATERAL), F32)],
        [((96, SPAN), F32), field_shape, field_shape, ((TOTAL_GROUPS, LANES), F32)],
        copied=4,
        to=(0, 1),
    )(*listed(blocks, RING), amplified, *gathered, polar, const["place"], occupations)
    return amplified, polar, occupied


def solution(mesh):
    return jax.shard_map(
        on_device,
        mesh=mesh,
        in_specs=(P(None, "tm", None), P("group", None), P("group"), P("group"), P("group")),
        out_specs=(P(None, "tm", None), P(None, "tm", None), P("group", None)),
        check_vma=False,
    )
```

```python
import functools

import jax
import jax.numpy as jnp
import numpy as np
from jax import lax
from jax.experimental import pallas as pl
from jax.experimental.pallas import tpu as pltpu
from jax.sharding import PartitionSpec as P

NCLASS = 32
POL_GAIN = 0.25
SATURATE = 1.5
DIFF_PHASE = 6.0
ANGLE_UNIT = 0.01

NX, NZ, NY = 4, 8, 4
LATERAL = 384
TOTAL_TIME = 4096
TOTAL_GROUPS = 512
SPAN = 512
OWN = 12
PAD = 16
PHASES = 8
ROWS = 64
LANES = 128

F32 = jnp.float32
BF16 = jnp.bfloat16


def split2_np(value):
    import ml_dtypes

    high = value.astype(np.float32).astype(ml_dtypes.bfloat16)
    low = (value - high.astype(np.float64)).astype(np.float32).astype(ml_dtypes.bfloat16)
    return high, low


@functools.cache
def lateral_constants():
    column = np.arange(LATERAL)
    signed = np.where(column < LATERAL // 2, column, column - LATERAL).astype(np.float64)
    phase = DIFF_PHASE * signed**2 / float((LATERAL // 2) ** 2)
    twist = np.exp(-1j * phase)

    def real_form(multiplier):
        kernel = np.fft.ifft(multiplier)
        full = kernel[(column[None, :] - column[:, None]) % LATERAL]
        return np.block([[full.real, full.imag], [-full.imag, full.real]])

    owner = np.arange(NX * NZ)[:, None, None]
    part = np.arange(2)[None, :, None]
    inner = np.arange(OWN)[None, None, :]
    owner = owner.reshape(NX, NZ).T.reshape(-1, 1, 1)
    order = (part * LATERAL + owner * OWN + inner).reshape(-1)
    once = real_form(twist)
    place = np.zeros((2 * LATERAL, 2 * LATERAL))
    place[np.arange(2 * LATERAL), order] = 1.0
    return {
        "natural": split2_np(once),
        "gathered": split2_np(once[order]),
        "place": split2_np(place)[0],
    }


def halves(value):
    high = value.astype(BF16)
    low = (value - high.astype(F32)).astype(BF16)
    return high, low


def thirds(value):
    high = value.astype(BF16)
    rest = value - high.astype(F32)
    mid = rest.astype(BF16)
    low = (rest - mid.astype(F32)).astype(BF16)
    return high, mid, low


def mm(left, right):
    return jnp.dot(left, right, preferred_element_type=F32)


def mm3(left, right):
    (lh, ll), (rh, rl) = left, right
    return mm(lh, rh) + (mm(lh, rl) + mm(ll, rh))


def exact_pick(value, pick):
    high, mid, low = thirds(value)
    return (mm(high, pick) + mm(mid, pick)) + mm(low, pick)


def nt(left, right):
    return lax.dot_general(left, right, (((1,), (1,)), ((), ())), preferred_element_type=F32)


def nt3(left, right):
    (lh, ll), (rh, rl) = left, right
    return nt(lh, rh) + (nt(lh, rl) + nt(ll, rh))


def exact_nt(pick, value):
    high, mid, low = thirds(value)
    return (nt(pick, high) + nt(pick, mid)) + nt(pick, low)


def exact_place(pick, value):
    high, mid, low = thirds(value)
    return (mm(pick, high) + mm(pick, mid)) + mm(pick, low)


def iota(shape, axis):
    return lax.broadcasted_iota(jnp.int32, shape, axis)


def flag(condition):
    return jnp.where(condition, 1.0, 0.0).astype(BF16)


def own_pick():
    first = lax.axis_index("group") * OWN
    lane = iota((LATERAL, LANES), 1) % PAD
    return flag((iota((LATERAL, LANES), 0) == first + lane) & (lane < OWN))


def lane_phase(rows):
    return iota((rows, LANES), 1) // PAD


def times(ar, ai, br, bi):
    return ar * br - ai * bi, ar * bi + ai * br


AV, A64 = 0, 16
MISC = 32
SMALL = 40
PIECE = 40


def powers(first, step, rate, wave):
    exponent = (iota((8, 1), 0) * step + first).astype(F32)
    magnitude = jnp.exp(-exponent * rate)
    angle = (exponent * wave) * ANGLE_UNIT
    return magnitude * jnp.cos(angle), -magnitude * jnp.sin(angle)


def time_rows(value):
    phase = lane_phase(ROWS)
    out = value[:ROWS]
    for q in range(1, PHASES):
        out = jnp.where(phase == q, value[q * ROWS : (q + 1) * ROWS], out)
    return out


def against(re, im, table):
    left = jnp.concatenate([jnp.concatenate([re, -im], 0), jnp.concatenate([im, re], 0)], 1).T
    out = mm3(halves(left), table)
    return out[:LANES], out[LANES:]


def run_edges(s, z, small_ref):
    step_r, step_i = small_ref[A64 + 1 : A64 + 2], small_ref[A64 + 9 : A64 + 10]
    states = []
    for q in range(PHASES):
        part = slice(q * PAD, (q + 1) * PAD)
        if s is None:
            states.append((jnp.zeros((PAD, TOTAL_GROUPS), F32),) * 2)
            s = z[0][part], z[1][part]
        else:
            states.append(s)
            r, i = times(step_r, step_i, *s)
            s = r + z[0][part], i + z[1][part]
    return states, s


def stacked(states):
    return jnp.concatenate([r for r, _ in states], 0), jnp.concatenate([i for _, i in states], 0)


def own_field_kernel(field_ref, rows_ref):
    pick = own_pick()
    rows_ref[:ROWS] = time_rows(exact_pick(field_ref[0], pick))
    rows_ref[ROWS:] = time_rows(exact_pick(field_ref[1], pick))


def pieces_kernel(occupied_ref, rate_ref, class_ref, count_ref, out_ref):
    groups = occupied_ref.shape[0]
    spread = flag(iota((groups, PAD * groups), 1) % groups == iota((groups, PAD * groups), 0))
    tiled = exact_pick(occupied_ref[...].T, spread)
    column = iota((LATERAL, PAD * groups), 0)
    tiled = jnp.where(column % OWN == iota((LATERAL, PAD * groups), 1) // groups, tiled, 0.0)
    owner = iota((NX * NZ, LATERAL), 0)
    out = exact_place(flag(iota((NX * NZ, LATERAL), 1) // OWN == owner), tiled)
    rates = [rate_ref[...], class_ref[...].astype(F32), count_ref[...].astype(F32)]
    lane = iota((8, PAD * groups), 1) // groups
    for k, value in enumerate(rates):
        row = exact_pick(jnp.broadcast_to(value.reshape(1, groups), (8, groups)), spread)
        out = out + jnp.where(lane == OWN + k, row, 0.0)[:1]
    out_ref[...] = out


def turn_kernel(field_ref, high_ref, low_ref, out_ref):
    real, imag = halves(field_ref[0]), halves(field_ref[1])
    for c in range(2):
        cols = slice(c * LATERAL, (c + 1) * LATERAL)
        out_ref[c] = mm3(real, (high_ref[:LATERAL, cols], low_ref[:LATERAL, cols])) + mm3(
            imag, (high_ref[LATERAL:, cols], low_ref[LATERAL:, cols])
        )


def make_tables(params_ref, fwd_ref, rev_ref, small_ref):
    rate = params_ref[12:13]
    wave = 2.0 * params_ref[13:14] - (NCLASS - 1)
    count = params_ref[14:15]
    av_r, av_i = powers(0, 1, rate, wave)
    back_r, back_i = powers(7, -1, rate, wave)
    a8_r, a8_i = powers(0, 8, rate, wave)
    a64_r, a64_i = powers(0, 64, rate, wave)
    far_r, far_i = powers(0, SPAN, rate, wave)
    for u in range(8):
        top = slice(8 * u, 8 * u + 8)
        bottom = slice(ROWS + 8 * u, ROWS + 8 * u + 8)
        fwd_ref[top], fwd_ref[bottom] = times(a8_r[u : u + 1], a8_i[u : u + 1], av_r, av_i)
        rev_ref[top], rev_ref[bottom] = times(
            a8_r[7 - u : 8 - u], a8_i[7 - u : 8 - u], back_r, back_i
        )
    small_ref[AV : AV + 8] = av_r
    small_ref[AV + 8 : AV + 16] = av_i
    small_ref[A64 : A64 + 8] = a64_r
    small_ref[A64 + 8 : A64 + 16] = a64_i
    drive = jnp.sqrt((1.0 - av_r[1:2]) ** 2 + av_i[1:2] ** 2)
    small_ref[MISC : MISC + 1] = far_r[1:2]
    small_ref[MISC + 1 : MISC + 2] = far_i[1:2]
    small_ref[MISC + 2 : MISC + 3] = far_r[2:3]
    small_ref[MISC + 3 : MISC + 4] = far_i[2:3]
    small_ref[MISC + 4 : MISC + 5] = POL_GAIN / TOTAL_GROUPS * count * drive
    small_ref[MISC + 5 : MISC + 6] = drive / TOTAL_TIME
    small_ref[MISC + 6 : MISC + 8] = jnp.zeros((2, TOTAL_GROUPS), F32)


def coupling_of(params_ref, small_ref):
    occupied = jnp.concatenate([params_ref[:OWN], jnp.zeros((PAD - OWN, TOTAL_GROUPS), F32)], 0)
    return small_ref[MISC + 4 : MISC + 5] * occupied


def shifts(rows_ref, shift_ref):
    row = iota((ROWS, LANES), 0)
    for c in range(2):
        value = rows_ref[c * ROWS : (c + 1) * ROWS]
        shift_ref[c, 0] = value
        for v in range(1, 8):
            shift_ref[c, v] = jnp.where(row >= v, pltpu.roll(value, v, 0), 0.0)


def inside_response(coupling, shift_ref, fwd_ref, kern_ref, polar_ref):
    weight = jnp.concatenate([coupling] * PHASES, 0)
    kern_ref[...] = nt3(halves(fwd_ref[...]), halves(weight))
    for j in range(8):
        acc_r = acc_i = None
        for u in range(j + 1):
            at = slice(8 * (j - u), 8 * (j - u) + 8)
            for v in range(8):
                k_r = kern_ref[8 * u + v : 8 * u + v + 1]
                k_i = kern_ref[ROWS + 8 * u + v : ROWS + 8 * u + v + 1]
                e_r, e_i = shift_ref[0, v, at], shift_ref[1, v, at]
                r, i = times(k_r, k_i, e_r, e_i)
                acc_r, acc_i = (r, i) if acc_r is None else (acc_r + r, acc_i + i)
        polar_ref[8 * j : 8 * j + 8] = acc_r
        polar_ref[ROWS + 8 * j : ROWS + 8 * j + 8] = acc_i


def entered_response(coupling, states_r, states_i, polar_ref, fwd_ref, small_ref, send_ref):
    weight = jnp.concatenate([coupling] * PHASES, 0)
    d_r, d_i = times(small_ref[AV + 1 : AV + 2], small_ref[AV + 9 : AV + 10], states_r, states_i)
    table = halves(fwd_ref[...])
    by_r = nt3(table, halves(weight * d_r))
    by_i = nt3(table, halves(weight * d_i))
    real = polar_ref[:ROWS] + (by_r[:ROWS] - by_i[ROWS:])
    imag = polar_ref[ROWS:] + (by_r[ROWS:] + by_i[:ROWS])
    for c, value in enumerate((real, imag)):
        turned = value.T
        parts = [turned[q * PAD : q * PAD + OWN] for q in range(PHASES)]
        send_ref[c * OWN : (c + 1) * OWN] = jnp.concatenate(parts, 1)


def by_chip(chips_ref, near_ref, swapped_ref):
    place = lax.axis_index("tm")
    y, odd = place // 2, place % 2
    chips_ref[lax.rem(y + 3 - 2 * odd, NY)] = near_ref[...]
    chips_ref[lax.rem(y + 1 + 2 * odd, NY)] = swapped_ref[...]


def first_kernel(
    params_ref, rows_ref, own_ref, near_ref, far_ref, swapped_ref,
    fwd_ref, rev_ref, small_ref, send_ref, states_ref, kern_ref, polar_ref, shift_ref, chips_ref,
):
    make_tables(params_ref, fwd_ref, rev_ref, small_ref)
    shifts(rows_ref, shift_ref)
    coupling = coupling_of(params_ref, small_ref)
    inside_response(coupling, shift_ref, fwd_ref, kern_ref, polar_ref)
    rev = halves(rev_ref[...])
    place = lax.axis_index("tm")
    by_chip(chips_ref, near_ref, swapped_ref)
    chips_ref[lax.rem(place // 2 + 2, NY)] = far_ref[...]
    chips_ref[place // 2] = own_ref[...]
    zero = jnp.zeros((PAD, TOTAL_GROUPS), F32)
    s = zero, zero
    for span in range(2 * NY):
        start = 2 * ROWS * (span % 2)
        rows = chips_ref[span // 2, start : start + 2 * ROWS]
        _, later = run_edges(s, against(rows[:ROWS], rows[ROWS:], rev), small_ref)
        before = span < lax.axis_index("tm")
        s = jnp.where(before, later[0], s[0]), jnp.where(before, later[1], s[1])
    states, _ = run_edges(s, against(rows_ref[:ROWS], rows_ref[ROWS:], rev), small_ref)
    states_r, states_i = stacked(states)
    states_ref[:LANES] = states_r
    states_ref[LANES:] = states_i
    entered_response(coupling, states_r, states_i, polar_ref, fwd_ref, small_ref, send_ref)


def stretch_correlation(rows_ref, shift_ref):
    corr_r, corr_i = [], []
    for u in range(8):
        sum_r, sum_i = [], []
        for v in range(8):
            acc_r = acc_i = None
            for j in range(u, 8):
                e_r = rows_ref[8 * j : 8 * j + 8]
                e_i = rows_ref[ROWS + 8 * j : ROWS + 8 * j + 8]
                at = slice(8 * (j - u), 8 * (j - u) + 8)
                r, i = times(e_r, -e_i, shift_ref[0, v, at], shift_ref[1, v, at])
                acc_r, acc_i = (r, i) if acc_r is None else (acc_r + r, acc_i + i)
            sum_r.append(jnp.sum(acc_r, axis=0, keepdims=True))
            sum_i.append(jnp.sum(acc_i, axis=0, keepdims=True))
        corr_r += sum_r
        corr_i += sum_i
    return jnp.concatenate(corr_r + [-value for value in corr_i], 0)


def inside_overlap(corr, fwd_ref):
    z = mm3(halves(corr.T), halves(fwd_ref[...]))
    return functools.reduce(lambda a, b: a + b, [z[q * PAD : (q + 1) * PAD] for q in range(PHASES)])


def entry_overlap(rows_ref, fwd_ref):
    return against(rows_ref[:ROWS], -rows_ref[ROWS:], halves(fwd_ref[...]))


def met_of(inside, z_r, z_i, states_r, states_i, small_ref):
    r, i = times(states_r, states_i, z_r, z_i)
    sum_r, sum_i = inside, jnp.zeros((PAD, TOTAL_GROUPS), F32)
    one_r, one_i = small_ref[AV + 1 : AV + 2], small_ref[AV + 9 : AV + 10]
    for q in range(PHASES):
        part = slice(q * PAD, (q + 1) * PAD)
        sum_r = sum_r + (one_r * r[part] - one_i * i[part])
    return sum_r * small_ref[MISC + 5 : MISC + 6]


def correlation_kernel(rows_ref, corr_ref, shift_ref):
    shifts(rows_ref, shift_ref)
    corr_ref[...] = stretch_correlation(rows_ref, shift_ref)


def first_overlap_kernel(rows_ref, corr_ref, fwd_ref, small_ref, states_ref, met_ref):
    inside = inside_overlap(corr_ref[...], fwd_ref)
    z_r, z_i = entry_overlap(rows_ref, fwd_ref)
    met_ref[...] = met_of(inside, z_r, z_i, states_ref[:LANES], states_ref[LANES:], small_ref)


def unpack(ref):
    return [ref[k * OWN : (k + 1) * OWN] for k in range(ref.shape[0] // OWN)]


def pack(ref, values):
    for k, value in enumerate(values):
        ref[k * OWN : (k + 1) * OWN] = value[:OWN]


def chip_kernel(own_ref, other_ref, states_ref, small_ref, out_ref, piece_ref, entered_ref):
    odd = (lax.axis_index("tm") % 2) == 1
    own, other = unpack(own_ref), unpack(other_ref)
    early = [jnp.where(odd, o, m) for o, m in zip(other, own)]
    late = [jnp.where(odd, m, o) for o, m in zip(other, own)]
    far_r, far_i = small_ref[MISC : MISC + 1], small_ref[MISC + 1 : MISC + 2]
    s_r, s_i = times(far_r, far_i, early[0], early[1])
    f_r, f_i = times(far_r, far_i, late[2], late[3])
    cross = early[0] * late[2] - early[1] * late[3]
    met = early[4] + late[4] + cross * small_ref[MISC + 5 : MISC + 6]
    pack(out_ref, [s_r + late[0], s_i + late[1], f_r + early[2], f_i + early[3], met, early[5] + late[5]])
    piece_ref[...] = jnp.where(odd, out_ref[6 * OWN - PIECE :], out_ref[:PIECE])
    fill = jnp.zeros((PAD - OWN, TOTAL_GROUPS), F32)
    r, i = carried(*[jnp.concatenate([jnp.where(odd, v, 0.0), fill], 0) for v in other[:2]], small_ref)
    entered_ref[:LANES] = states_ref[:LANES] + r
    entered_ref[LANES:] = states_ref[LANES:] + i


def carried(s_r, s_i, small_ref):
    return stacked(
        [
            times(small_ref[A64 + q : A64 + q + 1], small_ref[A64 + 8 + q : A64 + 9 + q], s_r, s_i)
            for q in range(PHASES)
        ]
    )


def second_finish_kernel(
    rows_at, params_ref, own_at, near_ref, swapped_ref, piece_ref, other_piece_ref, states_ref,
    fwd_ref, small_ref, send_ref, kern_ref, polar_ref, shift_ref, chips_ref, rows_ref, sems,
):
    place = lax.axis_index("tm")
    y = place // 2
    rows_copy = pltpu.make_async_copy(rows_at, rows_ref, sems.at[0])
    rows_copy.start()
    own_copy = pltpu.make_async_copy(own_at, chips_ref.at[y], sems.at[1])
    own_copy.start()
    odd = (place % 2) == 1
    by_chip(chips_ref, near_ref, swapped_ref)
    across = lax.rem(y + 2, NY)
    chips_ref[across, :PIECE] = jnp.where(odd, other_piece_ref[...], piece_ref[...])
    chips_ref[across, 6 * OWN - PIECE :] = jnp.where(odd, piece_ref[...], other_piece_ref[...])
    rows_copy.wait()
    shifts(rows_ref, shift_ref)
    own_copy.wait()
    far_r, far_i = small_ref[MISC + 2 : MISC + 3], small_ref[MISC + 3 : MISC + 4]
    scale = small_ref[MISC + 5 : MISC + 6]
    x_r = x_i = s_r = s_i = before = met = jnp.zeros((OWN, TOTAL_GROUPS), F32)
    for k in range(NY):
        e_r, e_i, f_r, f_i, here, first = unpack(chips_ref.at[k])
        s_r = jnp.where(y == k, x_r, s_r)
        s_i = jnp.where(y == k, x_i, s_i)
        before = before + first
        met = met + (here + (x_r * f_r - x_i * f_i) * scale)
        x_r, x_i = times(far_r, far_i, x_r, x_i)
        x_r, x_i = x_r + e_r, x_i + e_i
    send_ref[2 * OWN : 3 * OWN] = before + met
    send_ref[3 * OWN :] = jnp.zeros((PAD - OWN, TOTAL_GROUPS), F32)
    coupling = coupling_of(params_ref, small_ref)
    fill = jnp.zeros((PAD - OWN, TOTAL_GROUPS), F32)
    coupling = coupling * jnp.exp(-SATURATE * jnp.concatenate([before, fill], 0))
    inside_response(coupling, shift_ref, fwd_ref, kern_ref, polar_ref)
    later_r, later_i = times(small_ref[MISC : MISC + 1], small_ref[MISC + 1 : MISC + 2], s_r, s_i)
    s_r, s_i = jnp.where(odd, later_r, s_r), jnp.where(odd, later_i, s_i)
    s_r, s_i = jnp.concatenate([s_r, fill], 0), jnp.concatenate([s_i, fill], 0)
    states_r, states_i = carried(s_r, s_i, small_ref)
    states_r = states_r + states_ref[:LANES]
    states_i = states_i + states_ref[LANES:]
    entered_response(coupling, states_r, states_i, polar_ref, fwd_ref, small_ref, send_ref)


class Planes:
    def __init__(self, distances, refs):
        refs = list(refs)
        self.blocks = {d: [refs.pop(0) for _ in range(2 if d == 4 else 1)] for d in distances}

    @staticmethod
    def count(distances):
        return sum(2 if d == 4 else 1 for d in distances)

    def turned(self, distances, whole_ref):
        x = lax.axis_index("group") // NZ
        for n, d in enumerate(distances):
            for r in range(NX):
                at = pl.multiple_of(n * 96 + lax.rem(x - r + NX, NX) * 24, 8)
                block, low = self.blocks[d][0], 24 * r
                if d == 4 and r >= 2:
                    block, low = self.blocks[d][1], 24 * (r - 2)
                whole_ref[pl.ds(at, 24)] = block[low : low + 24]
        return whole_ref[: 96 * len(distances)].T

    @staticmethod
    def rows(distances, table_ref, cols):
        z = lax.axis_index("group") % NZ
        starts = [pl.multiple_of(lax.rem(z + d + NZ, NZ) * 96, 32) for d in distances]
        return jnp.concatenate([table_ref[pl.ds(at, 96), cols] for at in starts], 0)


def next_field_kernel(*refs):
    planes, refs = Planes(RING[7:], refs[:2]), refs[2:]
    field_in, high_ref, low_ref, fwd_ref, rev_ref, small_ref, met_ref = refs[:7]
    rows_out, states_ref, edge_ref, whole_ref, shift_ref, rows_ref, sems = refs[7:]
    pick = own_pick()
    turned = halves(planes.turned(RING[7:], whole_ref))
    for c in range(2):
        cols = slice(c * LATERAL, (c + 1) * LATERAL)
        table = [mm(Planes.rows(RING[7:], ref, cols), pick).astype(BF16) for ref in (high_ref, low_ref)]
        value = exact_pick(field_in[c], pick) + mm3(turned, table)
        rows_ref[c * ROWS : (c + 1) * ROWS] = time_rows(value)
    rows_copy = pltpu.make_async_copy(rows_ref, rows_out, sems.at[0])
    rows_copy.start()
    z = against(rows_ref[:ROWS], rows_ref[ROWS:], halves(rev_ref[...]))
    states, (s_r, s_i) = run_edges(None, z, small_ref)
    states_r, states_i = stacked(states)
    states_ref[:LANES] = states_r
    states_ref[LANES:] = states_i
    shifts(rows_ref, shift_ref)
    inside = inside_overlap(stretch_correlation(rows_ref, shift_ref), fwd_ref)
    z_r, z_i = entry_overlap(rows_ref, fwd_ref)
    met = met_of(inside, z_r, z_i, states_r, states_i, small_ref)
    f_r = f_i = jnp.zeros((PAD, TOTAL_GROUPS), F32)
    for q in range(PHASES):
        part = slice(q * PAD, (q + 1) * PAD)
        r, i = times(
            small_ref[A64 + q : A64 + q + 1], small_ref[A64 + 8 + q : A64 + 9 + q], z_r[part], z_i[part]
        )
        f_r, f_i = f_r + r, f_i + i
    f_r, f_i = times(small_ref[AV + 1 : AV + 2], small_ref[AV + 9 : AV + 10], f_r, f_i)
    pack(edge_ref, [s_r, s_i, f_r, f_i, met, met_ref[...]])
    rows_copy.wait()


def spread_kernel(distances, field_at, polar_at, start, *refs):
    count = Planes.count(distances)
    planes, refs = Planes(distances, refs[:count]), list(refs[count:])
    whole_ref = refs.pop()
    field_in = field_tables = polar_in = place_ref = None
    if field_at:
        field_in, field_tables = refs.pop(0), (refs.pop(0), refs.pop(0))
    if polar_at:
        polar_in = None if start else refs.pop(0)
        place_ref = refs.pop(0)
    if field_at:
        out_ref = refs.pop(0)
        turned = halves(planes.turned(field_at, whole_ref))
        for c in range(2):
            cols = slice(c * LATERAL, (c + 1) * LATERAL)
            table = [Planes.rows(field_at, ref, cols) for ref in field_tables]
            out_ref[c] = field_in[c] + mm3(turned, table)
    if polar_at:
        out_ref = refs.pop(0)
        turned = planes.turned(polar_at, whole_ref)
        for c in range(2):
            cols = slice(c * LATERAL, (c + 1) * LATERAL)
            value = exact_pick(turned, Planes.rows(polar_at, place_ref, cols))
            out_ref[c] = value if start else polar_in[c] + value


def last_kernel(*refs):
    planes, refs = Planes(RING, refs[:9]), refs[9:]
    field_in, high_ref, low_ref, polar_in, place_ref, occupied_ref = refs[:6]
    field_out, polar_out, occupied_out, whole_ref, field_ref, polar_ref, gathered_ref, sems = refs[6:]
    turned = planes.turned(RING[7:], whole_ref)
    pair = halves(turned)
    copies = []
    for c in range(2):
        cols = slice(c * LATERAL, (c + 1) * LATERAL)
        table = [Planes.rows(RING[7:], ref, cols) for ref in (high_ref, low_ref)]
        field_ref[c] = field_in[c] + mm3(pair, table)
        copies.append(pltpu.make_async_copy(field_ref.at[c], field_out.at[c], sems.at[c]))
        copies[-1].start()
    for c in range(2):
        cols = slice(c * LATERAL, (c + 1) * LATERAL)
        polar_ref[c] = polar_in[c] + exact_pick(turned, Planes.rows(RING[7:], place_ref, cols))
        copies.append(pltpu.make_async_copy(polar_ref.at[c], polar_out.at[c], sems.at[2 + c]))
        copies[-1].start()
    occupied_out[...] = occupied_ref[...] * jnp.exp(-SATURATE * gathered_met(planes, gathered_ref))
    for copy in copies:
        copy.wait()


def gathered_met(planes, gathered_ref):
    me = lax.axis_index("group")
    x, z = me // NZ, me % NZ
    for d in RING:
        for r in range(NX):
            owner = lax.rem(x - r + NX, NX) * NZ + lax.rem(z + d + NZ, NZ)
            at = pl.multiple_of(owner * PAD, 8)
            block, low = (planes.blocks[d][1], 48) if d == 4 else (planes.blocks[d][0], 96)
            gathered_ref[pl.ds(at, PAD)] = block[low:, LANES * r : LANES * r + LANES]
    mine = flag(iota((PAD, LANES), 1) == iota((PAD, LANES), 0) + PAD * z)
    turned = exact_nt(mine, gathered_ref[...])
    row = iota((TOTAL_GROUPS, LATERAL), 0)
    inner = row % PAD
    col = iota((TOTAL_GROUPS, LATERAL), 1)
    return exact_pick(turned, flag((inner < OWN) & (col == (row // PAD) * OWN + inner)))


RING = (0, -1, 1, -2, 2, -3, 3, 4)


VMEM = pl.BlockSpec(memory_space=pltpu.VMEM)
ANY = pl.BlockSpec(memory_space=pl.ANY)


def call(kernel, outs, scratch=(), cost=1e9, copied=0, at=None, to=()):
    specs = {"out_specs": [ANY if n in to else VMEM for n in range(len(outs))]}
    if at is not None:
        specs["in_specs"] = [ANY if n in at[1] else VMEM for n in range(at[0])]
    sems = [pltpu.SemaphoreType.DMA((copied,))] if copied else []
    return pl.pallas_call(
        kernel,
        out_shape=[jax.ShapeDtypeStruct(shape, dtype) for shape, dtype in outs],
        scratch_shapes=[pltpu.VMEM(shape, dtype) for shape, dtype in scratch] + sems,
        compiler_params=pltpu.CompilerParams(vmem_limit_bytes=16 * 1024 * 1024),
        cost_estimate=pl.CostEstimate(flops=int(cost), bytes_accessed=1 << 20, transcendentals=0),
        **specs,
    )


def to_group(value, dx, dz):
    pairs = [
        (x * NZ + z, ((x + dx) % NX) * NZ + (z + dz) % NZ) for x in range(NX) for z in range(NZ)
    ]
    return lax.ppermute(value, "group", pairs)


def across(value):
    return lax.ppermute(value, "tm", [(2 * y + c, 2 * ((y + 2) % NY) + c) for y in range(NY) for c in range(2)])


def to_side(value):
    pairs = [(2 * y + c, 2 * ((y + 1 - 2 * c) % NY) + c) for y in range(NY) for c in range(2)]
    return lax.ppermute(value, "tm", pairs)


def other_core(value):
    return lax.ppermute(value, "tm", [(i, i ^ 1) for i in range(2 * NY)])


def together(*values):
    return lax.optimization_barrier(values)


def step_on(blocks, d):
    if d == 4:
        return to_group(blocks[-3][0][:48], 0, 1), to_group(blocks[3][0][48:], 0, -1)
    near = (blocks[0][0], blocks[0][0]) if d == 1 else (blocks[1 - d][0], blocks[d - 1][0])
    return to_group(near[0], 0, 1), to_group(near[1], 0, -1)


def listed(blocks, distances):
    return [block for d in distances for block in blocks[d]]


def on_device(field, occupations, dephase, detune_class, dot_count):
    const = lateral_constants()
    natural, gathered = const["natural"], const["gathered"]
    table = ((2 * ROWS, TOTAL_GROUPS), F32)
    rows_shape = ((2 * ROWS, LANES), F32)
    shift_shape = ((2, 8, ROWS, LANES), F32)
    states_shape = ((2 * LANES, TOTAL_GROUPS), F32)
    edge_shape = ((6 * OWN, TOTAL_GROUPS), F32)
    met_shape = ((PAD, TOTAL_GROUPS), F32)
    field_shape = ((2, SPAN, LATERAL), F32)
    whole_shape = ((2 * LATERAL, SPAN), F32)

    def spread(blocks, field_at, polar_at, field_in=None, polar_in=None):
        distances = [d for d in RING if d in field_at or d in polar_at]
        extra = [field_in, *gathered] if field_at else []
        if polar_at:
            extra += ([] if polar_in is None else [polar_in]) + [const["place"]]
        outs = [field_shape] * (bool(field_at) + bool(polar_at))
        kernel = functools.partial(spread_kernel, distances, field_at, polar_at, polar_in is None)
        return call(kernel, outs, [whole_shape], 3e9)(*listed(blocks, distances), *extra)

    (pieces,) = call(pieces_kernel, [((NX * NZ, PAD * occupations.shape[0]), F32)])(
        occupations, dephase, detune_class, dot_count
    )
    (rows,) = call(own_field_kernel, [rows_shape])(field)
    other = other_core(rows)
    other, pieces = together(other, pieces)
    params = lax.all_to_all(pieces, "group", 0, 0, tiled=True)
    odd = (lax.axis_index("tm") % 2) == 1
    pair = jnp.concatenate([jnp.where(odd, other, rows), jnp.where(odd, rows, other)], 0)
    near = to_side(pair)
    far, swapped = to_side(near), other_core(near)
    (corr,) = call(correlation_kernel, [rows_shape], [shift_shape], 4e9)(rows)
    params, corr = together(params, corr)
    params = params.reshape(NX * NZ, PAD, -1).transpose(1, 0, 2).reshape(PAD, TOTAL_GROUPS)
    fwd, rev, small, send, states = call(
        first_kernel,
        [table, table, ((SMALL, TOTAL_GROUPS), F32), ((2 * OWN, SPAN), F32), states_shape],
        [rows_shape, rows_shape, shift_shape, ((NY, 4 * ROWS, LANES), F32)],
        3e9,
    )(params, rows, pair, near, far, swapped)

    near = [to_group(send, k, 0) for k in (1, 2, 3)]
    (met,) = call(first_overlap_kernel, [met_shape])(rows, corr, fwd, small, states)
    send, met, *near = together(send, met, *near)
    blocks = {0: [jnp.concatenate([send] + near, 0)]}
    f, b = step_on(blocks, 1)
    (turned,) = call(turn_kernel, [field_shape], (), 3e9)(field, *natural)
    b, turned = together(b, turned)
    blocks[-1], blocks[1] = [f], [b]
    f, b = step_on(blocks, 2)
    (turned,) = spread(blocks, RING[:3], (), turned)
    b, turned = together(b, turned)
    blocks[-2], blocks[2] = [f], [b]
    f, b = step_on(blocks, 3)
    (turned,) = spread(blocks, RING[3:5], (), turned)
    b, turned = together(b, turned)
    blocks[-3], blocks[3] = [f], [b]
    f, b = step_on(blocks, 4)
    (turned,) = spread(blocks, RING[5:7], (), turned)
    b, turned = together(b, turned)
    blocks[4] = [f, b]
    rows, states, edge = call(
        next_field_kernel,
        [rows_shape, states_shape, edge_shape],
        [((96, SPAN), F32), shift_shape, rows_shape],
        copied=1,
        to=(0,),
    )(*blocks[4], turned, *gathered, fwd, rev, small, met)

    other = other_core(edge)
    chip, piece, states = call(
        chip_kernel, [edge_shape, ((PIECE, TOTAL_GROUPS), F32), states_shape]
    )(edge, other, states, small)
    near, piece = to_side(chip), across(piece)
    (field,) = spread(blocks, RING[7:], (), turned)
    near, field = together(near, field)
    swapped, other_piece = other_core(near), other_core(piece)
    (send,) = call(
        second_finish_kernel,
        [((2 * OWN + PAD, SPAN), F32)],
        [rows_shape, rows_shape, shift_shape, ((NY, 6 * OWN, TOTAL_GROUPS), F32), rows_shape],
        copied=2,
        at=(10, (0, 2)),
    )(rows, params, chip, near, swapped, piece, other_piece, states, fwd, small)

    sent = [send] + [to_group(send, k, 0) for k in (1, 2, 3)]
    x = lax.axis_index("group") // NZ
    mets = [lax.dynamic_slice(g[2 * OWN :], (0, x * LANES), (PAD, LANES)) for g in sent]
    blocks = {0: [jnp.concatenate([g[: 2 * OWN] for g in sent] + [jnp.concatenate(mets, 1)], 0)]}
    f, b = step_on(blocks, 1)
    (turned,) = call(turn_kernel, [field_shape], (), 3e9)(field, *natural)
    b, turned = together(b, turned)
    blocks[-1], blocks[1] = [f], [b]
    f, b = step_on(blocks, 2)
    (polar,) = spread(blocks, (), RING[:3])
    b, polar = together(b, polar)
    blocks[-2], blocks[2] = [f], [b]
    f, b = step_on(blocks, 3)
    amplified, polar = spread(blocks, RING[:5], RING[3:5], turned, polar)
    b, amplified, polar = together(b, amplified, polar)
    blocks[-3], blocks[3] = [f], [b]
    f, b = step_on(blocks, 4)
    amplified, polar = spread(blocks, RING[5:7], RING[5:7], amplified, polar)
    b, polar, amplified = together(b, polar, amplified)
    blocks[4] = [f, b]
    amplified, polar, occupied = call(
        last_kernel,
        [field_shape, field_shape, ((PAD, LATERAL), F32)],
        [((96, SPAN), F32), field_shape, field_shape, ((TOTAL_GROUPS, LANES), F32)],
        copied=4,
        to=(0, 1),
    )(*listed(blocks, RING), amplified, *gathered, polar, const["place"], occupations)
    return amplified, polar, occupied


def solution(mesh):
    return jax.shard_map(
        on_device,
        mesh=mesh,
        in_specs=(P(None, "tm", None), P("group", None), P("group"), P("group"), P("group")),
        out_specs=(P(None, "tm", None), P(None, "tm", None), P("group", None)),
        check_vma=False,
    )
```

```python
import functools

import jax
import jax.numpy as jnp
import numpy as np
from jax import lax
from jax.experimental import pallas as pl
from jax.experimental.pallas import tpu as pltpu
from jax.sharding import PartitionSpec as P

NCLASS = 32
POL_GAIN = 0.25
SATURATE = 1.5
DIFF_PHASE = 6.0
ANGLE_UNIT = 0.01

NX, NZ, NY = 4, 8, 4
LATERAL = 384
TOTAL_TIME = 4096
TOTAL_GROUPS = 512
SPAN = 512
OWN = 12
PAD = 16
PHASES = 8
ROWS = 64
LANES = 128

F32 = jnp.float32
BF16 = jnp.bfloat16


def split2_np(value):
    import ml_dtypes

    high = value.astype(np.float32).astype(ml_dtypes.bfloat16)
    low = (value - high.astype(np.float64)).astype(np.float32).astype(ml_dtypes.bfloat16)
    return high, low


@functools.cache
def lateral_constants():
    column = np.arange(LATERAL)
    signed = np.where(column < LATERAL // 2, column, column - LATERAL).astype(np.float64)
    phase = DIFF_PHASE * signed**2 / float((LATERAL // 2) ** 2)
    twist = np.exp(-1j * phase)

    def real_form(multiplier):
        kernel = np.fft.ifft(multiplier)
        full = kernel[(column[None, :] - column[:, None]) % LATERAL]
        return np.block([[full.real, full.imag], [-full.imag, full.real]])

    owner = np.arange(NX * NZ)[:, None, None]
    part = np.arange(2)[None, :, None]
    inner = np.arange(OWN)[None, None, :]
    owner = owner.reshape(NX, NZ).T.reshape(-1, 1, 1)
    order = (part * LATERAL + owner * OWN + inner).reshape(-1)
    once = real_form(twist)
    place = np.zeros((2 * LATERAL, 2 * LATERAL))
    place[np.arange(2 * LATERAL), order] = 1.0
    return {
        "natural": split2_np(once),
        "gathered": split2_np(once[order]),
        "place": split2_np(place)[0],
    }


def halves(value):
    high = value.astype(BF16)
    low = (value - high.astype(F32)).astype(BF16)
    return high, low


def thirds(value):
    high = value.astype(BF16)
    rest = value - high.astype(F32)
    mid = rest.astype(BF16)
    low = (rest - mid.astype(F32)).astype(BF16)
    return high, mid, low


def mm(left, right):
    return jnp.dot(left, right, preferred_element_type=F32)


def mm3(left, right):
    (lh, ll), (rh, rl) = left, right
    return mm(lh, rh) + (mm(lh, rl) + mm(ll, rh))


def exact_pick(value, pick):
    high, mid, low = thirds(value)
    return (mm(high, pick) + mm(mid, pick)) + mm(low, pick)


def nt(left, right):
    return lax.dot_general(left, right, (((1,), (1,)), ((), ())), preferred_element_type=F32)


def nt3(left, right):
    (lh, ll), (rh, rl) = left, right
    return nt(lh, rh) + (nt(lh, rl) + nt(ll, rh))


def exact_nt(pick, value):
    high, mid, low = thirds(value)
    return (nt(pick, high) + nt(pick, mid)) + nt(pick, low)


def exact_place(pick, value):
    high, mid, low = thirds(value)
    return (mm(pick, high) + mm(pick, mid)) + mm(pick, low)


def iota(shape, axis):
    return lax.broadcasted_iota(jnp.int32, shape, axis)


def flag(condition):
    return jnp.where(condition, 1.0, 0.0).astype(BF16)


def own_pick():
    first = lax.axis_index("group") * OWN
    lane = iota((LATERAL, LANES), 1) % PAD
    return flag((iota((LATERAL, LANES), 0) == first + lane) & (lane < OWN))


def lane_phase(rows):
    return iota((rows, LANES), 1) // PAD


def times(ar, ai, br, bi):
    return ar * br - ai * bi, ar * bi + ai * br


AV, A64 = 0, 16
MISC = 32
SMALL = 40
PIECE = 40


def powers(first, step, rate, wave):
    exponent = (iota((8, 1), 0) * step + first).astype(F32)
    magnitude = jnp.exp(-exponent * rate)
    angle = (exponent * wave) * ANGLE_UNIT
    return magnitude * jnp.cos(angle), -magnitude * jnp.sin(angle)


def time_rows(value):
    phase = lane_phase(ROWS)
    out = value[:ROWS]
    for q in range(1, PHASES):
        out = jnp.where(phase == q, value[q * ROWS : (q + 1) * ROWS], out)
    return out


def against(re, im, table):
    left = jnp.concatenate([jnp.concatenate([re, -im], 0), jnp.concatenate([im, re], 0)], 1).T
    out = mm3(halves(left), table)
    return out[:LANES], out[LANES:]


def run_edges(s, z, small_ref):
    step_r, step_i = small_ref[A64 + 1 : A64 + 2], small_ref[A64 + 9 : A64 + 10]
    states = []
    for q in range(PHASES):
        part = slice(q * PAD, (q + 1) * PAD)
        if s is None:
            states.append((jnp.zeros((PAD, TOTAL_GROUPS), F32),) * 2)
            s = z[0][part], z[1][part]
        else:
            states.append(s)
            r, i = times(step_r, step_i, *s)
            s = r + z[0][part], i + z[1][part]
    return states, s


def stacked(states):
    return jnp.concatenate([r for r, _ in states], 0), jnp.concatenate([i for _, i in states], 0)


def own_field_kernel(field_ref, rows_ref):
    pick = own_pick()
    rows_ref[:ROWS] = time_rows(exact_pick(field_ref[0], pick))
    rows_ref[ROWS:] = time_rows(exact_pick(field_ref[1], pick))


def pieces_kernel(occupied_ref, rate_ref, class_ref, count_ref, out_ref):
    groups = occupied_ref.shape[0]
    spread = flag(iota((groups, PAD * groups), 1) % groups == iota((groups, PAD * groups), 0))
    tiled = exact_pick(occupied_ref[...].T, spread)
    column = iota((LATERAL, PAD * groups), 0)
    tiled = jnp.where(column % OWN == iota((LATERAL, PAD * groups), 1) // groups, tiled, 0.0)
    owner = iota((NX * NZ, LATERAL), 0)
    out = exact_place(flag(iota((NX * NZ, LATERAL), 1) // OWN == owner), tiled)
    rates = [rate_ref[...], class_ref[...].astype(F32), count_ref[...].astype(F32)]
    lane = iota((8, PAD * groups), 1) // groups
    for k, value in enumerate(rates):
        row = exact_pick(jnp.broadcast_to(value.reshape(1, groups), (8, groups)), spread)
        out = out + jnp.where(lane == OWN + k, row, 0.0)[:1]
    out_ref[...] = out


def turn_kernel(field_ref, high_ref, low_ref, out_ref):
    real, imag = halves(field_ref[0]), halves(field_ref[1])
    for c in range(2):
        cols = slice(c * LATERAL, (c + 1) * LATERAL)
        out_ref[c] = mm3(real, (high_ref[:LATERAL, cols], low_ref[:LATERAL, cols])) + mm3(
            imag, (high_ref[LATERAL:, cols], low_ref[LATERAL:, cols])
        )


def make_tables(params_ref, fwd_ref, rev_ref, small_ref):
    rate = params_ref[12:13]
    wave = 2.0 * params_ref[13:14] - (NCLASS - 1)
    count = params_ref[14:15]
    av_r, av_i = powers(0, 1, rate, wave)
    back_r, back_i = powers(7, -1, rate, wave)
    a8_r, a8_i = powers(0, 8, rate, wave)
    a64_r, a64_i = powers(0, 64, rate, wave)
    far_r, far_i = powers(0, SPAN, rate, wave)
    for u in range(8):
        top = slice(8 * u, 8 * u + 8)
        bottom = slice(ROWS + 8 * u, ROWS + 8 * u + 8)
        fwd_ref[top], fwd_ref[bottom] = times(a8_r[u : u + 1], a8_i[u : u + 1], av_r, av_i)
        rev_ref[top], rev_ref[bottom] = times(
            a8_r[7 - u : 8 - u], a8_i[7 - u : 8 - u], back_r, back_i
        )
    small_ref[AV : AV + 8] = av_r
    small_ref[AV + 8 : AV + 16] = av_i
    small_ref[A64 : A64 + 8] = a64_r
    small_ref[A64 + 8 : A64 + 16] = a64_i
    drive = jnp.sqrt((1.0 - av_r[1:2]) ** 2 + av_i[1:2] ** 2)
    small_ref[MISC : MISC + 1] = far_r[1:2]
    small_ref[MISC + 1 : MISC + 2] = far_i[1:2]
    small_ref[MISC + 2 : MISC + 3] = far_r[2:3]
    small_ref[MISC + 3 : MISC + 4] = far_i[2:3]
    small_ref[MISC + 4 : MISC + 5] = POL_GAIN / TOTAL_GROUPS * count * drive
    small_ref[MISC + 5 : MISC + 6] = drive / TOTAL_TIME
    small_ref[MISC + 6 : MISC + 8] = jnp.zeros((2, TOTAL_GROUPS), F32)


def coupling_of(params_ref, small_ref):
    occupied = jnp.concatenate([params_ref[:OWN], jnp.zeros((PAD - OWN, TOTAL_GROUPS), F32)], 0)
    return small_ref[MISC + 4 : MISC + 5] * occupied


def shifts(rows_ref, shift_ref):
    row = iota((ROWS, LANES), 0)
    for c in range(2):
        value = rows_ref[c * ROWS : (c + 1) * ROWS]
        shift_ref[c, 0] = value
        for v in range(1, 8):
            shift_ref[c, v] = jnp.where(row >= v, pltpu.roll(value, v, 0), 0.0)


def inside_response(coupling, shift_ref, fwd_ref, kern_ref, polar_ref):
    weight = jnp.concatenate([coupling] * PHASES, 0)
    kern_ref[...] = nt3(halves(fwd_ref[...]), halves(weight))
    for j in range(8):
        acc_r = acc_i = None
        for u in range(j + 1):
            at = slice(8 * (j - u), 8 * (j - u) + 8)
            for v in range(8):
                k_r = kern_ref[8 * u + v : 8 * u + v + 1]
                k_i = kern_ref[ROWS + 8 * u + v : ROWS + 8 * u + v + 1]
                e_r, e_i = shift_ref[0, v, at], shift_ref[1, v, at]
                r, i = times(k_r, k_i, e_r, e_i)
                acc_r, acc_i = (r, i) if acc_r is None else (acc_r + r, acc_i + i)
        polar_ref[8 * j : 8 * j + 8] = acc_r
        polar_ref[ROWS + 8 * j : ROWS + 8 * j + 8] = acc_i


def entered_response(coupling, states_r, states_i, polar_ref, fwd_ref, small_ref, send_ref):
    weight = jnp.concatenate([coupling] * PHASES, 0)
    d_r, d_i = times(small_ref[AV + 1 : AV + 2], small_ref[AV + 9 : AV + 10], states_r, states_i)
    table = halves(fwd_ref[...])
    by_r = nt3(table, halves(weight * d_r))
    by_i = nt3(table, halves(weight * d_i))
    real = polar_ref[:ROWS] + (by_r[:ROWS] - by_i[ROWS:])
    imag = polar_ref[ROWS:] + (by_r[ROWS:] + by_i[:ROWS])
    for c, value in enumerate((real, imag)):
        turned = value.T
        parts = [turned[q * PAD : q * PAD + OWN] for q in range(PHASES)]
        send_ref[c * OWN : (c + 1) * OWN] = jnp.concatenate(parts, 1)


def by_chip(chips_ref, near_ref, swapped_ref):
    place = lax.axis_index("tm")
    y, odd = place // 2, place % 2
    chips_ref[lax.rem(y + 3 - 2 * odd, NY)] = near_ref[...]
    chips_ref[lax.rem(y + 1 + 2 * odd, NY)] = swapped_ref[...]


def first_kernel(
    params_ref, rows_ref, own_ref, near_ref, far_ref, swapped_ref,
    fwd_ref, rev_ref, small_ref, send_ref, states_ref, kern_ref, polar_ref, shift_ref, chips_ref,
):
    make_tables(params_ref, fwd_ref, rev_ref, small_ref)
    shifts(rows_ref, shift_ref)
    coupling = coupling_of(params_ref, small_ref)
    inside_response(coupling, shift_ref, fwd_ref, kern_ref, polar_ref)
    rev = halves(rev_ref[...])
    place = lax.axis_index("tm")
    by_chip(chips_ref, near_ref, swapped_ref)
    chips_ref[lax.rem(place // 2 + 2, NY)] = far_ref[...]
    chips_ref[place // 2] = own_ref[...]
    zero = jnp.zeros((PAD, TOTAL_GROUPS), F32)
    s = zero, zero
    for span in range(2 * NY):
        start = 2 * ROWS * (span % 2)
        rows = chips_ref[span // 2, start : start + 2 * ROWS]
        _, later = run_edges(s, against(rows[:ROWS], rows[ROWS:], rev), small_ref)
        before = span < lax.axis_index("tm")
        s = jnp.where(before, later[0], s[0]), jnp.where(before, later[1], s[1])
    states, _ = run_edges(s, against(rows_ref[:ROWS], rows_ref[ROWS:], rev), small_ref)
    states_r, states_i = stacked(states)
    states_ref[:LANES] = states_r
    states_ref[LANES:] = states_i
    entered_response(coupling, states_r, states_i, polar_ref, fwd_ref, small_ref, send_ref)


def stretch_correlation(rows_ref, shift_ref):
    corr_r, corr_i = [], []
    for u in range(8):
        sum_r, sum_i = [], []
        for v in range(8):
            acc_r = acc_i = None
            for j in range(u, 8):
                e_r = rows_ref[8 * j : 8 * j + 8]
                e_i = rows_ref[ROWS + 8 * j : ROWS + 8 * j + 8]
                at = slice(8 * (j - u), 8 * (j - u) + 8)
                r, i = times(e_r, -e_i, shift_ref[0, v, at], shift_ref[1, v, at])
                acc_r, acc_i = (r, i) if acc_r is None else (acc_r + r, acc_i + i)
            sum_r.append(jnp.sum(acc_r, axis=0, keepdims=True))
            sum_i.append(jnp.sum(acc_i, axis=0, keepdims=True))
        corr_r += sum_r
        corr_i += sum_i
    return jnp.concatenate(corr_r + [-value for value in corr_i], 0)


def inside_overlap(corr, fwd_ref):
    z = mm3(halves(corr.T), halves(fwd_ref[...]))
    return functools.reduce(lambda a, b: a + b, [z[q * PAD : (q + 1) * PAD] for q in range(PHASES)])


def entry_overlap(rows_ref, fwd_ref):
    return against(rows_ref[:ROWS], -rows_ref[ROWS:], halves(fwd_ref[...]))


def met_of(inside, z_r, z_i, states_r, states_i, small_ref):
    r, i = times(states_r, states_i, z_r, z_i)
    sum_r, sum_i = inside, jnp.zeros((PAD, TOTAL_GROUPS), F32)
    one_r, one_i = small_ref[AV + 1 : AV + 2], small_ref[AV + 9 : AV + 10]
    for q in range(PHASES):
        part = slice(q * PAD, (q + 1) * PAD)
        sum_r = sum_r + (one_r * r[part] - one_i * i[part])
    return sum_r * small_ref[MISC + 5 : MISC + 6]


def correlation_kernel(rows_ref, corr_ref, shift_ref):
    shifts(rows_ref, shift_ref)
    corr_ref[...] = stretch_correlation(rows_ref, shift_ref)


def first_overlap_kernel(rows_ref, corr_ref, fwd_ref, small_ref, states_ref, met_ref):
    inside = inside_overlap(corr_ref[...], fwd_ref)
    z_r, z_i = entry_overlap(rows_ref, fwd_ref)
    met_ref[...] = met_of(inside, z_r, z_i, states_ref[:LANES], states_ref[LANES:], small_ref)


def unpack(ref):
    return [ref[k * OWN : (k + 1) * OWN] for k in range(ref.shape[0] // OWN)]


def pack(ref, values):
    for k, value in enumerate(values):
        ref[k * OWN : (k + 1) * OWN] = value[:OWN]


def chip_kernel(own_ref, other_ref, states_ref, small_ref, out_ref, piece_ref, entered_ref):
    odd = (lax.axis_index("tm") % 2) == 1
    own, other = unpack(own_ref), unpack(other_ref)
    early = [jnp.where(odd, o, m) for o, m in zip(other, own)]
    late = [jnp.where(odd, m, o) for o, m in zip(other, own)]
    far_r, far_i = small_ref[MISC : MISC + 1], small_ref[MISC + 1 : MISC + 2]
    s_r, s_i = times(far_r, far_i, early[0], early[1])
    f_r, f_i = times(far_r, far_i, late[2], late[3])
    cross = early[0] * late[2] - early[1] * late[3]
    met = early[4] + late[4] + cross * small_ref[MISC + 5 : MISC + 6]
    pack(out_ref, [s_r + late[0], s_i + late[1], f_r + early[2], f_i + early[3], met, early[5] + late[5]])
    piece_ref[...] = jnp.where(odd, out_ref[6 * OWN - PIECE :], out_ref[:PIECE])
    fill = jnp.zeros((PAD - OWN, TOTAL_GROUPS), F32)
    r, i = carried(*[jnp.concatenate([jnp.where(odd, v, 0.0), fill], 0) for v in other[:2]], small_ref)
    entered_ref[:LANES] = states_ref[:LANES] + r
    entered_ref[LANES:] = states_ref[LANES:] + i


def carried(s_r, s_i, small_ref):
    return stacked(
        [
            times(small_ref[A64 + q : A64 + q + 1], small_ref[A64 + 8 + q : A64 + 9 + q], s_r, s_i)
            for q in range(PHASES)
        ]
    )


def second_finish_kernel(
    rows_at, params_ref, own_at, near_ref, swapped_ref, piece_ref, other_piece_ref, states_ref,
    fwd_ref, small_ref, send_ref, kern_ref, polar_ref, shift_ref, chips_ref, rows_ref, sems,
):
    place = lax.axis_index("tm")
    y = place // 2
    rows_copy = pltpu.make_async_copy(rows_at, rows_ref, sems.at[0])
    rows_copy.start()
    own_copy = pltpu.make_async_copy(own_at, chips_ref.at[y], sems.at[1])
    own_copy.start()
    odd = (place % 2) == 1
    by_chip(chips_ref, near_ref, swapped_ref)
    across = lax.rem(y + 2, NY)
    chips_ref[across, :PIECE] = jnp.where(odd, other_piece_ref[...], piece_ref[...])
    chips_ref[across, 6 * OWN - PIECE :] = jnp.where(odd, piece_ref[...], other_piece_ref[...])
    rows_copy.wait()
    shifts(rows_ref, shift_ref)
    own_copy.wait()
    far_r, far_i = small_ref[MISC + 2 : MISC + 3], small_ref[MISC + 3 : MISC + 4]
    scale = small_ref[MISC + 5 : MISC + 6]
    x_r = x_i = s_r = s_i = before = met = jnp.zeros((OWN, TOTAL_GROUPS), F32)
    for k in range(NY):
        e_r, e_i, f_r, f_i, here, first = unpack(chips_ref.at[k])
        s_r = jnp.where(y == k, x_r, s_r)
        s_i = jnp.where(y == k, x_i, s_i)
        before = before + first
        met = met + (here + (x_r * f_r - x_i * f_i) * scale)
        x_r, x_i = times(far_r, far_i, x_r, x_i)
        x_r, x_i = x_r + e_r, x_i + e_i
    send_ref[2 * OWN : 3 * OWN] = before + met
    send_ref[3 * OWN :] = jnp.zeros((PAD - OWN, TOTAL_GROUPS), F32)
    coupling = coupling_of(params_ref, small_ref)
    fill = jnp.zeros((PAD - OWN, TOTAL_GROUPS), F32)
    coupling = coupling * jnp.exp(-SATURATE * jnp.concatenate([before, fill], 0))
    inside_response(coupling, shift_ref, fwd_ref, kern_ref, polar_ref)
    later_r, later_i = times(small_ref[MISC : MISC + 1], small_ref[MISC + 1 : MISC + 2], s_r, s_i)
    s_r, s_i = jnp.where(odd, later_r, s_r), jnp.where(odd, later_i, s_i)
    s_r, s_i = jnp.concatenate([s_r, fill], 0), jnp.concatenate([s_i, fill], 0)
    states_r, states_i = carried(s_r, s_i, small_ref)
    states_r = states_r + states_ref[:LANES]
    states_i = states_i + states_ref[LANES:]
    entered_response(coupling, states_r, states_i, polar_ref, fwd_ref, small_ref, send_ref)


class Planes:
    def __init__(self, distances, refs):
        refs = list(refs)
        self.blocks = {d: [refs.pop(0) for _ in range(2 if d == 4 else 1)] for d in distances}

    @staticmethod
    def count(distances):
        return sum(2 if d == 4 else 1 for d in distances)

    def turned(self, distances, whole_ref):
        x = lax.axis_index("group") // NZ
        for n, d in enumerate(distances):
            for r in range(NX):
                at = pl.multiple_of(n * 96 + lax.rem(x - r + NX, NX) * 24, 8)
                block, low = self.blocks[d][0], 24 * r
                if d == 4 and r >= 2:
                    block, low = self.blocks[d][1], 24 * (r - 2)
                whole_ref[pl.ds(at, 24)] = block[low : low + 24]
        return whole_ref[: 96 * len(distances)].T

    @staticmethod
    def rows(distances, table_ref, cols):
        z = lax.axis_index("group") % NZ
        starts = [pl.multiple_of(lax.rem(z + d + NZ, NZ) * 96, 32) for d in distances]
        return jnp.concatenate([table_ref[pl.ds(at, 96), cols] for at in starts], 0)


def next_field_kernel(*refs):
    planes, refs = Planes(RING[7:], refs[:2]), refs[2:]
    field_in, high_ref, low_ref, fwd_ref, rev_ref, small_ref, met_ref = refs[:7]
    rows_out, states_ref, edge_ref, whole_ref, shift_ref, rows_ref, sems = refs[7:]
    pick = own_pick()
    turned = halves(planes.turned(RING[7:], whole_ref))
    for c in range(2):
        cols = slice(c * LATERAL, (c + 1) * LATERAL)
        table = [mm(Planes.rows(RING[7:], ref, cols), pick).astype(BF16) for ref in (high_ref, low_ref)]
        value = exact_pick(field_in[c], pick) + mm3(turned, table)
        rows_ref[c * ROWS : (c + 1) * ROWS] = time_rows(value)
    rows_copy = pltpu.make_async_copy(rows_ref, rows_out, sems.at[0])
    rows_copy.start()
    z = against(rows_ref[:ROWS], rows_ref[ROWS:], halves(rev_ref[...]))
    states, (s_r, s_i) = run_edges(None, z, small_ref)
    states_r, states_i = stacked(states)
    states_ref[:LANES] = states_r
    states_ref[LANES:] = states_i
    shifts(rows_ref, shift_ref)
    inside = inside_overlap(stretch_correlation(rows_ref, shift_ref), fwd_ref)
    z_r, z_i = entry_overlap(rows_ref, fwd_ref)
    met = met_of(inside, z_r, z_i, states_r, states_i, small_ref)
    f_r = f_i = jnp.zeros((PAD, TOTAL_GROUPS), F32)
    for q in range(PHASES):
        part = slice(q * PAD, (q + 1) * PAD)
        r, i = times(
            small_ref[A64 + q : A64 + q + 1], small_ref[A64 + 8 + q : A64 + 9 + q], z_r[part], z_i[part]
        )
        f_r, f_i = f_r + r, f_i + i
    f_r, f_i = times(small_ref[AV + 1 : AV + 2], small_ref[AV + 9 : AV + 10], f_r, f_i)
    pack(edge_ref, [s_r, s_i, f_r, f_i, met, met_ref[...]])
    rows_copy.wait()


def spread_kernel(distances, field_at, polar_at, start, *refs):
    count = Planes.count(distances)
    planes, refs = Planes(distances, refs[:count]), list(refs[count:])
    whole_ref = refs.pop()
    field_in = field_tables = polar_in = place_ref = None
    if field_at:
        field_in, field_tables = refs.pop(0), (refs.pop(0), refs.pop(0))
    if polar_at:
        polar_in = None if start else refs.pop(0)
        place_ref = refs.pop(0)
    if field_at:
        out_ref = refs.pop(0)
        turned = halves(planes.turned(field_at, whole_ref))
        for c in range(2):
            cols = slice(c * LATERAL, (c + 1) * LATERAL)
            table = [Planes.rows(field_at, ref, cols) for ref in field_tables]
            out_ref[c] = field_in[c] + mm3(turned, table)
    if polar_at:
        out_ref = refs.pop(0)
        turned = planes.turned(polar_at, whole_ref)
        for c in range(2):
            cols = slice(c * LATERAL, (c + 1) * LATERAL)
            value = exact_pick(turned, Planes.rows(polar_at, place_ref, cols))
            out_ref[c] = value if start else polar_in[c] + value


def last_kernel(*refs):
    planes, refs = Planes(RING, refs[:9]), refs[9:]
    field_in, high_ref, low_ref, polar_in, place_ref, occupied_ref = refs[:6]
    field_out, polar_out, occupied_out, whole_ref, field_ref, polar_ref, gathered_ref, sems = refs[6:]
    turned = planes.turned(RING[7:], whole_ref)
    pair = halves(turned)
    copies = []
    for c in range(2):
        cols = slice(c * LATERAL, (c + 1) * LATERAL)
        table = [Planes.rows(RING[7:], ref, cols) for ref in (high_ref, low_ref)]
        field_ref[c] = field_in[c] + mm3(pair, table)
        copies.append(pltpu.make_async_copy(field_ref.at[c], field_out.at[c], sems.at[c]))
        copies[-1].start()
    for c in range(2):
        cols = slice(c * LATERAL, (c + 1) * LATERAL)
        polar_ref[c] = polar_in[c] + exact_pick(turned, Planes.rows(RING[7:], place_ref, cols))
        copies.append(pltpu.make_async_copy(polar_ref.at[c], polar_out.at[c], sems.at[2 + c]))
        copies[-1].start()
    occupied_out[...] = occupied_ref[...] * jnp.exp(-SATURATE * gathered_met(planes, gathered_ref))
    for copy in copies:
        copy.wait()


def gathered_met(planes, gathered_ref):
    me = lax.axis_index("group")
    x, z = me // NZ, me % NZ
    for d in RING:
        for r in range(NX):
            owner = lax.rem(x - r + NX, NX) * NZ + lax.rem(z + d + NZ, NZ)
            at = pl.multiple_of(owner * PAD, 8)
            block, low = (planes.blocks[d][1], 48) if d == 4 else (planes.blocks[d][0], 96)
            gathered_ref[pl.ds(at, PAD)] = block[low:, LANES * r : LANES * r + LANES]
    mine = flag(iota((PAD, LANES), 1) == iota((PAD, LANES), 0) + PAD * z)
    turned = exact_nt(mine, gathered_ref[...])
    row = iota((TOTAL_GROUPS, LATERAL), 0)
    inner = row % PAD
    col = iota((TOTAL_GROUPS, LATERAL), 1)
    return exact_pick(turned, flag((inner < OWN) & (col == (row // PAD) * OWN + inner)))


RING = (0, -1, 1, -2, 2, -3, 3, 4)


VMEM = pl.BlockSpec(memory_space=pltpu.VMEM)
ANY = pl.BlockSpec(memory_space=pl.ANY)


def call(kernel, outs, scratch=(), cost=1e9, copied=0, at=None, to=()):
    specs = {"out_specs": [ANY if n in to else VMEM for n in range(len(outs))]}
    if at is not None:
        specs["in_specs"] = [ANY if n in at[1] else VMEM for n in range(at[0])]
    sems = [pltpu.SemaphoreType.DMA((copied,))] if copied else []
    return pl.pallas_call(
        kernel,
        out_shape=[jax.ShapeDtypeStruct(shape, dtype) for shape, dtype in outs],
        scratch_shapes=[pltpu.VMEM(shape, dtype) for shape, dtype in scratch] + sems,
        compiler_params=pltpu.CompilerParams(vmem_limit_bytes=16 * 1024 * 1024),
        cost_estimate=pl.CostEstimate(flops=int(cost), bytes_accessed=1 << 20, transcendentals=0),
        **specs,
    )


def to_group(value, dx, dz):
    pairs = [
        (x * NZ + z, ((x + dx) % NX) * NZ + (z + dz) % NZ) for x in range(NX) for z in range(NZ)
    ]
    return lax.ppermute(value, "group", pairs)


def across(value):
    return lax.ppermute(value, "tm", [(2 * y + c, 2 * ((y + 2) % NY) + c) for y in range(NY) for c in range(2)])


def to_side(value):
    pairs = [(2 * y + c, 2 * ((y + 1 - 2 * c) % NY) + c) for y in range(NY) for c in range(2)]
    return lax.ppermute(value, "tm", pairs)


def other_core(value):
    return lax.ppermute(value, "tm", [(i, i ^ 1) for i in range(2 * NY)])


def together(*values):
    return lax.optimization_barrier(values)


def step_on(blocks, d):
    if d == 4:
        return to_group(blocks[-3][0][:48], 0, 1), to_group(blocks[3][0][48:], 0, -1)
    near = (blocks[0][0], blocks[0][0]) if d == 1 else (blocks[1 - d][0], blocks[d - 1][0])
    return to_group(near[0], 0, 1), to_group(near[1], 0, -1)


def listed(blocks, distances):
    return [block for d in distances for block in blocks[d]]


def on_device(field, occupations, dephase, detune_class, dot_count):
    const = lateral_constants()
    natural, gathered = const["natural"], const["gathered"]
    table = ((2 * ROWS, TOTAL_GROUPS), F32)
    rows_shape = ((2 * ROWS, LANES), F32)
    shift_shape = ((2, 8, ROWS, LANES), F32)
    states_shape = ((2 * LANES, TOTAL_GROUPS), F32)
    edge_shape = ((6 * OWN, TOTAL_GROUPS), F32)
    met_shape = ((PAD, TOTAL_GROUPS), F32)
    field_shape = ((2, SPAN, LATERAL), F32)
    whole_shape = ((2 * LATERAL, SPAN), F32)

    def spread(blocks, field_at, polar_at, field_in=None, polar_in=None):
        distances = [d for d in RING if d in field_at or d in polar_at]
        extra = [field_in, *gathered] if field_at else []
        if polar_at:
            extra += ([] if polar_in is None else [polar_in]) + [const["place"]]
        outs = [field_shape] * (bool(field_at) + bool(polar_at))
        kernel = functools.partial(spread_kernel, distances, field_at, polar_at, polar_in is None)
        return call(kernel, outs, [whole_shape], 3e9)(*listed(blocks, distances), *extra)

    (pieces,) = call(pieces_kernel, [((NX * NZ, PAD * occupations.shape[0]), F32)])(
        occupations, dephase, detune_class, dot_count
    )
    (rows,) = call(own_field_kernel, [rows_shape])(field)
    other = other_core(rows)
    other, pieces = together(other, pieces)
    params = lax.all_to_all(pieces, "group", 0, 0, tiled=True)
    odd = (lax.axis_index("tm") % 2) == 1
    pair = jnp.concatenate([jnp.where(odd, other, rows), jnp.where(odd, rows, other)], 0)
    near = to_side(pair)
    far, swapped = to_side(near), other_core(near)
    (corr,) = call(correlation_kernel, [rows_shape], [shift_shape], 4e9)(rows)
    params, corr = together(params, corr)
    params = params.reshape(NX * NZ, PAD, -1).transpose(1, 0, 2).reshape(PAD, TOTAL_GROUPS)
    fwd, rev, small, send, states = call(
        first_kernel,
        [table, table, ((SMALL, TOTAL_GROUPS), F32), ((2 * OWN, SPAN), F32), states_shape],
        [rows_shape, rows_shape, shift_shape, ((NY, 4 * ROWS, LANES), F32)],
        3e9,
    )(params, rows, pair, near, far, swapped)

    near = [to_group(send, k, 0) for k in (1, 2, 3)]
    (met,) = call(first_overlap_kernel, [met_shape])(rows, corr, fwd, small, states)
    send, met, *near = together(send, met, *near)
    blocks = {0: [jnp.concatenate([send] + near, 0)]}
    f, b = step_on(blocks, 1)
    (turned,) = call(turn_kernel, [field_shape], (), 3e9)(field, *natural)
    b, turned = together(b, turned)
    blocks[-1], blocks[1] = [f], [b]
    f, b = step_on(blocks, 2)
    (turned,) = spread(blocks, RING[:3], (), turned)
    b, turned = together(b, turned)
    blocks[-2], blocks[2] = [f], [b]
    f, b = step_on(blocks, 3)
    (turned,) = spread(blocks, RING[3:5], (), turned)
    b, turned = together(b, turned)
    blocks[-3], blocks[3] = [f], [b]
    f, b = step_on(blocks, 4)
    (turned,) = spread(blocks, RING[5:7], (), turned)
    b, turned = together(b, turned)
    blocks[4] = [f, b]
    rows, states, edge = call(
        next_field_kernel,
        [rows_shape, states_shape, edge_shape],
        [((96, SPAN), F32), shift_shape, rows_shape],
        copied=1,
        to=(0,),
    )(*blocks[4], turned, *gathered, fwd, rev, small, met)

    other = other_core(edge)
    chip, piece, states = call(
        chip_kernel, [edge_shape, ((PIECE, TOTAL_GROUPS), F32), states_shape]
    )(edge, other, states, small)
    near, piece = to_side(chip), across(piece)
    (field,) = spread(blocks, RING[7:], (), turned)
    near, field = together(near, field)
    swapped, other_piece = other_core(near), other_core(piece)
    (send,) = call(
        second_finish_kernel,
        [((2 * OWN + PAD, SPAN), F32)],
        [rows_shape, rows_shape, shift_shape, ((NY, 6 * OWN, TOTAL_GROUPS), F32), rows_shape],
        copied=2,
        at=(10, (0, 2)),
    )(rows, params, chip, near, swapped, piece, other_piece, states, fwd, small)

    sent = [send] + [to_group(send, k, 0) for k in (1, 2, 3)]
    (turned,) = call(turn_kernel, [field_shape], (), 3e9)(field, *natural)
    turned, *sent = together(turned, *sent)
    x = lax.axis_index("group") // NZ
    mets = [lax.dynamic_slice(g[2 * OWN :], (0, x * LANES), (PAD, LANES)) for g in sent]
    blocks = {0: [jnp.concatenate([g[: 2 * OWN] for g in sent] + [jnp.concatenate(mets, 1)], 0)]}
    f, b = step_on(blocks, 1)
    blocks[-1], blocks[1] = [f], [b]
    f, b = step_on(blocks, 2)
    (polar,) = spread(blocks, (), RING[:3])
    b, polar = together(b, polar)
    blocks[-2], blocks[2] = [f], [b]
    f, b = step_on(blocks, 3)
    amplified, polar = spread(blocks, RING[:5], RING[3:5], turned, polar)
    b, amplified, polar = together(b, amplified, polar)
    blocks[-3], blocks[3] = [f], [b]
    f, b = step_on(blocks, 4)
    amplified, polar = spread(blocks, RING[5:7], RING[5:7], amplified, polar)
    b, polar, amplified = together(b, polar, amplified)
    blocks[4] = [f, b]
    amplified, polar, occupied = call(
        last_kernel,
        [field_shape, field_shape, ((PAD, LATERAL), F32)],
        [((96, SPAN), F32), field_shape, field_shape, ((TOTAL_GROUPS, LANES), F32)],
        copied=4,
        to=(0, 1),
    )(*listed(blocks, RING), amplified, *gathered, polar, const["place"], occupations)
    return amplified, polar, occupied


def solution(mesh):
    return jax.shard_map(
        on_device,
        mesh=mesh,
        in_specs=(P(None, "tm", None), P("group", None), P("group"), P("group"), P("group")),
        out_specs=(P(None, "tm", None), P(None, "tm", None), P("group", None)),
        check_vma=False,
    )
```
